32 devices in a mesh: seq: 8 (over z, core), tp: 4 (over y, x).
Axes of the slice: x: 2, y: 2, z: 4, core: 2. Of those that a mesh axis runs over, the one named last changes fastest.
Arguments:
- tokens: bfloat16 [4096, 2048], P(('seq', 'tp')), may hold values from -6 to 6
- mixer_gain: bfloat16 [2048], P('tp'), may hold values from 0.5 to 1.5
- in_proj: bfloat16 [2048, 2816], P(None, 'tp'), may hold values from -0.125 to 0.125
- branch_proj: bfloat16 [2048, 2816], P(None, 'tp'), may hold values from -0.125 to 0.125
- conv_taps: float32 [4, 2816], P(None, 'tp'), may hold values from -3 to 3
- conv_bias: float32 [2816], P('tp'), may hold values from -3 to 3
- rate_blocks: bfloat16 [16, 176, 176], P('tp'), may hold values from -0.4375 to 0.4375
- rate_bias: float32 [2816], P('tp'), may hold values from -4 to 4
- input_blocks: bfloat16 [16, 176, 176], P('tp'), may hold values from -0.4375 to 0.4375
- input_bias: float32 [2816], P('tp'), may hold values from -4 to 4
- decay_param: float32 [2816], P('tp')
- out_proj: bfloat16 [2816, 2048], P('tp'), may hold values from -0.4375 to 0.4375
- dense_gain: bfloat16 [2048], P('tp'), may hold values from 0.5 to 1.5
- gate_proj: bfloat16 [2048, 6144], P(None, 'tp'), may hold values from -0.125 to 0.125
- up_proj: bfloat16 [2048, 6144], P(None, 'tp'), may hold values from -0.125 to 0.125
- down_proj: bfloat16 [6144, 2048], P('tp'), may hold values from -0.15625 to 0.15625
- segment_ids: int32 [4096], P('seq'), may hold values from 0 to 6, as said below
- cotangent: bfloat16 [4096, 2048], P(('seq', 'tp')), may hold values from -6 to 6
Outputs:
- output: bfloat16 [4096, 2048], P(('seq', 'tp'))
- tokens_grad: float32 [4096, 2048], P(('seq', 'tp'))
- mixer_gain_grad: float32 [2048], P('tp')
- in_proj_grad: float32 [2048, 2816], P(None, 'tp')
- branch_proj_grad: float32 [2048, 2816], P(None, 'tp')
- conv_taps_grad: float32 [4, 2816], P(None, 'tp')
- conv_bias_grad: float32 [2816], P('tp')
- rate_blocks_grad: float32 [16, 176, 176], P('tp')
- rate_bias_grad: float32 [2816], P('tp')
- input_blocks_grad: float32 [16, 176, 176], P('tp')
- input_bias_grad: float32 [2816], P('tp')
- decay_grad: float32 [2816], P('tp')
- out_proj_grad: float32 [2816, 2048], P('tp')
- dense_gain_grad: float32 [2048], P('tp')
- gate_proj_grad: float32 [2048, 6144], P(None, 'tp')
- up_proj_grad: float32 [2048, 6144], P(None, 'tp')
- down_proj_grad: float32 [6144, 2048], P('tp')
The draws below stay inside these ranges and needn't reach their ends.
Inputs may be any that keep to these rules, and one draw needn't show every extreme that they name: `segment_ids`: ids never fall along the stream, begin at 0 and end at 6; a new id marks a document start.
All inputs are finite; a program needn't handle non-finite values.
Results may differ from the reference program's by a relative error of at most 0.015.
Values may be sent and summed in bfloat16 or wider, within the bound.
No kernel may reach another device: no remote copies, remote signals or barrier semaphores. Data moves between devices by JAX's collectives and lax.ppermute only.
A program may use at most 320 MiB of HBM per device.

```python
import functools
import math
import jax
import jax.numpy as jnp
from jax import lax

D = 2048
NB = 16
BW = 176
FF = 6144
KW = 4
TOK_DEV = 128
RW = 2816
TOKENS = 4096
N_SEQ = 8


def draw_decay_param(key, part):
    key = jax.random.fold_in(key, 11)
    uniform_draw = jax.random.uniform(key, (RW,), jnp.float32)
    upper = math.log(TOKENS) + 1.5
    return 5.0 + (upper - 5.0) * jnp.sqrt(jnp.sqrt(uniform_draw))


def draw_segment_ids(key, part):
    key = jax.random.fold_in(key, 23)
    early_key, rim_key, late_key = jax.random.split(key, 3)
    group = TOKENS // N_SEQ
    early_marks = jax.random.permutation(early_key, group - 5)[:2].astype(jnp.int32) + 1
    rim_mark = group - jax.random.randint(rim_key, (1,), 1, 3).astype(jnp.int32)
    late_marks = jax.random.permutation(late_key, TOK_DEV)[:3].astype(jnp.int32) + (TOKENS - TOK_DEV)
    marks = jnp.concatenate([early_marks, rim_mark, late_marks])
    places = jnp.arange(TOKENS, dtype=jnp.int32)
    return jnp.sum((places[:, None] >= marks[None, :]).astype(jnp.int32), axis=1)


def block_levels(rng, extent, shards, low, largest):
    def one(dim, blocks):
        steps = jax.random.uniform(jax.random.fold_in(jax.random.fold_in(rng, 6), dim), (blocks,), jnp.float32, low / len(shards), largest / len(shards))
        return jnp.repeat(jnp.exp(steps), extent[dim] // blocks).reshape((-1,) + (1,) * (len(extent) - dim - 1))

    loudness = one(*shards[0])
    for cut in shards[1:]:
        loudness = loudness * one(*cut)
    return loudness


def bell_draw(stream_key, shape, deviation, most, cuts=(), kind=jnp.bfloat16):
    factor_of = block_levels(stream_key, shape, cuts, -0.22, 0.18) if cuts else 1.0
    values = jax.random.normal(stream_key, shape, jnp.float32) * deviation * factor_of
    return jnp.minimum(jnp.maximum(values, -most), most).astype(kind)


def setup_inputs(seed: int = 0) -> dict:
    arg_keys = jax.random.split(jax.random.key(seed), 19)
    return {
        "tokens": bell_draw(arg_keys[0], (TOKENS, D), 1.0, 6.0, ((0, 32),)),
        "mixer_gain": jnp.clip(1.0 + 0.1 * jax.random.normal(arg_keys[1], (D,), jnp.float32), 0.5, 1.5).astype(jnp.bfloat16),
        "in_proj": bell_draw(arg_keys[2], (D, RW), D ** -0.5, 0.125, ((1, 4),)),
        "branch_proj": bell_draw(arg_keys[3], (D, RW), D ** -0.5, 0.125, ((1, 4),)),
        "conv_taps": bell_draw(arg_keys[4], (KW, RW), 0.5, 3.0, ((1, 4),), jnp.float32),
        "conv_bias": bell_draw(arg_keys[5], (RW,), 0.5, 3.0, ((0, 4),), jnp.float32),
        "rate_blocks": bell_draw(arg_keys[6], (NB, BW, BW), BW ** -0.5, 0.4375, ((0, 4),)),
        "rate_bias": bell_draw(arg_keys[7], (RW,), 1.0, 4.0, ((0, 4),), jnp.float32),
        "input_blocks": bell_draw(arg_keys[8], (NB, BW, BW), BW ** -0.5, 0.4375, ((0, 4),)),
        "input_bias": bell_draw(arg_keys[9], (RW,), 1.0, 4.0, ((0, 4),), jnp.float32),
        "decay_param": draw_decay_param(jax.random.fold_in(arg_keys[18], 71), 0),
        "out_proj": bell_draw(arg_keys[11], (RW, D), (RW // 16) ** -0.5, 0.4375, ((0, 4),)),
        "dense_gain": jnp.clip(1.0 + 0.1 * jax.random.normal(arg_keys[12], (D,), jnp.float32), 0.5, 1.5).astype(jnp.bfloat16),
        "gate_proj": bell_draw(arg_keys[13], (D, FF), D ** -0.5, 0.125, ((1, 4),)),
        "up_proj": bell_draw(arg_keys[14], (D, FF), D ** -0.5, 0.125, ((1, 4),)),
        "down_proj": bell_draw(arg_keys[15], (FF, D), (FF // 4) ** -0.5, 0.15625, ((0, 4),)),
        "segment_ids": draw_segment_ids(jax.random.fold_in(arg_keys[18], 71), 0),
        "cotangent": bell_draw(arg_keys[17], (TOKENS, D), 1.0, 6.0, ((0, 32),)),
    }


@jax.custom_vjp
def low(v):
    return lax.optimization_barrier(v.astype(jnp.bfloat16)).astype(jnp.float32)

@jax.custom_vjp
def low_back(v):
    return v

def low_keep(v):
    return (low(v), None)

def low_pass(kept, grad):
    return (grad,)

def back_keep(v):
    return (v, None)

def back_low(kept, grad):
    return (low(grad),)
low.defvjp(low_keep, low_pass)
low_back.defvjp(back_keep, back_low)
HIGHEST = lax.Precision.HIGHEST
epsilon = 1e-06

def matmul(left, right):
    return jnp.dot(left, right, precision=HIGHEST)

def rms_scale(values):
    return values * lax.rsqrt(lax.optimization_barrier(jnp.mean(values * values, axis=-1, keepdims=True)) + epsilon)

def gelu_tanh(values):
    return jax.nn.gelu(values, approximate=True)

def combine(earlier, later):
    return (earlier[0] * later[0], later[0] * earlier[1] + later[1])

def causal_conv(extended, ext_ids, taps, bias):
    rim_width = taps.shape[0] - 1
    length = extended.shape[0] - rim_width
    own_ids = ext_ids[rim_width:]
    result = jnp.broadcast_to(bias, (length, extended.shape[1]))
    for offset in range(taps.shape[0]):
        window = extended[rim_width - offset:rim_width - offset + length]
        same = (ext_ids[rim_width - offset:rim_width - offset + length] == own_ids).astype(extended.dtype)
        result = result + taps[offset] * window * same[:, None]
    return result

def gate_terms(rate_raw, input_raw, conv_out, rate_bias, input_bias, decay_param, starts):
    log_decay = -8.0 * jax.nn.sigmoid(rate_raw + rate_bias) * jax.nn.softplus(-decay_param)
    keep = jnp.exp(log_decay) * (1.0 - starts)[:, None]
    drive = jnp.sqrt(-jnp.expm1(2.0 * log_decay)) * jax.nn.sigmoid(input_raw + input_bias) * conv_out
    return (keep, drive)

def block_product(values, blocks):
    split = values.reshape(values.shape[0], blocks.shape[0], blocks.shape[1])
    return jnp.einsum('tnc,ncd->tnd', split, blocks, precision=HIGHEST).reshape(values.shape[0], -1)

def block_step(params, carry, inputs):
    mixer_gain, in_proj, branch_proj, conv_taps, conv_bias, rate_blocks, rate_bias, input_blocks, input_bias, decay_param, out_proj, dense_gain, gate_proj, up_proj, down_proj = params
    state_in, rim_values, rim_ids = carry
    rows, seg_block = inputs
    rim_width = conv_taps.shape[0] - 1
    normed = low(rms_scale(rows) * mixer_gain)
    inner_proj = low_back(matmul(normed, in_proj))
    branch_pre = low_back(matmul(normed, branch_proj))
    branch = gelu_tanh(branch_pre)
    extended = jnp.concatenate([rim_values, inner_proj], axis=0)
    ext_ids = jnp.concatenate([rim_ids, seg_block], axis=0)
    conv_out = causal_conv(extended, ext_ids, conv_taps, conv_bias)
    starts = (ext_ids[rim_width:] != ext_ids[rim_width - 1:-1]).astype(rows.dtype)
    conv_low = low(conv_out)
    rate_raw = low_back(block_product(conv_low, rate_blocks))
    input_raw = low_back(block_product(conv_low, input_blocks))
    keep, drive = gate_terms(rate_raw, input_raw, conv_out, rate_bias, input_bias, decay_param, starts)
    prefix_keep, prefix_drive = lax.associative_scan(combine, (keep, drive), axis=0)
    state = prefix_drive + prefix_keep * state_in
    mixed = low(state * branch)
    mid = rows + low_back(matmul(mixed, out_proj))
    normed_two = low(rms_scale(mid) * dense_gain)
    gate_pre = low_back(matmul(normed_two, gate_proj))
    up_pre = low_back(matmul(normed_two, up_proj))
    hidden = low(gelu_tanh(gate_pre) * up_pre)
    result = mid + low_back(matmul(hidden, down_proj))
    return ((state[-1], inner_proj[-rim_width:], ext_ids[-rim_width:]), result)

def reference(tokens, mixer_gain, in_proj, branch_proj, conv_taps, conv_bias, rate_blocks, rate_bias, input_blocks, input_bias, decay_param, out_proj, dense_gain, gate_proj, up_proj, down_proj, segment_ids, cotangent):
    weights = (mixer_gain, in_proj, branch_proj, conv_taps, conv_bias, rate_blocks, rate_bias, input_blocks, input_bias, decay_param, out_proj, dense_gain, gate_proj, up_proj, down_proj)
    params = tuple((member.astype(jnp.float32) for member in weights))
    rows = tokens.astype(jnp.float32)
    block_rows = math.gcd(TOKENS, 4096)
    block_count = TOKENS // block_rows
    rim_width = KW - 1

    def forward(rows_in, params_in):
        stepper = jax.checkpoint(functools.partial(block_step, params_in))
        start_carry = (jnp.zeros((RW,), jnp.float32), jnp.zeros((rim_width, RW), jnp.float32), jnp.zeros((rim_width,), jnp.int32))
        final_carry, pieces = lax.scan(stepper, start_carry, (rows_in.reshape(block_count, block_rows, D), segment_ids.reshape(block_count, block_rows)))
        return pieces.reshape(TOKENS, D)
    result, pullback = jax.vjp(forward, rows, params)
    rows_grad, grads = pullback(cotangent.astype(jnp.float32))
    return (result.astype(jnp.bfloat16), rows_grad, grads[0], grads[1], grads[2], grads[3], grads[4], grads[5], grads[6], grads[7], grads[8], grads[9], grads[10], grads[11], grads[12], grads[13], grads[14])
```

```python
import functools

import jax
import jax.numpy as jnp
from jax import lax
from jax.experimental import pallas as pl
from jax.experimental.pallas import tpu as pltpu
from jax.sharding import PartitionSpec as P

epsilon = 1e-06
f32 = jnp.float32
bf16 = jnp.bfloat16
TILE = 8
VMEM_LIMIT = 50 * 1024 * 1024


def product(left, right):
    return jnp.dot(left, right, preferred_element_type=f32)


def product_left_t(left, right):
    return lax.dot_general(left, right, (((0,), (0,)), ((), ())), preferred_element_type=f32)


def product_right_t(left, right):
    return lax.dot_general(left, right, (((1,), (1,)), ((), ())), preferred_element_type=f32)


def gelu_tanh(values):
    return jax.nn.gelu(values, approximate=True)


def dense_act(gate_values, up_values):
    return gelu_tanh(gate_values) * up_values


def swap(value, axis, bit):
    count = lax.axis_size(axis)
    return lax.ppermute(value, axis, [(i, i ^ bit) for i in range(count)])


def gather_rel(rows):
    count = lax.axis_size("tp")
    return jnp.stack([rows] + [swap(rows, "tp", r) for r in range(1, count)], axis=0)


def scatter_rel(blocks):
    count = lax.axis_size("tp")
    total = blocks[0].astype(f32)
    for r in range(1, count):
        total = total + swap(blocks[r], "tp", r).astype(f32)
    return total


def carry_in(keep_total, value_total, backward):
    place = lax.axis_index("seq")
    total = jnp.stack([keep_total, value_total])
    before = jnp.stack([jnp.ones_like(keep_total), jnp.zeros_like(value_total)])
    bit = 1
    while bit < lax.axis_size("seq"):
        other = swap(total, "seq", bit)
        upper = (place & bit) != 0
        earlier = jnp.logical_not(upper) if backward else upper
        joined_before = jnp.stack([other[0] * before[0], before[0] * other[1] + before[1]])
        before = jnp.where(earlier, joined_before, before)
        first = jnp.where(earlier, other, total)
        second = jnp.where(earlier, total, other)
        total = jnp.stack([first[0] * second[0], second[0] * first[1] + second[1]])
        bit *= 2
    return before[1]


def sum_bits(value, axis):
    bit = 1
    while bit < lax.axis_size(axis):
        value = value + swap(value, axis, bit)
        bit *= 2
    return value


def line_pairs(kind):
    pairs = []
    for i in range(lax.axis_size("seq")):
        chip, core = i // 2, i % 2
        base, z = chip // 4 * 4, chip % 4
        to = {"in": {0: 1, 3: 2}, "mid": {1: 2, 2: 1}, "out": {1: 0, 2: 3}}[kind].get(z)
        if to is not None:
            pairs.append((i, (base + to) * 2 + core))
    return pairs


def line_sum(part):
    z = lax.axis_index("seq") // 2 % 4
    at_end = jnp.logical_or(z == 0, z == 3)
    half = part + lax.ppermute(part, "seq", line_pairs("in"))
    total = half + lax.ppermute(half, "seq", line_pairs("mid"))
    bit = 8
    while bit < lax.axis_size("seq"):
        total = total + swap(total, "seq", bit)
        bit *= 2
    return jnp.where(at_end, lax.ppermute(total, "seq", line_pairs("out")), total)


def both_halves(mine, theirs, core):
    first = jnp.where(core == 0, mine, theirs)
    second = jnp.where(core == 0, theirs, mine)
    return first, second


def summed_grad(left, right, core):
    width = left.shape[1] // 2
    theirs = lax.dynamic_slice_in_dim(left, (1 - core) * width, width, 1)
    ours = lax.dynamic_slice_in_dim(left, core * width, width, 1)
    away = product_left_t(theirs, right).astype(bf16)
    back = swap(away, "seq", 1)
    part = (product_left_t(ours, right) + back.astype(f32)).astype(bf16)
    total = line_sum(part)
    other = swap(total, "seq", 1)
    first, second = both_halves(total, other, core)
    return jnp.concatenate([first, second], axis=0).astype(f32)


def minus_expm1(x):
    series = 1.0 / 40320.0
    for term in (1.0 / 5040.0, 1.0 / 720.0, 1.0 / 120.0, 1.0 / 24.0, 1.0 / 6.0, 0.5, 1.0):
        series = series * x + term
    return jnp.where(x > -0.35, -x * series, 1.0 - jnp.exp(x))


def rows_of(shape):
    return lax.broadcasted_iota(jnp.int32, shape, 0)


def down(cur, prev, by, row):
    return jnp.where(row >= by, pltpu.roll(cur, by, 0), pltpu.roll(prev, by, 0))


def up(cur, after, by, row):
    return jnp.where(row < TILE - by, pltpu.roll(cur, TILE - by, 0), pltpu.roll(after, TILE - by, 0))


def last_row(tile):
    return jnp.broadcast_to(tile[TILE - 1 :, :], tile.shape)


def first_row(tile):
    return jnp.broadcast_to(tile[:1, :], tile.shape)


def forward_kernel(
    place_ref,
    inner_ref,
    mask_ref,
    rim_ref,
    taps_ref,
    vec_ref,
    rate_ref,
    input_ref,
    conv_ref,
    low_ref,
    sig_rate_ref,
    sig_input_ref,
    keep_ref,
    value_ref,
    end_ref,
    prev_ref,
    carry_ref,
    rate_raw_ref,
    input_raw_ref,
):
    step = pl.program_id(0)
    length, width = inner_ref.shape[1:]
    tiles = length // TILE
    taps_n = taps_ref.shape[0]

    @pl.when(step == 0)
    def _():
        prev_ref[...] = rim_ref[...]
        carry_ref[0] = jnp.ones((TILE, width), f32)
        carry_ref[1] = jnp.zeros((TILE, width), f32)

    row = rows_of((TILE, width))

    def conv_tile(i, prev):
        at = pl.ds(pl.multiple_of(i * TILE, TILE), TILE)
        cur = inner_ref[0, at, :]
        masks = mask_ref[at, :]
        total = vec_ref[0:1, :] + taps_ref[0:1, :] * cur
        for k in range(1, taps_n):
            total = total + taps_ref[k : k + 1, :] * (down(cur, prev, k, row) * masks[:, k : k + 1])
        conv_ref[0, at, :] = total
        return cur

    prev_ref[...] = lax.fori_loop(0, tiles, conv_tile, prev_ref[...])
    low = conv_ref[0].astype(bf16)
    low_ref[0] = low
    rate_raw_ref[...] = jnp.dot(low, rate_ref[...], preferred_element_type=f32)
    input_raw_ref[...] = jnp.dot(low, input_ref[...], preferred_element_type=f32)

    def gate_tile(i, carry):
        keep_in, value_in = carry
        at = pl.ds(pl.multiple_of(i * TILE, TILE), TILE)
        sig_rate = jax.nn.sigmoid(rate_raw_ref[at, :] + vec_ref[1:2, :])
        sig_input = jax.nn.sigmoid(input_raw_ref[at, :] + vec_ref[2:3, :])
        sig_rate_ref[0, at, :] = sig_rate
        sig_input_ref[0, at, :] = sig_input
        log_decay = sig_rate * vec_ref[3:4, :]
        a = jnp.exp(log_decay) * mask_ref[at, 0:1]
        b = jnp.sqrt(minus_expm1(2.0 * log_decay)) * sig_input * conv_ref[0, at, :]
        for d in (1, 2, 4):
            a_before = jnp.where(row >= d, pltpu.roll(a, d, 0), 1.0)
            b_before = jnp.where(row >= d, pltpu.roll(b, d, 0), 0.0)
            b = b + a * b_before
            a = a * a_before
        b = b + a * value_in
        a = a * keep_in
        keep_ref[0, at, :] = a
        value_ref[0, at, :] = b
        return last_row(a), last_row(b)

    keep_end, value_end = lax.fori_loop(0, tiles, gate_tile, (carry_ref[0], carry_ref[1]))
    carry_ref[0] = keep_end
    carry_ref[1] = value_end
    end_ref[0] = keep_end
    end_ref[1] = value_end


def backward_kernel(
    place_ref,
    direct_ref,
    state_ref,
    state_prev_ref,
    conv_ref,
    sig_rate_ref,
    sig_input_ref,
    inner_ref,
    inner_prev_ref,
    mask_ref,
    rim_ref,
    state_in_ref,
    after_ref,
    taps_ref,
    vec_ref,
    rate_ref,
    input_ref,
    rate_grad_ref,
    input_grad_ref,
    inner_grad_ref,
    tail_ref,
    rim_grad_ref,
    sums_ref,
    carry_ref,
    next_ref,
    acc_ref,
    rate_f_ref,
    input_f_ref,
    conv_f_ref,
):
    step = pl.program_id(0)
    steps = pl.num_programs(0)
    length, width = direct_ref.shape[1:]
    tiles = length // TILE
    taps_n = taps_ref.shape[0]
    row = rows_of((TILE, width))
    is_first_block = step == steps - 1

    @pl.when(step == 0)
    def _():
        carry_ref[...] = after_ref[...]
        next_ref[...] = jnp.zeros_like(next_ref)
        acc_ref[...] = jnp.zeros_like(acc_ref)

    edge_state = jnp.where(is_first_block, state_in_ref[...], state_prev_ref[0])
    edge_inner = jnp.where(is_first_block, rim_ref[...], inner_prev_ref[0])
    neg_rate = vec_ref[3:4, :]

    def gate_tile(n, carry):
        after, acc_rate, acc_input, acc_decay = carry
        i = tiles - 1 - n
        at = pl.ds(pl.multiple_of(i * TILE, TILE), TILE)
        before = pl.ds(pl.multiple_of(jnp.maximum(i - 1, 0) * TILE, TILE), TILE)
        direct = direct_ref[0, at, :]
        sig_rate = sig_rate_ref[0, at, :]
        sig_input = sig_input_ref[0, at, :]
        conv = conv_ref[0, at, :]
        log_decay = sig_rate * neg_rate
        decay = jnp.exp(log_decay)
        keep = decay * mask_ref[at, 0:1]
        room = minus_expm1(2.0 * log_decay)
        root = jnp.sqrt(room)
        a = keep
        b = keep * direct
        for d in (1, 2, 4):
            a_after = jnp.where(row < TILE - d, pltpu.roll(a, TILE - d, 0), 1.0)
            b_after = jnp.where(row < TILE - d, pltpu.roll(b, TILE - d, 0), 0.0)
            b = b + a * b_after
            a = a * a_after
        reach = b + a * after
        grad = direct + up(reach, after, 1, row)
        prev_tile = jnp.where(i == 0, edge_state, state_ref[0, before, :])
        state_prev = down(state_ref[0, at, :], prev_tile, 1, row)
        grad_root = grad * root
        gated = grad_root * sig_input
        decay_grad = grad * (keep * state_prev - sig_input * conv * (decay * decay) / root)
        rate_grad = decay_grad * neg_rate * (sig_rate * (1.0 - sig_rate))
        input_grad = gated * conv * (1.0 - sig_input)
        rate_f_ref[at, :] = rate_grad
        input_f_ref[at, :] = input_grad
        conv_f_ref[at, :] = gated
        return (
            first_row(reach),
            acc_rate + rate_grad,
            acc_input + input_grad,
            acc_decay + decay_grad * sig_rate,
        )

    after, acc_rate, acc_input, acc_decay = lax.fori_loop(
        0, tiles, gate_tile, (carry_ref[...], acc_ref[0], acc_ref[1], acc_ref[2])
    )
    carry_ref[...] = after
    acc_ref[0] = acc_rate
    acc_ref[1] = acc_input
    acc_ref[2] = acc_decay
    rate_low = rate_f_ref[...].astype(bf16)
    input_low = input_f_ref[...].astype(bf16)
    rate_grad_ref[0] = rate_low
    input_grad_ref[0] = input_low
    right_t = (((1,), (1,)), ((), ()))
    conv_f_ref[...] += lax.dot_general(
        rate_low, rate_ref[...], right_t, preferred_element_type=f32
    ) + lax.dot_general(input_low, input_ref[...], right_t, preferred_element_type=f32)

    def conv_tile(n, carry):
        acc_bias, acc_taps, nexts = carry
        i = tiles - 1 - n
        at = pl.ds(pl.multiple_of(i * TILE, TILE), TILE)
        before = pl.ds(pl.multiple_of(jnp.maximum(i - 1, 0) * TILE, TILE), TILE)
        grad = conv_f_ref[at, :]
        masks = mask_ref[at, :]
        cur = inner_ref[0, at, :]
        prev = jnp.where(i == 0, edge_inner, inner_ref[0, before, :])
        total = grad * taps_ref[0:1, :]
        new_taps = [acc_taps[0] + grad * cur]
        new_nexts = []
        for k in range(1, taps_n):
            masked = grad * masks[:, k : k + 1]
            part = masked * taps_ref[k : k + 1, :]
            total = total + up(part, nexts[k - 1], k, row)
            new_taps.append(acc_taps[k] + masked * down(cur, prev, k, row))
            new_nexts.append(part)
        rate_f_ref[at, :] = total
        return acc_bias + grad, tuple(new_taps), tuple(new_nexts)

    acc_bias, acc_taps, nexts = lax.fori_loop(
        0,
        tiles,
        conv_tile,
        (
            acc_ref[3],
            tuple(acc_ref[4 + k] for k in range(taps_n)),
            tuple(next_ref[k] for k in range(taps_n - 1)),
        ),
    )
    acc_ref[3] = acc_bias
    for k in range(taps_n):
        acc_ref[4 + k] = acc_taps[k]
    for k in range(taps_n - 1):
        next_ref[k] = nexts[k]
    inner_grad_ref[0] = rate_f_ref[...].astype(bf16)

    @pl.when(step == 0)
    def _():
        tail_ref[...] = rate_f_ref[length - TILE :, :]

    @pl.when(is_first_block)
    def _():
        zero = jnp.zeros((TILE, width), f32)
        total = zero
        for k in range(1, taps_n):
            total = total + up(zero, nexts[k - 1], k, row)
        rim_grad_ref[...] = total
        sums_ref[...] = jnp.sum(acc_ref[...], axis=1)


def recur_forward(place, inner, masks, rim, taps, vecs, rate_dense, input_dense):
    blocks, length, width = inner.shape
    whole = lambda *shape: pl.BlockSpec(shape, lambda j, p: (0,) * len(shape))
    block = pl.BlockSpec((1, length, width), lambda j, p: (j ^ p[0], 0, 0))
    full = jax.ShapeDtypeStruct((blocks, length, width), f32)
    return pl.pallas_call(
        forward_kernel,
        grid_spec=pltpu.PrefetchScalarGridSpec(
            num_scalar_prefetch=1,
            grid=(blocks,),
            in_specs=[
                block,
                pl.BlockSpec((length, masks.shape[1]), lambda j, p: (j, 0)),
                whole(*rim.shape),
                whole(*taps.shape),
                whole(*vecs.shape),
                whole(*rate_dense.shape),
                whole(*input_dense.shape),
            ],
            out_specs=[block, block, block, block, block, block, whole(2, TILE, width)],
            scratch_shapes=[
                pltpu.VMEM((TILE, width), f32),
                pltpu.VMEM((2, TILE, width), f32),
                pltpu.VMEM((length, width), f32),
                pltpu.VMEM((length, width), f32),
            ],
        ),
        out_shape=[
            full,
            jax.ShapeDtypeStruct((blocks, length, width), bf16),
            full,
            full,
            full,
            full,
            jax.ShapeDtypeStruct((2, TILE, width), f32),
        ],
        compiler_params=pltpu.CompilerParams(vmem_limit_bytes=VMEM_LIMIT),
        name="recur_forward",
    )(place, inner, masks, rim, taps, vecs, rate_dense, input_dense)


def recur_backward(
    place, direct, state, conv, sig_rate, sig_input, inner, masks, rim, state_in, after, taps, vecs, rate_dense, input_dense
):
    blocks, length, width = inner.shape
    last = length // TILE - 1
    whole = lambda *shape: pl.BlockSpec(shape, lambda j, p: (0,) * len(shape))
    block = pl.BlockSpec((1, length, width), lambda j, p: ((blocks - 1 - j) ^ p[0], 0, 0))
    edge = pl.BlockSpec(
        (1, TILE, width), lambda j, p: (jnp.maximum(blocks - 2 - j, 0) ^ p[0], last, 0)
    )
    low = jax.ShapeDtypeStruct((blocks, length, width), bf16)
    tile = jax.ShapeDtypeStruct((TILE, width), f32)
    count = 4 + taps.shape[0]
    return pl.pallas_call(
        backward_kernel,
        grid_spec=pltpu.PrefetchScalarGridSpec(
            num_scalar_prefetch=1,
            grid=(blocks,),
            in_specs=[
                block,
                block,
                edge,
                block,
                block,
                block,
                block,
                edge,
                pl.BlockSpec((length, masks.shape[1]), lambda j, p: (blocks - 1 - j, 0)),
                whole(*rim.shape),
                whole(*state_in.shape),
                whole(*after.shape),
                whole(*taps.shape),
                whole(*vecs.shape),
                whole(*rate_dense.shape),
                whole(*input_dense.shape),
            ],
            out_specs=[
                block,
                block,
                block,
                whole(TILE, width),
                whole(TILE, width),
                whole(count, width),
            ],
            scratch_shapes=[
                pltpu.VMEM((TILE, width), f32),
                pltpu.VMEM((taps.shape[0] - 1, TILE, width), f32),
                pltpu.VMEM((count, TILE, width), f32),
                pltpu.VMEM((length, width), f32),
                pltpu.VMEM((length, width), f32),
                pltpu.VMEM((length, width), f32),
            ],
        ),
        out_shape=[low, low, low, tile, tile, jax.ShapeDtypeStruct((count, width), f32)],
        compiler_params=pltpu.CompilerParams(vmem_limit_bytes=VMEM_LIMIT),
        name="recur_backward",
    )(
        place,
        direct,
        state,
        state,
        conv,
        sig_rate,
        sig_input,
        inner,
        inner,
        masks,
        rim,
        state_in,
        after,
        taps,
        vecs,
        rate_dense,
        input_dense,
    )


def dense_blocks(blocks):
    count, rows_in, cols_out = blocks.shape
    tall = blocks.reshape(count * rows_in, cols_out)
    wide = jnp.concatenate([tall] * count, axis=1)
    row = lax.broadcasted_iota(jnp.int32, wide.shape, 0) // rows_in
    col = lax.broadcasted_iota(jnp.int32, wide.shape, 1) // cols_out
    return jnp.where(row == col, wide, jnp.zeros_like(wide))


def diagonal_blocks(full, count):
    rows, cols = full.shape[0] // count, full.shape[1] // count
    return jnp.stack([full[i * rows : (i + 1) * rows, i * cols : (i + 1) * cols] for i in range(count)])


def rms(values):
    return lax.rsqrt(jnp.mean(values * values, axis=-1, keepdims=True) + epsilon)


def norm_back(grad, xhat, scale, root):
    e = grad * scale
    return root * (e - xhat * jnp.mean(e * xhat, axis=-1, keepdims=True)), jnp.sum(grad * xhat, axis=0)


def shards(
    tokens,
    mixer_gain,
    in_proj,
    branch_proj,
    conv_taps,
    conv_bias,
    rate_blocks,
    rate_bias,
    input_blocks,
    input_bias,
    decay_param,
    out_proj,
    dense_gain,
    gate_proj,
    up_proj,
    down_proj,
    segment_ids,
    cotangent,
):
    tp_place = lax.axis_index("tp")
    seq_place = lax.axis_index("seq")
    core = seq_place % 2
    tp_size = lax.axis_size("tp")
    seq_size = lax.axis_size("seq")
    place = tp_place.astype(jnp.int32)[None]
    gain_share = mixer_gain.shape[0]
    taps_n, width = conv_taps.shape
    rim_width = taps_n - 1
    length, model = tokens.shape
    group = length * tp_size
    blocks_n = rate_blocks.shape[0]
    hidden_n = gate_proj.shape[1]
    onward = [(i, i + 1) for i in range(seq_size - 1)]
    backward_pairs = [(i + 1, i) for i in range(seq_size - 1)]

    rows_rel = gather_rel(tokens)
    gains = gather_rel(jnp.stack([mixer_gain, dense_gain]))
    order = tp_place ^ jnp.arange(tp_size)
    gains = jnp.take(gains, order, axis=0).transpose(1, 0, 2).reshape(2, -1).astype(f32)
    mixer_scale, dense_scale = gains[0], gains[1]
    rim_ids = lax.ppermute(segment_ids[-rim_width:], "seq", onward)
    ext_ids = jnp.concatenate([rim_ids, segment_ids])
    same = [ext_ids[rim_width - k : rim_width - k + group] == segment_ids for k in range(1, taps_n)]
    masks = jnp.stack([same[0]] + same, axis=1).astype(f32)

    rate_dense = dense_blocks(rate_blocks)
    input_dense = dense_blocks(input_blocks)
    decay_rate = jax.nn.softplus(-decay_param)
    vecs = jnp.stack([conv_bias, rate_bias, input_bias, -8.0 * decay_rate])

    rows_f = rows_rel.reshape(group, model).astype(f32)
    normed = (rows_f * rms(rows_f) * mixer_scale).astype(bf16)
    inner = product(normed, in_proj).reshape(tp_size, length, width)
    last_block = lax.dynamic_index_in_dim(inner, (tp_size - 1) ^ tp_place, 0, False)
    rim = lax.ppermute(last_block[-TILE:], "seq", onward)
    branch_pre = product(normed, branch_proj)
    conv, conv_low, sig_rate, sig_input, keep_prefix, value_prefix, ends = recur_forward(
        place, inner, masks, rim, conv_taps, vecs, rate_dense, input_dense
    )
    state_in = carry_in(ends[0, 0], ends[1, 0], False)
    state = value_prefix + keep_prefix * state_in
    branch = gelu_tanh(branch_pre).reshape(state.shape)
    mixed = (state * branch).astype(bf16).reshape(group, width)
    mixer_out = scatter_rel(product(mixed, out_proj).astype(bf16).reshape(tp_size, length, model))
    mid = tokens.astype(f32) + mixer_out
    mid_root = rms(mid)
    xhat_dense = mid * mid_root
    normed_two = (xhat_dense * dense_scale).astype(bf16)

    rows_two = gather_rel(normed_two).reshape(group, model)
    cot_rows = gather_rel(cotangent).reshape(group, model)
    gate_pre = product(rows_two, gate_proj)
    up_pre = product(rows_two, up_proj)
    hidden_float, act_pull = jax.vjp(dense_act, gate_pre, up_pre)
    hidden = hidden_float.astype(bf16)
    hidden_grad = product_right_t(cot_rows, down_proj)
    gate_float, up_float = act_pull(hidden_grad)
    gate_grad = gate_float.astype(bf16)
    up_grad = up_float.astype(bf16)
    down_sum = summed_grad(hidden, cot_rows, core)
    gate_sum = summed_grad(rows_two, gate_grad, core)
    up_sum = summed_grad(rows_two, up_grad, core)
    normed_two_part = product_right_t(gate_grad, gate_proj) + product_right_t(up_grad, up_proj)
    normed_two_grad = scatter_rel(normed_two_part.astype(bf16).reshape(tp_size, length, model))
    dense_out = scatter_rel(product(hidden, down_proj).astype(bf16).reshape(tp_size, length, model))
    output = (mid + dense_out).astype(bf16)
    mid_from_norm, dense_gain_part = norm_back(normed_two_grad, xhat_dense, dense_scale, mid_root)
    mid_grad = cotangent.astype(f32) + mid_from_norm

    mid_rows = gather_rel(mid_grad.astype(bf16)).reshape(group, model)
    mixed_grad = product_right_t(mid_rows, out_proj).reshape(state.shape)
    work_branch, branch_pull = jax.vjp(gelu_tanh, branch_pre.reshape(state.shape))
    direct = mixed_grad * work_branch
    reach = jnp.sum(direct * keep_prefix, axis=(0, 1))
    out_sum = summed_grad(mixed, mid_rows, core)
    branch_pre_grad = branch_pull(mixed_grad * state)[0].astype(bf16).reshape(group, width)
    branch_sum = summed_grad(normed, branch_pre_grad, core)
    after = carry_in(ends[0, 0], reach, True)
    tile = lambda v: jnp.broadcast_to(v, (TILE, width))
    rate_low, input_low, inner_grad, tail, rim_grad, sums = recur_backward(
        place,
        direct,
        state,
        conv,
        sig_rate,
        sig_input,
        inner,
        masks,
        rim,
        tile(state_in),
        tile(after),
        conv_taps,
        vecs,
        rate_dense,
        input_dense,
    )
    fixed = tail + lax.ppermute(rim_grad, "seq", backward_pairs)
    inner_grad = lax.dynamic_update_slice(
        inner_grad, fixed.astype(bf16)[None], ((tp_size - 1) ^ tp_place, length - TILE, 0)
    ).reshape(group, width)
    in_sum = summed_grad(normed, inner_grad, core)
    low_rows = conv_low.reshape(group, width)
    rate_w = diagonal_blocks(product_left_t(low_rows, rate_low.reshape(group, width)), blocks_n)
    input_w = diagonal_blocks(product_left_t(low_rows, input_low.reshape(group, width)), blocks_n)
    rate_w, input_w = rate_w.astype(bf16), input_w.astype(bf16)
    ours, theirs = both_halves(rate_w, input_w, core)
    block_total = line_sum((ours.astype(f32) + swap(theirs, "seq", 1).astype(f32)).astype(bf16))
    rate_sum, input_sum = both_halves(block_total, swap(block_total, "seq", 1), core)
    normed_part = product_right_t(inner_grad, in_proj) + product_right_t(branch_pre_grad, branch_proj)
    normed_grad = scatter_rel(normed_part.astype(bf16).reshape(tp_size, length, model))
    own = tokens.astype(f32)
    own_root = rms(own)
    rows_grad, mixer_gain_part = norm_back(normed_grad, own * own_root, mixer_scale, own_root)
    tokens_grad = mid_grad + rows_grad

    gain_parts = sum_bits(jnp.stack([mixer_gain_part, dense_gain_part]), "tp")
    gain_own = lax.dynamic_slice_in_dim(gain_parts, tp_place * gain_share, gain_share, 1)
    gain_sum = sum_bits(gain_own, "seq")
    sums = sum_bits(sums, "seq")
    decay_sum = 8.0 * jax.nn.sigmoid(-decay_param) * sums[2]
    return (
        output,
        tokens_grad,
        gain_sum[0],
        in_sum,
        branch_sum,
        sums[4 : 4 + taps_n],
        sums[3],
        rate_sum.astype(f32),
        sums[0],
        input_sum.astype(f32),
        sums[1],
        decay_sum,
        out_sum,
        gain_sum[1],
        gate_sum,
        up_sum,
        down_sum,
    )


def solution(mesh):
    return jax.shard_map(
        shards,
        mesh=mesh,
        in_specs=(
            P(("seq", "tp"), None),
            P("tp"),
            P(None, "tp"),
            P(None, "tp"),
            P(None, "tp"),
            P("tp"),
            P("tp", None, None),
            P("tp"),
            P("tp", None, None),
            P("tp"),
            P("tp"),
            P("tp", None),
            P("tp"),
            P(None, "tp"),
            P(None, "tp"),
            P("tp", None),
            P("seq"),
            P(("seq", "tp"), None),
        ),
        out_specs=(
            P(("seq", "tp"), None),
            P(("seq", "tp"), None),
            P("tp"),
            P(None, "tp"),
            P(None, "tp"),
            P(None, "tp"),
            P("tp"),
            P("tp", None, None),
            P("tp"),
            P("tp", None, None),
            P("tp"),
            P("tp"),
            P("tp", None),
            P("tp"),
            P(None, "tp"),
            P(None, "tp"),
            P("tp", None),
        ),
        check_vma=False,
    )
```

```python
import math

import jax
import jax.numpy as jnp
from jax import lax
from jax.experimental import pallas as pl
from jax.experimental.pallas import tpu as pltpu
from jax.sharding import PartitionSpec as P

epsilon = 1e-06
f32 = jnp.float32
bf16 = jnp.bfloat16
TILE = 8
VMEM_LIMIT = 50 * 1024 * 1024


def product(left, right):
    return jnp.dot(left, right, preferred_element_type=f32)


def product_left_t(left, right):
    return lax.dot_general(left, right, (((0,), (0,)), ((), ())), preferred_element_type=f32)


def product_right_t(left, right):
    return lax.dot_general(left, right, (((1,), (1,)), ((), ())), preferred_element_type=f32)


def gelu_tanh(values):
    return jax.nn.gelu(values, approximate=True)


def tied(*values):
    return lax.optimization_barrier(values)


def swap(value, axis, bit):
    count = lax.axis_size(axis)
    return lax.ppermute(value, axis, [(i, i ^ bit) for i in range(count)])


def gather_rows(rows):
    count = lax.axis_size("tp")
    place = lax.axis_index("tp")
    whole = jnp.zeros((count,) + rows.shape, rows.dtype)
    for r in range(count):
        block = rows if r == 0 else swap(rows, "tp", r)
        whole = lax.dynamic_update_index_in_dim(whole, block, place ^ r, 0)
    return whole


def scatter_rows(blocks):
    place = lax.axis_index("tp")
    block = lambda r: lax.dynamic_index_in_dim(blocks, place ^ r, 0, False)
    total = block(0).astype(f32)
    for r in range(1, lax.axis_size("tp")):
        total = total + swap(block(r), "tp", r).astype(f32)
    return total


def carry_in(keep_total, value_total, backward):
    place = lax.axis_index("seq")
    total = jnp.stack([keep_total, value_total])
    before = jnp.stack([jnp.ones_like(keep_total), jnp.zeros_like(value_total)])
    bit = 1
    while bit < lax.axis_size("seq"):
        other = swap(total, "seq", bit)
        upper = (place & bit) != 0
        earlier = jnp.logical_not(upper) if backward else upper
        joined_before = jnp.stack([other[0] * before[0], before[0] * other[1] + before[1]])
        before = jnp.where(earlier, joined_before, before)
        first = jnp.where(earlier, other, total)
        second = jnp.where(earlier, total, other)
        total = jnp.stack([first[0] * second[0], second[0] * first[1] + second[1]])
        bit *= 2
    return before[1]


def from_neighbour(value, step):
    count = lax.axis_size("seq")
    place = lax.axis_index("seq")
    inside = lax.ppermute(value, "seq", [(i, i ^ 1) for i in range(count)])
    pairs = [(i, i + 1) for i in range(1, count - 1, 2)] + [(i + 1, i) for i in range(1, count - 1, 2)]
    across = lax.ppermute(value, "seq", pairs)
    return jnp.where((place % 2 == 0) == (step == 1), inside, across)


def sum_bits(value, axis):
    bit = 1
    while bit < lax.axis_size(axis):
        value = value + swap(value, axis, bit)
        bit *= 2
    return value


def both_halves(mine, theirs, core):
    first = jnp.where(core == 0, mine, theirs)
    second = jnp.where(core == 0, theirs, mine)
    return first, second


def gelu_grads(gate_pre, up_pre, hidden_grad):
    square = gate_pre * gate_pre
    inner = math.sqrt(2.0 / math.pi) * gate_pre * (1.0 + 0.044715 * square)
    half = 0.5 * (1.0 + jnp.tanh(inner))
    act = gate_pre * half
    slope = half + 2.0 * math.sqrt(2.0 / math.pi) * act * (1.0 - half) * (1.0 + 3.0 * 0.044715 * square)
    return act * up_pre, hidden_grad * up_pre * slope, hidden_grad * act


def dense_weight_grads(mine, theirs, cot_all, gate_proj, up_proj, down_proj, places):
    tp_size, chips, block, model = mine.shape
    half = gate_proj.shape[1] // 2
    cot_all = cot_all.reshape(chips, 2, tp_size, block, model)
    part = math.gcd(chips, 4)
    length = part * block
    per_core = tp_size * chips // part
    steps, outs = 2 * per_core, 4
    tile = math.gcd(half, 256)
    left_t = (((0,), (0,)), ((), ()))
    right_t = (((1,), (1,)), ((), ()))

    def kernel(core_ref, mine_ref, theirs_ref, cot_ref, gate_ref, up_ref, down_ref, *rest):
        gate_out, up_out, down_out, acc_g, acc_u, acc_d, hid, gg, ug, x_ref = rest
        i = pl.program_id(0)

        @pl.when(i < per_core)
        def _():
            x_ref[...] = mine_ref[...].reshape(length, model)

        @pl.when(jnp.logical_and(i >= per_core, i < steps))
        def _():
            x_ref[...] = theirs_ref[...].reshape(length, model)

        @pl.when(i == 0)
        def _():
            acc_g[...] = jnp.zeros_like(acc_g)
            acc_u[...] = jnp.zeros_like(acc_u)
            acc_d[...] = jnp.zeros_like(acc_d)

        @pl.when(i < steps)
        def _():
            cots = cot_ref[...].reshape(length, model)
            for n in range(half // tile):
                cols = slice(n * tile, (n + 1) * tile)
                gate_pre = jnp.dot(x_ref[...], gate_ref[:, cols], preferred_element_type=f32)
                up_pre = jnp.dot(x_ref[...], up_ref[:, cols], preferred_element_type=f32)
                hidden_grad = lax.dot_general(cots, down_ref[cols, :], right_t, preferred_element_type=f32)
                a, b, c = gelu_grads(gate_pre, up_pre, hidden_grad)
                hid[:, cols] = a.astype(bf16)
                gg[:, cols] = b.astype(bf16)
                ug[:, cols] = c.astype(bf16)
            acc_g[...] += lax.dot_general(x_ref[...], gg[...], left_t, preferred_element_type=f32)
            acc_u[...] += lax.dot_general(x_ref[...], ug[...], left_t, preferred_element_type=f32)
            acc_d[...] += lax.dot_general(hid[...], cots, left_t, preferred_element_type=f32)

        @pl.when(i >= steps)
        def _():
            wide = pl.ds(pl.multiple_of((i - steps) * (model // outs), model // outs), model // outs)
            low = pl.ds(pl.multiple_of((i - steps) * (half // outs), half // outs), half // outs)
            gate_out[...] = acc_g[wide, :].astype(bf16)
            up_out[...] = acc_u[wide, :].astype(bf16)
            down_out[...] = acc_d[low, :].astype(bf16)

    once = pl.Buffered(1)
    groups = chips // part
    out_index = lambda i, c: (jnp.maximum(i - steps, 0), 0)

    def cot_index(i, c):
        i = jnp.minimum(i, steps - 1)
        n = i % per_core
        return n % groups, c[0] ^ (i // per_core), n // groups, 0, 0

    def rows_index(first):
        def index(i, c):
            n = jnp.clip(i - first, 0, per_core - 1)
            return n // groups, n % groups, 0, 0

        return pl.BlockSpec((1, part, block, model), index)

    return pl.pallas_call(
        kernel,
        grid_spec=pltpu.PrefetchScalarGridSpec(
            num_scalar_prefetch=1,
            grid=(steps + outs,),
            in_specs=[
                rows_index(0),
                rows_index(per_core),
                pl.BlockSpec((part, 1, 1, block, model), cot_index),
                pl.BlockSpec((model, half), lambda i, c: (0, c[0]), pipeline_mode=once),
                pl.BlockSpec((model, half), lambda i, c: (0, c[0]), pipeline_mode=once),
                pl.BlockSpec((half, model), lambda i, c: (c[0], 0), pipeline_mode=once),
            ],
            out_specs=[
                pl.BlockSpec((model // outs, half), out_index),
                pl.BlockSpec((model // outs, half), out_index),
                pl.BlockSpec((half // outs, model), out_index),
            ],
            scratch_shapes=[
                pltpu.VMEM((model, half), f32),
                pltpu.VMEM((model, half), f32),
                pltpu.VMEM((half, model), f32),
                pltpu.VMEM((length, half), bf16),
                pltpu.VMEM((length, half), bf16),
                pltpu.VMEM((length, half), bf16),
                pltpu.VMEM((length, model), bf16),
            ],
        ),
        out_shape=[
            jax.ShapeDtypeStruct((model, half), bf16),
            jax.ShapeDtypeStruct((model, half), bf16),
            jax.ShapeDtypeStruct((half, model), bf16),
        ],
        compiler_params=pltpu.CompilerParams(vmem_limit_bytes=60 * 1024 * 1024),
        cost_estimate=pl.CostEstimate(flops=1000, bytes_accessed=1000, transcendentals=0),
        name="dense_weight_grads",
    )(places, mine, theirs, cot_all, gate_proj, up_proj, down_proj)


def joined(mine, theirs, core, axis):
    rows, cols = mine.shape
    block = math.gcd(rows, 256)
    steps = rows // block

    def kernel(core_ref, mine_ref, theirs_ref, out_ref):
        for low in range(2):

            @pl.when(core_ref[0] == low)
            def _(low=low):
                pair = (mine_ref, theirs_ref) if low == 0 else (theirs_ref, mine_ref)
                if axis == 1:
                    out_ref[:, :cols] = pair[0][...].astype(f32)
                    out_ref[:, cols:] = pair[1][...].astype(f32)
                else:
                    out_ref[0] = pair[0][...].astype(f32)
                    out_ref[1] = pair[1][...].astype(f32)

    half = pl.BlockSpec((block, cols), lambda i, c: (i, 0))
    if axis == 1:
        out_spec = pl.BlockSpec((block, 2 * cols), lambda i, c: (i, 0))
        out_shape = jax.ShapeDtypeStruct((rows, 2 * cols), f32)
    else:
        out_spec = pl.BlockSpec((2, block, cols), lambda i, c: (0, i, 0))
        out_shape = jax.ShapeDtypeStruct((2, rows, cols), f32)
    out = pl.pallas_call(
        kernel,
        grid_spec=pltpu.PrefetchScalarGridSpec(
            num_scalar_prefetch=1, grid=(steps,), in_specs=[half, half], out_specs=out_spec
        ),
        out_shape=out_shape,
        compiler_params=pltpu.CompilerParams(vmem_limit_bytes=VMEM_LIMIT),
        cost_estimate=pl.CostEstimate(flops=1000, bytes_accessed=1000, transcendentals=0),
        name="joined",
    )(core, mine, theirs)
    return out if axis == 1 else out.reshape(2 * rows, cols)


def dense_rows(rows, cot_all, group_place, gate_proj, up_proj, down_proj):
    length, model = rows.shape
    width = gate_proj.shape[1]
    tile = math.gcd(width, 256)
    out_tile = math.gcd(model, 256)
    first, second = width // tile, model // out_tile
    right_t = (((1,), (1,)), ((), ()))

    def kernel(place_ref, x_ref, c_ref, gate_ref, up_ref, down_ref, hidden_ref, grad_ref, gates, ups, gate_grads, up_grads):
        j = pl.program_id(0)

        @pl.when(j < first)
        def _():
            gate_pre = jnp.dot(x_ref[...], gate_ref[...], preferred_element_type=f32)
            up_pre = jnp.dot(x_ref[...], up_ref[...], preferred_element_type=f32)
            hidden_grad = lax.dot_general(c_ref[...], down_ref[...], right_t, preferred_element_type=f32)
            hidden, gate_grad, up_grad = gelu_grads(gate_pre, up_pre, hidden_grad)
            hidden_ref[...] = hidden.astype(bf16)
            at = pl.ds(pl.multiple_of(j * tile, tile), tile)
            gates[:, at] = gate_ref[...]
            ups[:, at] = up_ref[...]
            gate_grads[:, at] = gate_grad.astype(bf16)
            up_grads[:, at] = up_grad.astype(bf16)

        @pl.when(j >= first)
        def _():
            at = pl.ds(pl.multiple_of((j - first) * out_tile, out_tile), out_tile)
            part = lax.dot_general(gate_grads[...], gates[at, :], right_t, preferred_element_type=f32)
            part = part + lax.dot_general(up_grads[...], ups[at, :], right_t, preferred_element_type=f32)
            grad_ref[...] = part.astype(bf16)

    clamp = lambda j: jnp.minimum(j, first - 1)
    wide = pl.BlockSpec((model, tile), lambda j, p: (0, clamp(j)))
    return pl.pallas_call(
        kernel,
        grid_spec=pltpu.PrefetchScalarGridSpec(
            num_scalar_prefetch=1,
            grid=(first + second,),
            in_specs=[
                pl.BlockSpec((length, model), lambda j, p: (0, 0)),
                pl.BlockSpec((length, model), lambda j, p: (p[0], 0)),
                wide,
                wide,
                pl.BlockSpec((tile, model), lambda j, p: (clamp(j), 0)),
            ],
            out_specs=[
                pl.BlockSpec((length, tile), lambda j, p: (0, clamp(j))),
                pl.BlockSpec((length, out_tile), lambda j, p: (0, jnp.maximum(j - first, 0))),
            ],
            scratch_shapes=[
                pltpu.VMEM((model, width), bf16),
                pltpu.VMEM((model, width), bf16),
                pltpu.VMEM((length, width), bf16),
                pltpu.VMEM((length, width), bf16),
            ],
        ),
        out_shape=[
            jax.ShapeDtypeStruct((length, width), bf16),
            jax.ShapeDtypeStruct((length, model), bf16),
        ],
        compiler_params=pltpu.CompilerParams(vmem_limit_bytes=VMEM_LIMIT),
        name="dense_rows",
    )(group_place, rows, cot_all, gate_proj, up_proj, down_proj)


def project_t(rows, weight_t):
    total, model = rows.shape
    width = weight_t.shape[0]
    length = math.gcd(total, 256)

    def kernel(rows_ref, weight_ref, out_ref):
        out_ref[...] = lax.dot_general(
            rows_ref[...], weight_ref[...], (((1,), (1,)), ((), ())), preferred_element_type=f32
        )

    return pl.pallas_call(
        kernel,
        grid=(total // length,),
        in_specs=[
            pl.BlockSpec((length, model), lambda j: (j, 0)),
            pl.BlockSpec((width, model), lambda j: (0, 0)),
        ],
        out_specs=pl.BlockSpec((length, width), lambda j: (j, 0)),
        out_shape=jax.ShapeDtypeStruct((total, width), f32),
        compiler_params=pltpu.CompilerParams(vmem_limit_bytes=VMEM_LIMIT),
        name="project_t",
    )(rows, weight_t)


def mix_out(value_prefix, keep_prefix, branch_pre, state_in, out_proj):
    blocks, length, width = value_prefix.shape
    model = out_proj.shape[1]

    def kernel(value_ref, keep_ref, branch_ref, in_ref, out_ref, state_ref, mixed_ref, part_ref):
        state = value_ref[0] + keep_ref[0] * in_ref[...]
        state_ref[0] = state
        mixed = (state * gelu_tanh(branch_ref[0])).astype(bf16)
        mixed_ref[0] = mixed
        part_ref[0] = jnp.dot(mixed, out_ref[...], preferred_element_type=f32).astype(bf16)

    block = pl.BlockSpec((1, length, width), lambda j: (j, 0, 0))
    whole = lambda *shape: pl.BlockSpec(shape, lambda j: (0,) * len(shape))
    return pl.pallas_call(
        kernel,
        grid=(blocks,),
        in_specs=[block, block, block, whole(1, width), whole(width, model)],
        out_specs=[block, block, pl.BlockSpec((1, length, model), lambda j: (j, 0, 0))],
        out_shape=[
            jax.ShapeDtypeStruct((blocks, length, width), f32),
            jax.ShapeDtypeStruct((blocks, length, width), bf16),
            jax.ShapeDtypeStruct((blocks, length, model), bf16),
        ],
        compiler_params=pltpu.CompilerParams(vmem_limit_bytes=VMEM_LIMIT),
        name="mix_out",
    )(value_prefix, keep_prefix, branch_pre, state_in, out_proj)


def mix_back(mid_rows, out_proj, branch_pre, state, keep_prefix):
    blocks, length, width = state.shape
    model = out_proj.shape[1]
    tiles = length // 16

    def kernel(mid_ref, out_ref, branch_ref, state_ref, keep_ref, direct_ref, branch_grad_ref, reach_ref, mixed, acc):
        j = pl.program_id(0)
        mixed[...] = lax.dot_general(
            mid_ref[0], out_ref[...], (((1,), (1,)), ((), ())), preferred_element_type=f32
        )

        @pl.when(j == 0)
        def _():
            acc[...] = jnp.zeros_like(acc)

        def tile(i, total):
            at = pl.ds(pl.multiple_of(i * 16, 16), 16)
            grad = mixed[at, :]
            pre = branch_ref[0, at, :]
            square = pre * pre
            inner = math.sqrt(2.0 / math.pi) * pre * (1.0 + 0.044715 * square)
            half = 0.5 * (1.0 + jnp.tanh(inner))
            act = pre * half
            slope = half + 2.0 * math.sqrt(2.0 / math.pi) * act * (1.0 - half) * (1.0 + 3.0 * 0.044715 * square)
            direct = grad * act
            direct_ref[0, at, :] = direct
            branch_grad_ref[0, at, :] = (grad * state_ref[0, at, :] * slope).astype(bf16)
            return total + direct * keep_ref[0, at, :]

        acc[...] = lax.fori_loop(0, tiles, tile, acc[...])

        @pl.when(j == blocks - 1)
        def _():
            reach_ref[...] = jnp.sum(acc[...], axis=0, keepdims=True)

    block = pl.BlockSpec((1, length, width), lambda j: (j, 0, 0))
    whole = lambda *shape: pl.BlockSpec(shape, lambda j: (0,) * len(shape))
    return pl.pallas_call(
        kernel,
        grid=(blocks,),
        in_specs=[pl.BlockSpec((1, length, model), lambda j: (j, 0, 0)), whole(width, model), block, block, block],
        out_specs=[block, block, whole(1, width)],
        out_shape=[
            jax.ShapeDtypeStruct((blocks, length, width), f32),
            jax.ShapeDtypeStruct((blocks, length, width), bf16),
            jax.ShapeDtypeStruct((1, width), f32),
        ],
        scratch_shapes=[pltpu.VMEM((length, width), f32), pltpu.VMEM((16, width), f32)],
        compiler_params=pltpu.CompilerParams(vmem_limit_bytes=VMEM_LIMIT),
        name="mix_back",
    )(mid_rows, out_proj, branch_pre, state, keep_prefix)


def minus_expm1(x):
    series = 1.0 / 40320.0
    for term in (1.0 / 5040.0, 1.0 / 720.0, 1.0 / 120.0, 1.0 / 24.0, 1.0 / 6.0, 0.5, 1.0):
        series = series * x + term
    return jnp.where(x > -0.35, -x * series, 1.0 - jnp.exp(x))


def rows_of(shape):
    return lax.broadcasted_iota(jnp.int32, shape, 0)


def down(cur, prev, by, row):
    return jnp.where(row >= by, pltpu.roll(cur, by, 0), pltpu.roll(prev, by, 0))


def up(cur, after, by, row):
    return jnp.where(row < TILE - by, pltpu.roll(cur, TILE - by, 0), pltpu.roll(after, TILE - by, 0))


def last_row(tile):
    return jnp.broadcast_to(tile[TILE - 1 :, :], tile.shape)


def first_row(tile):
    return jnp.broadcast_to(tile[:1, :], tile.shape)


def forward_kernel(
    inner_ref,
    mask_ref,
    rim_ref,
    taps_ref,
    vec_ref,
    rate_ref,
    input_ref,
    conv_ref,
    low_ref,
    sig_rate_ref,
    sig_input_ref,
    keep_ref,
    value_ref,
    end_ref,
    prev_ref,
    carry_ref,
    rate_raw_ref,
    input_raw_ref,
):
    step = pl.program_id(0)
    length, width = inner_ref.shape[1:]
    tiles = length // TILE
    taps_n = taps_ref.shape[0]

    @pl.when(step == 0)
    def _():
        prev_ref[...] = rim_ref[...]
        carry_ref[0] = jnp.ones((TILE, width), f32)
        carry_ref[1] = jnp.zeros((TILE, width), f32)

    row = rows_of((TILE, width))

    def conv_tile(i, prev):
        at = pl.ds(pl.multiple_of(i * TILE, TILE), TILE)
        cur = inner_ref[0, at, :]
        masks = mask_ref[at, :]
        total = vec_ref[0:1, :] + taps_ref[0:1, :] * cur
        for k in range(1, taps_n):
            total = total + taps_ref[k : k + 1, :] * (down(cur, prev, k, row) * masks[:, k : k + 1])
        conv_ref[0, at, :] = total
        return cur

    prev_ref[...] = lax.fori_loop(0, tiles, conv_tile, prev_ref[...])
    low = conv_ref[0].astype(bf16)
    low_ref[0] = low
    rate_raw_ref[...] = jnp.dot(low, rate_ref[...], preferred_element_type=f32)
    input_raw_ref[...] = jnp.dot(low, input_ref[...], preferred_element_type=f32)

    def gate_tile(i, carry):
        keep_in, value_in = carry
        at = pl.ds(pl.multiple_of(i * TILE, TILE), TILE)
        sig_rate = jax.nn.sigmoid(rate_raw_ref[at, :] + vec_ref[1:2, :])
        sig_input = jax.nn.sigmoid(input_raw_ref[at, :] + vec_ref[2:3, :])
        sig_rate_ref[0, at, :] = sig_rate
        sig_input_ref[0, at, :] = sig_input
        log_decay = sig_rate * vec_ref[3:4, :]
        a = jnp.exp(log_decay) * mask_ref[at, 0:1]
        b = jnp.sqrt(minus_expm1(2.0 * log_decay)) * sig_input * conv_ref[0, at, :]
        for d in (1, 2, 4):
            a_before = jnp.where(row >= d, pltpu.roll(a, d, 0), 1.0)
            b_before = jnp.where(row >= d, pltpu.roll(b, d, 0), 0.0)
            b = b + a * b_before
            a = a * a_before
        b = b + a * value_in
        a = a * keep_in
        keep_ref[0, at, :] = a
        value_ref[0, at, :] = b
        return last_row(a), last_row(b)

    keep_end, value_end = lax.fori_loop(0, tiles, gate_tile, (carry_ref[0], carry_ref[1]))
    carry_ref[0] = keep_end
    carry_ref[1] = value_end
    end_ref[0] = keep_end
    end_ref[1] = value_end


def backward_kernel(
    direct_ref,
    state_ref,
    state_prev_ref,
    conv_ref,
    sig_rate_ref,
    sig_input_ref,
    inner_ref,
    inner_prev_ref,
    mask_ref,
    rim_ref,
    state_in_ref,
    after_ref,
    taps_ref,
    vec_ref,
    rate_ref,
    input_ref,
    rate_grad_ref,
    input_grad_ref,
    inner_grad_ref,
    tail_ref,
    rim_grad_ref,
    sums_ref,
    carry_ref,
    next_ref,
    acc_ref,
    rate_f_ref,
    input_f_ref,
    conv_f_ref,
):
    step = pl.program_id(0)
    steps = pl.num_programs(0)
    length, width = direct_ref.shape[1:]
    tiles = length // TILE
    taps_n = taps_ref.shape[0]
    row = rows_of((TILE, width))
    is_first_block = step == steps - 1

    @pl.when(step == 0)
    def _():
        carry_ref[...] = after_ref[...]
        next_ref[...] = jnp.zeros_like(next_ref)
        acc_ref[...] = jnp.zeros_like(acc_ref)

    edge_state = jnp.where(is_first_block, state_in_ref[...], state_prev_ref[0])
    edge_inner = jnp.where(is_first_block, rim_ref[...], inner_prev_ref[0])
    neg_rate = vec_ref[3:4, :]

    def gate_tile(n, carry):
        after, acc_rate, acc_input, acc_decay = carry
        i = tiles - 1 - n
        at = pl.ds(pl.multiple_of(i * TILE, TILE), TILE)
        before = pl.ds(pl.multiple_of(jnp.maximum(i - 1, 0) * TILE, TILE), TILE)
        direct = direct_ref[0, at, :]
        sig_rate = sig_rate_ref[0, at, :]
        sig_input = sig_input_ref[0, at, :]
        conv = conv_ref[0, at, :]
        log_decay = sig_rate * neg_rate
        decay = jnp.exp(log_decay)
        keep = decay * mask_ref[at, 0:1]
        room = minus_expm1(2.0 * log_decay)
        root = jnp.sqrt(room)
        a = keep
        b = keep * direct
        for d in (1, 2, 4):
            a_after = jnp.where(row < TILE - d, pltpu.roll(a, TILE - d, 0), 1.0)
            b_after = jnp.where(row < TILE - d, pltpu.roll(b, TILE - d, 0), 0.0)
            b = b + a * b_after
            a = a * a_after
        reach = b + a * after
        grad = direct + up(reach, after, 1, row)
        prev_tile = jnp.where(i == 0, edge_state, state_ref[0, before, :])
        state_prev = down(state_ref[0, at, :], prev_tile, 1, row)
        grad_root = grad * root
        gated = grad_root * sig_input
        decay_grad = grad * (keep * state_prev - sig_input * conv * (decay * decay) / root)
        rate_grad = decay_grad * neg_rate * (sig_rate * (1.0 - sig_rate))
        input_grad = gated * conv * (1.0 - sig_input)
        rate_f_ref[at, :] = rate_grad
        input_f_ref[at, :] = input_grad
        conv_f_ref[at, :] = gated
        return (
            first_row(reach),
            acc_rate + rate_grad,
            acc_input + input_grad,
            acc_decay + decay_grad * sig_rate,
        )

    after, acc_rate, acc_input, acc_decay = lax.fori_loop(
        0, tiles, gate_tile, (carry_ref[...], acc_ref[0], acc_ref[1], acc_ref[2])
    )
    carry_ref[...] = after
    acc_ref[0] = acc_rate
    acc_ref[1] = acc_input
    acc_ref[2] = acc_decay
    rate_low = rate_f_ref[...].astype(bf16)
    input_low = input_f_ref[...].astype(bf16)
    rate_grad_ref[0] = rate_low
    input_grad_ref[0] = input_low
    right_t = (((1,), (1,)), ((), ()))
    conv_f_ref[...] += lax.dot_general(
        rate_low, rate_ref[...], right_t, preferred_element_type=f32
    ) + lax.dot_general(input_low, input_ref[...], right_t, preferred_element_type=f32)

    def conv_tile(n, carry):
        acc_bias, acc_taps, nexts = carry
        i = tiles - 1 - n
        at = pl.ds(pl.multiple_of(i * TILE, TILE), TILE)
        before = pl.ds(pl.multiple_of(jnp.maximum(i - 1, 0) * TILE, TILE), TILE)
        grad = conv_f_ref[at, :]
        masks = mask_ref[at, :]
        cur = inner_ref[0, at, :]
        prev = jnp.where(i == 0, edge_inner, inner_ref[0, before, :])
        total = grad * taps_ref[0:1, :]
        new_taps = [acc_taps[0] + grad * cur]
        new_nexts = []
        for k in range(1, taps_n):
            masked = grad * masks[:, k : k + 1]
            part = masked * taps_ref[k : k + 1, :]
            total = total + up(part, nexts[k - 1], k, row)
            new_taps.append(acc_taps[k] + masked * down(cur, prev, k, row))
            new_nexts.append(part)
        rate_f_ref[at, :] = total
        return acc_bias + grad, tuple(new_taps), tuple(new_nexts)

    acc_bias, acc_taps, nexts = lax.fori_loop(
        0,
        tiles,
        conv_tile,
        (
            acc_ref[3],
            tuple(acc_ref[4 + k] for k in range(taps_n)),
            tuple(next_ref[k] for k in range(taps_n - 1)),
        ),
    )
    acc_ref[3] = acc_bias
    for k in range(taps_n):
        acc_ref[4 + k] = acc_taps[k]
    for k in range(taps_n - 1):
        next_ref[k] = nexts[k]
    inner_grad_ref[0] = rate_f_ref[...].astype(bf16)

    @pl.when(step == 0)
    def _():
        tail_ref[...] = rate_f_ref[length - TILE :, :]

    @pl.when(is_first_block)
    def _():
        zero = jnp.zeros((TILE, width), f32)
        total = zero
        for k in range(1, taps_n):
            total = total + up(zero, nexts[k - 1], k, row)
        rim_grad_ref[...] = total
        sums_ref[...] = jnp.sum(acc_ref[...], axis=1)


def norm_project(blocks, place, gain, weight_t):
    count = len(blocks)
    length, model = blocks[0].shape
    width = weight_t.shape[0]

    def kernel(place_ref, *refs):
        ins, gain_ref, weight_ref, normed_ref, out_ref = refs[:count], *refs[count:]
        j = pl.program_id(0)
        for r in range(count):

            @pl.when((j ^ place_ref[0]) == r)
            def _(source=ins[r]):
                x = source[...].astype(f32)
                root = lax.rsqrt(jnp.mean(x * x, axis=-1, keepdims=True) + epsilon)
                normed_ref[...] = (x * root * gain_ref[...]).astype(bf16)

        out_ref[0] = lax.dot_general(
            normed_ref[...], weight_ref[...], (((1,), (1,)), ((), ())), preferred_element_type=f32
        )

    whole = lambda *shape: pl.BlockSpec(shape, lambda j, p: (0,) * len(shape))
    return pl.pallas_call(
        kernel,
        grid_spec=pltpu.PrefetchScalarGridSpec(
            num_scalar_prefetch=1,
            grid=(count,),
            in_specs=[whole(length, model)] * count + [whole(1, model), whole(width, model)],
            out_specs=[
                pl.BlockSpec((length, model), lambda j, p: (j, 0)),
                pl.BlockSpec((1, length, width), lambda j, p: (j, 0, 0)),
            ],
        ),
        out_shape=[
            jax.ShapeDtypeStruct((count * length, model), bf16),
            jax.ShapeDtypeStruct((count, length, width), f32),
        ],
        compiler_params=pltpu.CompilerParams(vmem_limit_bytes=VMEM_LIMIT),
        name="norm_project",
    )(place, *blocks, gain, weight_t)


def recur_forward(inner, masks, rim, taps, vecs, rate_dense, input_dense):
    blocks, length, width = inner.shape
    whole = lambda *shape: pl.BlockSpec(shape, lambda j: (0,) * len(shape))
    block = pl.BlockSpec((1, length, width), lambda j: (j, 0, 0))
    full = jax.ShapeDtypeStruct((blocks, length, width), f32)
    return pl.pallas_call(
        forward_kernel,
        grid_spec=pltpu.PrefetchScalarGridSpec(
            num_scalar_prefetch=0,
            grid=(blocks,),
            in_specs=[
                block,
                pl.BlockSpec((length, masks.shape[1]), lambda j: (j, 0)),
                whole(*rim.shape),
                whole(*taps.shape),
                whole(*vecs.shape),
                whole(*rate_dense.shape),
                whole(*input_dense.shape),
            ],
            out_specs=[block, block, block, block, block, block, whole(2, TILE, width)],
            scratch_shapes=[
                pltpu.VMEM((TILE, width), f32),
                pltpu.VMEM((2, TILE, width), f32),
                pltpu.VMEM((length, width), f32),
                pltpu.VMEM((length, width), f32),
            ],
        ),
        out_shape=[
            full,
            jax.ShapeDtypeStruct((blocks, length, width), bf16),
            full,
            full,
            full,
            full,
            jax.ShapeDtypeStruct((2, TILE, width), f32),
        ],
        compiler_params=pltpu.CompilerParams(vmem_limit_bytes=VMEM_LIMIT),
        name="recur_forward",
    )(inner, masks, rim, taps, vecs, rate_dense, input_dense)


def recur_backward(
    direct, state, conv, sig_rate, sig_input, inner, masks, rim, state_in, after, taps, vecs, rate_dense, input_dense
):
    blocks, length, width = inner.shape
    last = length // TILE - 1
    whole = lambda *shape: pl.BlockSpec(shape, lambda j: (0,) * len(shape))
    block = pl.BlockSpec((1, length, width), lambda j: (blocks - 1 - j, 0, 0))
    edge = pl.BlockSpec(
        (1, TILE, width), lambda j: (jnp.maximum(blocks - 2 - j, 0), last, 0)
    )
    low = jax.ShapeDtypeStruct((blocks, length, width), bf16)
    tile = jax.ShapeDtypeStruct((TILE, width), f32)
    count = 4 + taps.shape[0]
    return pl.pallas_call(
        backward_kernel,
        grid_spec=pltpu.PrefetchScalarGridSpec(
            num_scalar_prefetch=0,
            grid=(blocks,),
            in_specs=[
                block,
                block,
                edge,
                block,
                block,
                block,
                block,
                edge,
                pl.BlockSpec((length, masks.shape[1]), lambda j: (blocks - 1 - j, 0)),
                whole(*rim.shape),
                whole(*state_in.shape),
                whole(*after.shape),
                whole(*taps.shape),
                whole(*vecs.shape),
                whole(*rate_dense.shape),
                whole(*input_dense.shape),
            ],
            out_specs=[
                block,
                block,
                block,
                whole(TILE, width),
                whole(TILE, width),
                whole(count, width),
            ],
            scratch_shapes=[
                pltpu.VMEM((TILE, width), f32),
                pltpu.VMEM((taps.shape[0] - 1, TILE, width), f32),
                pltpu.VMEM((count, TILE, width), f32),
                pltpu.VMEM((length, width), f32),
                pltpu.VMEM((length, width), f32),
                pltpu.VMEM((length, width), f32),
            ],
        ),
        out_shape=[low, low, low, tile, tile, jax.ShapeDtypeStruct((count, width), f32)],
        compiler_params=pltpu.CompilerParams(vmem_limit_bytes=VMEM_LIMIT),
        cost_estimate=pl.CostEstimate(flops=1000, bytes_accessed=1000, transcendentals=0),
        name="recur_backward",
    )(
        direct,
        state,
        state,
        conv,
        sig_rate,
        sig_input,
        inner,
        inner,
        masks,
        rim,
        state_in,
        after,
        taps,
        vecs,
        rate_dense,
        input_dense,
    )


def dense_blocks(blocks):
    count, rows_in, cols_out = blocks.shape
    tall = blocks.reshape(count * rows_in, cols_out)
    wide = jnp.concatenate([tall] * count, axis=1)
    row = lax.broadcasted_iota(jnp.int32, wide.shape, 0) // rows_in
    col = lax.broadcasted_iota(jnp.int32, wide.shape, 1) // cols_out
    return jnp.where(row == col, wide, jnp.zeros_like(wide))


def diagonal_blocks(full, count):
    rows, cols = full.shape[0] // count, full.shape[1] // count
    return jnp.stack([full[i * rows : (i + 1) * rows, i * cols : (i + 1) * cols] for i in range(count)])


def rms(values):
    return lax.rsqrt(jnp.mean(values * values, axis=-1, keepdims=True) + epsilon)


def norm_back(grad, xhat, scale, root):
    e = grad * scale
    return root * (e - xhat * jnp.mean(e * xhat, axis=-1, keepdims=True)), jnp.sum(grad * xhat, axis=0)


def shards(
    tokens,
    mixer_gain,
    in_proj,
    branch_proj,
    conv_taps,
    conv_bias,
    rate_blocks,
    rate_bias,
    input_blocks,
    input_bias,
    decay_param,
    out_proj,
    dense_gain,
    gate_proj,
    up_proj,
    down_proj,
    segment_ids,
    cotangent,
):
    tp_place = lax.axis_index("tp")
    seq_place = lax.axis_index("seq")
    seq_size = lax.axis_size("seq")
    core = seq_place % 2
    tp_size = lax.axis_size("tp")
    gain_share = mixer_gain.shape[0]
    taps_n, width = conv_taps.shape
    rim_width = taps_n - 1
    length, model = tokens.shape
    group = length * tp_size
    blocks_n = rate_blocks.shape[0]

    in_t, branch_t = in_proj.T, branch_proj.T
    place = tp_place.astype(jnp.int32)[None]

    blocks = [tokens] + [swap(tokens, "tp", r) for r in range(1, tp_size)]
    blocks[1], gains, ids, rate_in, input_in, vec_in = tied(
        blocks[1],
        jnp.stack([mixer_gain, dense_gain]),
        segment_ids,
        rate_blocks,
        input_blocks,
        (conv_bias, rate_bias, input_bias, decay_param),
    )
    gains = gather_rows(gains)
    gains = gains.transpose(1, 0, 2).reshape(2, -1).astype(f32)
    mixer_scale, dense_scale = gains[0], gains[1]
    rim_ids = from_neighbour(ids[-rim_width:], -1)
    ext_ids = jnp.concatenate([rim_ids, ids])
    same = [ext_ids[rim_width - k : rim_width - k + group] == ids for k in range(1, taps_n)]
    masks = jnp.stack([same[0]] + same, axis=1).astype(f32)
    rate_dense = dense_blocks(rate_in)
    input_dense = dense_blocks(input_in)
    vecs = jnp.stack([*vec_in[:3], -8.0 * jax.nn.softplus(-vec_in[3])])
    *blocks, masks, rate_dense, input_dense, vecs = tied(*blocks, masks, rate_dense, input_dense, vecs)
    cot_all = lax.all_gather(cotangent, ("seq", "tp"), axis=0, tiled=True)

    normed, inner = norm_project(blocks, place, mixer_scale[None], in_t)
    rim = from_neighbour(inner[-1, -TILE:], -1)
    conv, conv_low, sig_rate, sig_input, keep_prefix, value_prefix, ends = recur_forward(
        inner, masks, rim, conv_taps, vecs, rate_dense, input_dense
    )
    ends, normed_b = tied(ends, normed)
    state_in = carry_in(ends[0, 0], ends[1, 0], False)
    branch_pre = project_t(normed_b, branch_t).reshape(inner.shape)
    state, mixed, mixer_part = mix_out(value_prefix, keep_prefix, branch_pre, state_in[None], out_proj)
    mixed = mixed.reshape(group, width)
    mixer_out = scatter_rows(mixer_part)
    mid = tokens.astype(f32) + mixer_out
    mid_root = rms(mid)
    xhat_dense = mid * mid_root
    normed_two = (xhat_dense * dense_scale).astype(bf16)

    chips = seq_size // 2
    same_core = [[core_no + 2 * i for i in range(chips)] for core_no in range(2)]
    rows_z = lax.all_gather(normed_two, "seq", axis=0, tiled=True, axis_index_groups=same_core)
    rows_two, cot_all = tied(gather_rows(normed_two).reshape(group, model), cot_all)
    hidden, normed_two_part = dense_rows(
        rows_two, cot_all, seq_place.astype(jnp.int32)[None], gate_proj, up_proj, down_proj
    )
    normed_two_grad = scatter_rows(normed_two_part.reshape(tp_size, length, model))
    dense_part = product(hidden, down_proj).astype(bf16)
    normed_two_grad, dense_part, rows_z = tied(normed_two_grad, dense_part, rows_z)
    rows_mine = lax.all_gather(rows_z, "tp", axis=0, tiled=True)
    mid_from_norm, dense_gain_part = norm_back(normed_two_grad, xhat_dense, dense_scale, mid_root)
    mid_grad = cotangent.astype(f32) + mid_from_norm
    mid_blocks = gather_rows(mid_grad.astype(bf16))
    mid_blocks, dense_part = tied(mid_blocks, dense_part)

    dense_out = scatter_rows(dense_part.reshape(tp_size, length, model))
    direct, branch_pre_grad, reach = mix_back(mid_blocks, out_proj, branch_pre, state, keep_prefix)
    branch_pre_grad = branch_pre_grad.reshape(group, width)
    mid_rows = mid_blocks.reshape(group, model)
    reach, direct, branch_pre_grad, mid_rows = tied(reach[0], direct, branch_pre_grad, mid_rows)
    after = carry_in(ends[0, 0], reach, True)
    out_full = product_left_t(mixed, mid_rows).astype(bf16)
    branch_full = product_left_t(branch_pre_grad, normed).astype(bf16)
    after, out_full, branch_full = tied(after, out_full, branch_full)
    out_sum, branch_sum = lax.psum((out_full, branch_full), "seq")
    tile = lambda v: jnp.broadcast_to(v, (TILE, width))
    rate_low, input_low, inner_grad, tail, rim_grad, sums = recur_backward(
        direct,
        state,
        conv,
        sig_rate,
        sig_input,
        inner,
        masks,
        rim,
        tile(state_in),
        tile(after),
        conv_taps,
        vecs,
        rate_dense,
        input_dense,
    )
    rim_grad, rows_mine = tied(rim_grad, rows_mine)
    fixed = tail + from_neighbour(rim_grad, 1)
    low_rows = conv_low.reshape(group, width)
    rate_w = diagonal_blocks(product_left_t(low_rows, rate_low.reshape(group, width)), blocks_n)
    input_w = diagonal_blocks(product_left_t(low_rows, input_low.reshape(group, width)), blocks_n)
    inner_grad = lax.dynamic_update_slice(
        inner_grad, fixed.astype(bf16)[None], (tp_size - 1, length - TILE, 0)
    ).reshape(group, width)
    in_full = product_left_t(inner_grad, normed).astype(bf16)
    block_full = jnp.concatenate([rate_w, input_w]).astype(bf16)
    normed_part = (product(inner_grad, in_t) + product(branch_pre_grad, branch_t)).astype(bf16)
    rows_theirs = swap(rows_mine, "seq", 1)
    normed_part, in_full, block_full, rows_theirs, dense_out = tied(
        normed_part, in_full, block_full, rows_theirs, dense_out
    )
    in_sum, block_sum = lax.psum((in_full, block_full), "seq", axis_index_groups=[list(range(seq_size))[::-1]])
    normed_grad = scatter_rows(normed_part.reshape(tp_size, length, model))

    core_no = core.astype(jnp.int32)[None]
    blocked = lambda rows: rows.reshape(tp_size, chips, length, model)
    gate_w, up_w, down_w = dense_weight_grads(
        blocked(rows_mine), blocked(rows_theirs), cot_all, gate_proj, up_proj, down_proj, core_no
    )
    gate_w, up_w, down_w, out_sum, branch_sum, normed_grad = tied(
        gate_w, up_w, down_w, out_sum, branch_sum, normed_grad
    )
    gate_sum = joined(gate_w, swap(gate_w, "seq", 1), core_no, 1)
    up_sum = joined(up_w, swap(up_w, "seq", 1), core_no, 1)
    down_sum = joined(down_w, swap(down_w, "seq", 1), core_no, 0)
    gate_sum, up_sum, down_sum, in_sum, block_sum = tied(gate_sum, up_sum, down_sum, in_sum, block_sum)

    output = (mid + dense_out).astype(bf16)
    own = tokens.astype(f32)
    own_root = rms(own)
    rows_grad, mixer_gain_part = norm_back(normed_grad, own * own_root, mixer_scale, own_root)
    tokens_grad = mid_grad + rows_grad
    gain_parts = sum_bits(jnp.stack([mixer_gain_part, dense_gain_part]), "tp")
    gain_own = lax.dynamic_slice_in_dim(gain_parts, tp_place * gain_share, gain_share, 1)
    gain_sum = sum_bits(gain_own, "seq")
    sums = sum_bits(sums, "seq")
    decay_sum = 8.0 * jax.nn.sigmoid(-decay_param) * sums[2]
    rate_sum, input_sum = block_sum[:blocks_n].astype(f32), block_sum[blocks_n:].astype(f32)
    return (
        output,
        tokens_grad,
        gain_sum[0],
        in_sum.astype(f32).T,
        branch_sum.astype(f32).T,
        sums[4 : 4 + taps_n],
        sums[3],
        rate_sum,
        sums[0],
        input_sum,
        sums[1],
        decay_sum,
        out_sum.astype(f32),
        gain_sum[1],
        gate_sum,
        up_sum,
        down_sum,
    )


def solution(mesh):
    return jax.shard_map(
        shards,
        mesh=mesh,
        in_specs=(
            P(("seq", "tp"), None),
            P("tp"),
            P(None, "tp"),
            P(None, "tp"),
            P(None, "tp"),
            P("tp"),
            P("tp", None, None),
            P("tp"),
            P("tp", None, None),
            P("tp"),
            P("tp"),
            P("tp", None),
            P("tp"),
            P(None, "tp"),
            P(None, "tp"),
            P("tp", None),
            P("seq"),
            P(("seq", "tp"), None),
        ),
        out_specs=(
            P(("seq", "tp"), None),
            P(("seq", "tp"), None),
            P("tp"),
            P(None, "tp"),
            P(None, "tp"),
            P(None, "tp"),
            P("tp"),
            P("tp", None, None),
            P("tp"),
            P("tp", None, None),
            P("tp"),
            P("tp"),
            P("tp", None),
            P("tp"),
            P(None, "tp"),
            P(None, "tp"),
            P("tp", None),
        ),
        check_vma=False,
    )
```

```python
import math

import jax
import jax.numpy as jnp
from jax import lax
from jax.experimental import pallas as pl
from jax.experimental.pallas import tpu as pltpu
from jax.sharding import PartitionSpec as P

epsilon = 1e-06
f32 = jnp.float32
bf16 = jnp.bfloat16
TILE = 8
VMEM_LIMIT = 50 * 1024 * 1024


def product(left, right):
    return jnp.dot(left, right, preferred_element_type=f32)


def product_left_t(left, right):
    return lax.dot_general(left, right, (((0,), (0,)), ((), ())), preferred_element_type=f32)


def product_right_t(left, right):
    return lax.dot_general(left, right, (((1,), (1,)), ((), ())), preferred_element_type=f32)


def gelu_tanh(values):
    return jax.nn.gelu(values, approximate=True)


def tied(*values):
    return lax.optimization_barrier(values)


def swap(value, axis, bit):
    count = lax.axis_size(axis)
    return lax.ppermute(value, axis, [(i, i ^ bit) for i in range(count)])


def gather_rows(rows):
    count = lax.axis_size("tp")
    place = lax.axis_index("tp")
    whole = jnp.zeros((count,) + rows.shape, rows.dtype)
    for r in range(count):
        block = rows if r == 0 else swap(rows, "tp", r)
        whole = lax.dynamic_update_index_in_dim(whole, block, place ^ r, 0)
    return whole


def spread(rows):
    count = lax.axis_size("tp")
    if count != 4:
        whole = jnp.stack([rows] + [swap(rows, "tp", r) for r in range(1, count)])
        return lambda *after: tied(whole, *after)
    half = rows.shape[0] // 2
    sides = swap(rows, "tp", 1), swap(rows, "tp", 2)

    def finish(*after):
        one, two, *after = tied(*sides, *after)
        far = jnp.concatenate([swap(two[:half], "tp", 1), swap(one[half:], "tp", 2)])
        return (jnp.stack([rows, one, two, far]), *after)

    return finish


def scatter_rows(blocks):
    place = lax.axis_index("tp")
    block = lambda r: lax.dynamic_index_in_dim(blocks, place ^ r, 0, False)
    total = block(0).astype(f32)
    for r in range(1, lax.axis_size("tp")):
        total = total + swap(block(r), "tp", r).astype(f32)
    return total


def carry_in(keep_total, value_total, backward):
    place = lax.axis_index("seq")
    total = jnp.stack([keep_total, value_total])
    before = jnp.stack([jnp.ones_like(keep_total), jnp.zeros_like(value_total)])
    bit = 1
    while bit < lax.axis_size("seq"):
        other = swap(total, "seq", bit)
        upper = (place & bit) != 0
        earlier = jnp.logical_not(upper) if backward else upper
        joined_before = jnp.stack([other[0] * before[0], before[0] * other[1] + before[1]])
        before = jnp.where(earlier, joined_before, before)
        first = jnp.where(earlier, other, total)
        second = jnp.where(earlier, total, other)
        total = jnp.stack([first[0] * second[0], second[0] * first[1] + second[1]])
        bit *= 2
    return before[1]


def from_neighbour(value, step):
    count = lax.axis_size("seq")
    place = lax.axis_index("seq")
    inside = lax.ppermute(value, "seq", [(i, i ^ 1) for i in range(count)])
    pairs = [(i, i + 1) for i in range(1, count - 1, 2)] + [(i + 1, i) for i in range(1, count - 1, 2)]
    across = lax.ppermute(value, "seq", pairs)
    return jnp.where((place % 2 == 0) == (step == 1), inside, across)


def sum_bits(value, axis):
    bit = 1
    while bit < lax.axis_size(axis):
        value = value + swap(value, axis, bit)
        bit *= 2
    return value


def both_halves(mine, theirs, core):
    first = jnp.where(core == 0, mine, theirs)
    second = jnp.where(core == 0, theirs, mine)
    return first, second


def gelu_grads(gate_pre, up_pre, hidden_grad):
    square = gate_pre * gate_pre
    inner = math.sqrt(2.0 / math.pi) * gate_pre * (1.0 + 0.044715 * square)
    half = 0.5 * (1.0 + jnp.tanh(inner))
    act = gate_pre * half
    slope = half + 2.0 * math.sqrt(2.0 / math.pi) * act * (1.0 - half) * (1.0 + 3.0 * 0.044715 * square)
    return act * up_pre, hidden_grad * up_pre * slope, hidden_grad * act


def dense_weight_grads(mine, theirs, cot_all, gate_proj, up_proj, down_proj, places, half, base):
    tp_size, chips, block, model = mine.shape
    cot_all = cot_all.reshape(chips, 2, tp_size, block, model)
    part = math.gcd(chips, 4)
    length = part * block
    per_core = tp_size * chips // part
    steps, outs = 2 * per_core, 4
    tile = math.gcd(half, 256)
    left_t = (((0,), (0,)), ((), ()))
    right_t = (((1,), (1,)), ((), ()))

    def kernel(core_ref, mine_ref, theirs_ref, cot_ref, gate_ref, up_ref, down_ref, *rest):
        gate_out, up_out, down_out, acc_g, acc_u, acc_d, hid, gg, ug, x_ref = rest
        i = pl.program_id(0)

        @pl.when(i < per_core)
        def _():
            x_ref[...] = mine_ref[...].reshape(length, model)

        @pl.when(jnp.logical_and(i >= per_core, i < steps))
        def _():
            x_ref[...] = theirs_ref[...].reshape(length, model)

        @pl.when(i == 0)
        def _():
            acc_g[...] = jnp.zeros_like(acc_g)
            acc_u[...] = jnp.zeros_like(acc_u)
            acc_d[...] = jnp.zeros_like(acc_d)

        @pl.when(i < steps)
        def _():
            cots = cot_ref[...].reshape(length, model)
            for n in range(half // tile):
                cols = slice(n * tile, (n + 1) * tile)
                gate_pre = jnp.dot(x_ref[...], gate_ref[:, cols], preferred_element_type=f32)
                up_pre = jnp.dot(x_ref[...], up_ref[:, cols], preferred_element_type=f32)
                hidden_grad = lax.dot_general(cots, down_ref[cols, :], right_t, preferred_element_type=f32)
                a, b, c = gelu_grads(gate_pre, up_pre, hidden_grad)
                hid[:, cols] = a.astype(bf16)
                gg[:, cols] = b.astype(bf16)
                ug[:, cols] = c.astype(bf16)
            acc_g[...] += lax.dot_general(x_ref[...], gg[...], left_t, preferred_element_type=f32)
            acc_u[...] += lax.dot_general(x_ref[...], ug[...], left_t, preferred_element_type=f32)
            acc_d[...] += lax.dot_general(hid[...], cots, left_t, preferred_element_type=f32)

        @pl.when(i >= steps)
        def _():
            wide = pl.ds(pl.multiple_of((i - steps) * (model // outs), model // outs), model // outs)
            low = pl.ds(pl.multiple_of((i - steps) * (half // outs), half // outs), half // outs)
            gate_out[...] = acc_g[wide, :].astype(bf16)
            up_out[...] = acc_u[wide, :].astype(bf16)
            down_out[...] = acc_d[low, :].astype(bf16)

    once = pl.Buffered(1)
    groups = chips // part
    out_index = lambda i, c: (jnp.maximum(i - steps, 0), 0)

    def cot_index(i, c):
        i = jnp.minimum(i, steps - 1)
        n = i % per_core
        return n % groups, c[0] ^ (i // per_core), c[1] ^ (n // groups), 0, 0

    def rows_index(first):
        def index(i, c):
            n = jnp.clip(i - first, 0, per_core - 1)
            return n // groups, n % groups, 0, 0

        return pl.BlockSpec((1, part, block, model), index)

    return pl.pallas_call(
        kernel,
        grid_spec=pltpu.PrefetchScalarGridSpec(
            num_scalar_prefetch=1,
            grid=(steps + outs,),
            in_specs=[
                rows_index(0),
                rows_index(per_core),
                pl.BlockSpec((part, 1, 1, block, model), cot_index),
                pl.BlockSpec((model, half), lambda i, c: (0, base + c[0]), pipeline_mode=once),
                pl.BlockSpec((model, half), lambda i, c: (0, base + c[0]), pipeline_mode=once),
                pl.BlockSpec((half, model), lambda i, c: (base + c[0], 0), pipeline_mode=once),
            ],
            out_specs=[
                pl.BlockSpec((model // outs, half), out_index),
                pl.BlockSpec((model // outs, half), out_index),
                pl.BlockSpec((half // outs, model), out_index),
            ],
            scratch_shapes=[
                pltpu.VMEM((model, half), f32),
                pltpu.VMEM((model, half), f32),
                pltpu.VMEM((half, model), f32),
                pltpu.VMEM((length, half), bf16),
                pltpu.VMEM((length, half), bf16),
                pltpu.VMEM((length, half), bf16),
                pltpu.VMEM((length, model), bf16),
            ],
        ),
        out_shape=[
            jax.ShapeDtypeStruct((model, half), bf16),
            jax.ShapeDtypeStruct((model, half), bf16),
            jax.ShapeDtypeStruct((half, model), bf16),
        ],
        compiler_params=pltpu.CompilerParams(vmem_limit_bytes=60 * 1024 * 1024),
        cost_estimate=pl.CostEstimate(flops=1000, bytes_accessed=1000, transcendentals=0),
        name="dense_weight_grads",
    )(places, mine, theirs, cot_all, gate_proj, up_proj, down_proj)


def joined(big, small, core, axis):
    sizes = [pair[0].shape[axis] for pair in (big, small)]
    total = 2 * sum(sizes)
    other = big[0].shape[1 - axis]
    block = math.gcd(other, 256)

    def kernel(core_ref, *refs):
        out_ref = refs[-1]
        for low in range(2):

            @pl.when(core_ref[0] == low)
            def _(low=low):
                first = 0
                for n, size in enumerate(sizes):
                    for half in range(2):
                        source = refs[2 * n + (half ^ low)]
                        at = slice(first, first + size)
                        if axis == 1:
                            out_ref[:, at] = source[...].astype(f32)
                        else:
                            out_ref[at, :] = source[...].astype(f32)
                        first += size

    if axis == 1:
        spec = lambda size: pl.BlockSpec((block, size), lambda i, c: (i, 0))
        out_shape = (other, total)
    else:
        spec = lambda size: pl.BlockSpec((size, block), lambda i, c: (0, i))
        out_shape = (total, other)
    return pl.pallas_call(
        kernel,
        grid_spec=pltpu.PrefetchScalarGridSpec(
            num_scalar_prefetch=1,
            grid=(other // block,),
            in_specs=[spec(sizes[0])] * 2 + [spec(sizes[1])] * 2,
            out_specs=spec(total),
        ),
        out_shape=jax.ShapeDtypeStruct(out_shape, f32),
        compiler_params=pltpu.CompilerParams(vmem_limit_bytes=VMEM_LIMIT),
        cost_estimate=pl.CostEstimate(flops=1000, bytes_accessed=1000, transcendentals=0),
        name="joined",
    )(core, *big, *small)


def dense_rows(rows, cot_all, group_place, gate_proj, up_proj, down_proj):
    length, model = rows.shape
    width = gate_proj.shape[1]
    tile = math.gcd(width, 256)
    out_tile = math.gcd(model, 256)
    first, second = width // tile, model // out_tile
    right_t = (((1,), (1,)), ((), ()))

    def kernel(place_ref, x_ref, c_ref, gate_ref, up_ref, down_ref, hidden_ref, grad_ref, gates, ups, gate_grads, up_grads):
        j = pl.program_id(0)

        @pl.when(j < first)
        def _():
            gate_pre = jnp.dot(x_ref[...], gate_ref[...], preferred_element_type=f32)
            up_pre = jnp.dot(x_ref[...], up_ref[...], preferred_element_type=f32)
            hidden_grad = lax.dot_general(c_ref[...], down_ref[...], right_t, preferred_element_type=f32)
            hidden, gate_grad, up_grad = gelu_grads(gate_pre, up_pre, hidden_grad)
            hidden_ref[...] = hidden.astype(bf16)
            at = pl.ds(pl.multiple_of(j * tile, tile), tile)
            gates[:, at] = gate_ref[...]
            ups[:, at] = up_ref[...]
            gate_grads[:, at] = gate_grad.astype(bf16)
            up_grads[:, at] = up_grad.astype(bf16)

        @pl.when(j >= first)
        def _():
            at = pl.ds(pl.multiple_of((j - first) * out_tile, out_tile), out_tile)
            part = lax.dot_general(gate_grads[...], gates[at, :], right_t, preferred_element_type=f32)
            part = part + lax.dot_general(up_grads[...], ups[at, :], right_t, preferred_element_type=f32)
            grad_ref[...] = part.astype(bf16)

    clamp = lambda j: jnp.minimum(j, first - 1)
    wide = pl.BlockSpec((model, tile), lambda j, p: (0, clamp(j)))
    return pl.pallas_call(
        kernel,
        grid_spec=pltpu.PrefetchScalarGridSpec(
            num_scalar_prefetch=1,
            grid=(first + second,),
            in_specs=[
                pl.BlockSpec((length, model), lambda j, p: (0, 0)),
                pl.BlockSpec((length, model), lambda j, p: (p[0], 0)),
                wide,
                wide,
                pl.BlockSpec((tile, model), lambda j, p: (clamp(j), 0)),
            ],
            out_specs=[
                pl.BlockSpec((length, tile), lambda j, p: (0, clamp(j))),
                pl.BlockSpec((length, out_tile), lambda j, p: (0, jnp.maximum(j - first, 0))),
            ],
            scratch_shapes=[
                pltpu.VMEM((model, width), bf16),
                pltpu.VMEM((model, width), bf16),
                pltpu.VMEM((length, width), bf16),
                pltpu.VMEM((length, width), bf16),
            ],
        ),
        out_shape=[
            jax.ShapeDtypeStruct((length, width), bf16),
            jax.ShapeDtypeStruct((length, model), bf16),
        ],
        compiler_params=pltpu.CompilerParams(vmem_limit_bytes=VMEM_LIMIT),
        name="dense_rows",
    )(group_place, rows, cot_all, gate_proj, up_proj, down_proj)


def project_t(rows, weight_t):
    total, model = rows.shape
    width = weight_t.shape[0]
    length = math.gcd(total, 256)

    def kernel(rows_ref, weight_ref, out_ref):
        out_ref[...] = lax.dot_general(
            rows_ref[...], weight_ref[...], (((1,), (1,)), ((), ())), preferred_element_type=f32
        )

    return pl.pallas_call(
        kernel,
        grid=(total // length,),
        in_specs=[
            pl.BlockSpec((length, model), lambda j: (j, 0)),
            pl.BlockSpec((width, model), lambda j: (0, 0)),
        ],
        out_specs=pl.BlockSpec((length, width), lambda j: (j, 0)),
        out_shape=jax.ShapeDtypeStruct((total, width), f32),
        compiler_params=pltpu.CompilerParams(vmem_limit_bytes=VMEM_LIMIT),
        name="project_t",
    )(rows, weight_t)


def mix_out(value_prefix, keep_prefix, branch_pre, state_in, out_proj):
    blocks, length, width = value_prefix.shape
    model = out_proj.shape[1]

    def kernel(value_ref, keep_ref, branch_ref, in_ref, out_ref, state_ref, mixed_ref, part_ref):
        state = value_ref[0] + keep_ref[0] * in_ref[...]
        state_ref[0] = state
        mixed = (state * gelu_tanh(branch_ref[0])).astype(bf16)
        mixed_ref[0] = mixed
        part_ref[0] = jnp.dot(mixed, out_ref[...], preferred_element_type=f32).astype(bf16)

    block = pl.BlockSpec((1, length, width), lambda j: (j, 0, 0))
    whole = lambda *shape: pl.BlockSpec(shape, lambda j: (0,) * len(shape))
    return pl.pallas_call(
        kernel,
        grid=(blocks,),
        in_specs=[block, block, block, whole(1, width), whole(width, model)],
        out_specs=[block, block, pl.BlockSpec((1, length, model), lambda j: (j, 0, 0))],
        out_shape=[
            jax.ShapeDtypeStruct((blocks, length, width), f32),
            jax.ShapeDtypeStruct((blocks, length, width), bf16),
            jax.ShapeDtypeStruct((blocks, length, model), bf16),
        ],
        compiler_params=pltpu.CompilerParams(vmem_limit_bytes=VMEM_LIMIT),
        name="mix_out",
    )(value_prefix, keep_prefix, branch_pre, state_in, out_proj)


def mix_back(mid_rows, out_proj, branch_pre, state, keep_prefix):
    blocks, length, width = state.shape
    model = out_proj.shape[1]
    tiles = length // 16

    def kernel(mid_ref, out_ref, branch_ref, state_ref, keep_ref, direct_ref, branch_grad_ref, reach_ref, mixed, acc):
        j = pl.program_id(0)
        mixed[...] = lax.dot_general(
            mid_ref[0], out_ref[...], (((1,), (1,)), ((), ())), preferred_element_type=f32
        )

        @pl.when(j == 0)
        def _():
            acc[...] = jnp.zeros_like(acc)

        def tile(i, total):
            at = pl.ds(pl.multiple_of(i * 16, 16), 16)
            grad = mixed[at, :]
            pre = branch_ref[0, at, :]
            square = pre * pre
            inner = math.sqrt(2.0 / math.pi) * pre * (1.0 + 0.044715 * square)
            half = 0.5 * (1.0 + jnp.tanh(inner))
            act = pre * half
            slope = half + 2.0 * math.sqrt(2.0 / math.pi) * act * (1.0 - half) * (1.0 + 3.0 * 0.044715 * square)
            direct = grad * act
            direct_ref[0, at, :] = direct
            branch_grad_ref[0, at, :] = (grad * state_ref[0, at, :] * slope).astype(bf16)
            return total + direct * keep_ref[0, at, :]

        acc[...] = lax.fori_loop(0, tiles, tile, acc[...])

        @pl.when(j == blocks - 1)
        def _():
            reach_ref[...] = jnp.sum(acc[...], axis=0, keepdims=True)

    block = pl.BlockSpec((1, length, width), lambda j: (j, 0, 0))
    whole = lambda *shape: pl.BlockSpec(shape, lambda j: (0,) * len(shape))
    return pl.pallas_call(
        kernel,
        grid=(blocks,),
        in_specs=[pl.BlockSpec((1, length, model), lambda j: (j, 0, 0)), whole(width, model), block, block, block],
        out_specs=[block, block, whole(1, width)],
        out_shape=[
            jax.ShapeDtypeStruct((blocks, length, width), f32),
            jax.ShapeDtypeStruct((blocks, length, width), bf16),
            jax.ShapeDtypeStruct((1, width), f32),
        ],
        scratch_shapes=[pltpu.VMEM((length, width), f32), pltpu.VMEM((16, width), f32)],
        compiler_params=pltpu.CompilerParams(vmem_limit_bytes=VMEM_LIMIT),
        name="mix_back",
    )(mid_rows, out_proj, branch_pre, state, keep_prefix)


def minus_expm1(x):
    series = 1.0 / 40320.0
    for term in (1.0 / 5040.0, 1.0 / 720.0, 1.0 / 120.0, 1.0 / 24.0, 1.0 / 6.0, 0.5, 1.0):
        series = series * x + term
    return jnp.where(x > -0.35, -x * series, 1.0 - jnp.exp(x))


def rows_of(shape):
    return lax.broadcasted_iota(jnp.int32, shape, 0)


def down(cur, prev, by, row):
    return jnp.where(row >= by, pltpu.roll(cur, by, 0), pltpu.roll(prev, by, 0))


def up(cur, after, by, row):
    return jnp.where(row < TILE - by, pltpu.roll(cur, TILE - by, 0), pltpu.roll(after, TILE - by, 0))


def last_row(tile):
    return jnp.broadcast_to(tile[TILE - 1 :, :], tile.shape)


def first_row(tile):
    return jnp.broadcast_to(tile[:1, :], tile.shape)


def forward_kernel(
    inner_ref,
    mask_ref,
    rim_ref,
    taps_ref,
    vec_ref,
    rate_ref,
    input_ref,
    conv_ref,
    low_ref,
    sig_rate_ref,
    sig_input_ref,
    keep_ref,
    value_ref,
    end_ref,
    prev_ref,
    carry_ref,
    rate_raw_ref,
    input_raw_ref,
):
    step = pl.program_id(0)
    length, width = inner_ref.shape[1:]
    tiles = length // TILE
    taps_n = taps_ref.shape[0]

    @pl.when(step == 0)
    def _():
        prev_ref[...] = rim_ref[...]
        carry_ref[0] = jnp.ones((TILE, width), f32)
        carry_ref[1] = jnp.zeros((TILE, width), f32)

    row = rows_of((TILE, width))

    def conv_tile(i, prev):
        at = pl.ds(pl.multiple_of(i * TILE, TILE), TILE)
        cur = inner_ref[0, at, :]
        masks = mask_ref[at, :]
        total = vec_ref[0:1, :] + taps_ref[0:1, :] * cur
        for k in range(1, taps_n):
            total = total + taps_ref[k : k + 1, :] * (down(cur, prev, k, row) * masks[:, k : k + 1])
        conv_ref[0, at, :] = total
        return cur

    prev_ref[...] = lax.fori_loop(0, tiles, conv_tile, prev_ref[...])
    low = conv_ref[0].astype(bf16)
    low_ref[0] = low
    rate_raw_ref[...] = jnp.dot(low, rate_ref[...], preferred_element_type=f32)
    input_raw_ref[...] = jnp.dot(low, input_ref[...], preferred_element_type=f32)

    def gate_tile(i, carry):
        keep_in, value_in = carry
        at = pl.ds(pl.multiple_of(i * TILE, TILE), TILE)
        sig_rate = jax.nn.sigmoid(rate_raw_ref[at, :] + vec_ref[1:2, :])
        sig_input = jax.nn.sigmoid(input_raw_ref[at, :] + vec_ref[2:3, :])
        sig_rate_ref[0, at, :] = sig_rate
        sig_input_ref[0, at, :] = sig_input
        log_decay = sig_rate * vec_ref[3:4, :]
        a = jnp.exp(log_decay) * mask_ref[at, 0:1]
        b = jnp.sqrt(minus_expm1(2.0 * log_decay)) * sig_input * conv_ref[0, at, :]
        for d in (1, 2, 4):
            a_before = jnp.where(row >= d, pltpu.roll(a, d, 0), 1.0)
            b_before = jnp.where(row >= d, pltpu.roll(b, d, 0), 0.0)
            b = b + a * b_before
            a = a * a_before
        b = b + a * value_in
        a = a * keep_in
        keep_ref[0, at, :] = a
        value_ref[0, at, :] = b
        return last_row(a), last_row(b)

    keep_end, value_end = lax.fori_loop(0, tiles, gate_tile, (carry_ref[0], carry_ref[1]))
    carry_ref[0] = keep_end
    carry_ref[1] = value_end
    end_ref[0] = keep_end
    end_ref[1] = value_end


def backward_kernel(
    direct_ref,
    state_ref,
    state_prev_ref,
    conv_ref,
    sig_rate_ref,
    sig_input_ref,
    inner_ref,
    inner_prev_ref,
    mask_ref,
    rim_ref,
    state_in_ref,
    after_ref,
    taps_ref,
    vec_ref,
    rate_ref,
    input_ref,
    rate_grad_ref,
    input_grad_ref,
    inner_grad_ref,
    tail_ref,
    rim_grad_ref,
    sums_ref,
    carry_ref,
    next_ref,
    acc_ref,
    rate_f_ref,
    input_f_ref,
    conv_f_ref,
):
    step = pl.program_id(0)
    steps = pl.num_programs(0)
    length, width = direct_ref.shape[1:]
    tiles = length // TILE
    taps_n = taps_ref.shape[0]
    row = rows_of((TILE, width))
    is_first_block = step == steps - 1

    @pl.when(step == 0)
    def _():
        carry_ref[...] = after_ref[...]
        next_ref[...] = jnp.zeros_like(next_ref)
        acc_ref[...] = jnp.zeros_like(acc_ref)

    edge_state = jnp.where(is_first_block, state_in_ref[...], state_prev_ref[0])
    edge_inner = jnp.where(is_first_block, rim_ref[...], inner_prev_ref[0])
    neg_rate = vec_ref[3:4, :]

    def gate_tile(n, carry):
        after, acc_rate, acc_input, acc_decay = carry
        i = tiles - 1 - n
        at = pl.ds(pl.multiple_of(i * TILE, TILE), TILE)
        before = pl.ds(pl.multiple_of(jnp.maximum(i - 1, 0) * TILE, TILE), TILE)
        direct = direct_ref[0, at, :]
        sig_rate = sig_rate_ref[0, at, :]
        sig_input = sig_input_ref[0, at, :]
        conv = conv_ref[0, at, :]
        log_decay = sig_rate * neg_rate
        decay = jnp.exp(log_decay)
        keep = decay * mask_ref[at, 0:1]
        room = minus_expm1(2.0 * log_decay)
        root = jnp.sqrt(room)
        a = keep
        b = keep * direct
        for d in (1, 2, 4):
            a_after = jnp.where(row < TILE - d, pltpu.roll(a, TILE - d, 0), 1.0)
            b_after = jnp.where(row < TILE - d, pltpu.roll(b, TILE - d, 0), 0.0)
            b = b + a * b_after
            a = a * a_after
        reach = b + a * after
        grad = direct + up(reach, after, 1, row)
        prev_tile = jnp.where(i == 0, edge_state, state_ref[0, before, :])
        state_prev = down(state_ref[0, at, :], prev_tile, 1, row)
        grad_root = grad * root
        gated = grad_root * sig_input
        decay_grad = grad * (keep * state_prev - sig_input * conv * (decay * decay) / root)
        rate_grad = decay_grad * neg_rate * (sig_rate * (1.0 - sig_rate))
        input_grad = gated * conv * (1.0 - sig_input)
        rate_f_ref[at, :] = rate_grad
        input_f_ref[at, :] = input_grad
        conv_f_ref[at, :] = gated
        return (
            first_row(reach),
            acc_rate + rate_grad,
            acc_input + input_grad,
            acc_decay + decay_grad * sig_rate,
        )

    after, acc_rate, acc_input, acc_decay = lax.fori_loop(
        0, tiles, gate_tile, (carry_ref[...], acc_ref[0], acc_ref[1], acc_ref[2])
    )
    carry_ref[...] = after
    acc_ref[0] = acc_rate
    acc_ref[1] = acc_input
    acc_ref[2] = acc_decay
    rate_low = rate_f_ref[...].astype(bf16)
    input_low = input_f_ref[...].astype(bf16)
    rate_grad_ref[0] = rate_low
    input_grad_ref[0] = input_low
    right_t = (((1,), (1,)), ((), ()))
    conv_f_ref[...] += lax.dot_general(
        rate_low, rate_ref[...], right_t, preferred_element_type=f32
    ) + lax.dot_general(input_low, input_ref[...], right_t, preferred_element_type=f32)

    def conv_tile(n, carry):
        acc_bias, acc_taps, nexts = carry
        i = tiles - 1 - n
        at = pl.ds(pl.multiple_of(i * TILE, TILE), TILE)
        before = pl.ds(pl.multiple_of(jnp.maximum(i - 1, 0) * TILE, TILE), TILE)
        grad = conv_f_ref[at, :]
        masks = mask_ref[at, :]
        cur = inner_ref[0, at, :]
        prev = jnp.where(i == 0, edge_inner, inner_ref[0, before, :])
        total = grad * taps_ref[0:1, :]
        new_taps = [acc_taps[0] + grad * cur]
        new_nexts = []
        for k in range(1, taps_n):
            masked = grad * masks[:, k : k + 1]
            part = masked * taps_ref[k : k + 1, :]
            total = total + up(part, nexts[k - 1], k, row)
            new_taps.append(acc_taps[k] + masked * down(cur, prev, k, row))
            new_nexts.append(part)
        rate_f_ref[at, :] = total
        return acc_bias + grad, tuple(new_taps), tuple(new_nexts)

    acc_bias, acc_taps, nexts = lax.fori_loop(
        0,
        tiles,
        conv_tile,
        (
            acc_ref[3],
            tuple(acc_ref[4 + k] for k in range(taps_n)),
            tuple(next_ref[k] for k in range(taps_n - 1)),
        ),
    )
    acc_ref[3] = acc_bias
    for k in range(taps_n):
        acc_ref[4 + k] = acc_taps[k]
    for k in range(taps_n - 1):
        next_ref[k] = nexts[k]
    inner_grad_ref[0] = rate_f_ref[...].astype(bf16)

    @pl.when(step == 0)
    def _():
        tail_ref[...] = rate_f_ref[length - TILE :, :]

    @pl.when(is_first_block)
    def _():
        zero = jnp.zeros((TILE, width), f32)
        total = zero
        for k in range(1, taps_n):
            total = total + up(zero, nexts[k - 1], k, row)
        rim_grad_ref[...] = total
        sums_ref[...] = jnp.sum(acc_ref[...], axis=1)


def norm_project(blocks, place, gain, weight_t):
    count = len(blocks)
    length, model = blocks[0].shape
    width = weight_t.shape[0]

    def kernel(place_ref, *refs):
        ins, gain_ref, weight_ref, normed_ref, out_ref = refs[:count], *refs[count:]
        j = pl.program_id(0)
        for r in range(count):

            @pl.when((j ^ place_ref[0]) == r)
            def _(source=ins[r]):
                x = source[...].astype(f32)
                root = lax.rsqrt(jnp.mean(x * x, axis=-1, keepdims=True) + epsilon)
                normed_ref[...] = (x * root * gain_ref[...]).astype(bf16)

        out_ref[0] = lax.dot_general(
            normed_ref[...], weight_ref[...], (((1,), (1,)), ((), ())), preferred_element_type=f32
        )

    whole = lambda *shape: pl.BlockSpec(shape, lambda j, p: (0,) * len(shape))
    return pl.pallas_call(
        kernel,
        grid_spec=pltpu.PrefetchScalarGridSpec(
            num_scalar_prefetch=1,
            grid=(count,),
            in_specs=[whole(length, model)] * count + [whole(1, model), whole(width, model)],
            out_specs=[
                pl.BlockSpec((length, model), lambda j, p: (j, 0)),
                pl.BlockSpec((1, length, width), lambda j, p: (j, 0, 0)),
            ],
        ),
        out_shape=[
            jax.ShapeDtypeStruct((count * length, model), bf16),
            jax.ShapeDtypeStruct((count, length, width), f32),
        ],
        compiler_params=pltpu.CompilerParams(vmem_limit_bytes=VMEM_LIMIT),
        name="norm_project",
    )(place, *blocks, gain, weight_t)


def recur_forward(inner, masks, rim, taps, vecs, rate_dense, input_dense):
    blocks, length, width = inner.shape
    whole = lambda *shape: pl.BlockSpec(shape, lambda j: (0,) * len(shape))
    block = pl.BlockSpec((1, length, width), lambda j: (j, 0, 0))
    full = jax.ShapeDtypeStruct((blocks, length, width), f32)
    return pl.pallas_call(
        forward_kernel,
        grid_spec=pltpu.PrefetchScalarGridSpec(
            num_scalar_prefetch=0,
            grid=(blocks,),
            in_specs=[
                block,
                pl.BlockSpec((length, masks.shape[1]), lambda j: (j, 0)),
                whole(*rim.shape),
                whole(*taps.shape),
                whole(*vecs.shape),
                whole(*rate_dense.shape),
                whole(*input_dense.shape),
            ],
            out_specs=[block, block, block, block, block, block, whole(2, TILE, width)],
            scratch_shapes=[
                pltpu.VMEM((TILE, width), f32),
                pltpu.VMEM((2, TILE, width), f32),
                pltpu.VMEM((length, width), f32),
                pltpu.VMEM((length, width), f32),
            ],
        ),
        out_shape=[
            full,
            jax.ShapeDtypeStruct((blocks, length, width), bf16),
            full,
            full,
            full,
            full,
            jax.ShapeDtypeStruct((2, TILE, width), f32),
        ],
        compiler_params=pltpu.CompilerParams(vmem_limit_bytes=VMEM_LIMIT),
        name="recur_forward",
    )(inner, masks, rim, taps, vecs, rate_dense, input_dense)


def recur_backward(
    direct, state, conv, sig_rate, sig_input, inner, masks, rim, state_in, after, taps, vecs, rate_dense, input_dense
):
    blocks, length, width = inner.shape
    last = length // TILE - 1
    whole = lambda *shape: pl.BlockSpec(shape, lambda j: (0,) * len(shape))
    block = pl.BlockSpec((1, length, width), lambda j: (blocks - 1 - j, 0, 0))
    edge = pl.BlockSpec(
        (1, TILE, width), lambda j: (jnp.maximum(blocks - 2 - j, 0), last, 0)
    )
    low = jax.ShapeDtypeStruct((blocks, length, width), bf16)
    tile = jax.ShapeDtypeStruct((TILE, width), f32)
    count = 4 + taps.shape[0]
    return pl.pallas_call(
        backward_kernel,
        grid_spec=pltpu.PrefetchScalarGridSpec(
            num_scalar_prefetch=0,
            grid=(blocks,),
            in_specs=[
                block,
                block,
                edge,
                block,
                block,
                block,
                block,
                edge,
                pl.BlockSpec((length, masks.shape[1]), lambda j: (blocks - 1 - j, 0)),
                whole(*rim.shape),
                whole(*state_in.shape),
                whole(*after.shape),
                whole(*taps.shape),
                whole(*vecs.shape),
                whole(*rate_dense.shape),
                whole(*input_dense.shape),
            ],
            out_specs=[
                block,
                block,
                block,
                whole(TILE, width),
                whole(TILE, width),
                whole(count, width),
            ],
            scratch_shapes=[
                pltpu.VMEM((TILE, width), f32),
                pltpu.VMEM((taps.shape[0] - 1, TILE, width), f32),
                pltpu.VMEM((count, TILE, width), f32),
                pltpu.VMEM((length, width), f32),
                pltpu.VMEM((length, width), f32),
                pltpu.VMEM((length, width), f32),
            ],
        ),
        out_shape=[low, low, low, tile, tile, jax.ShapeDtypeStruct((count, width), f32)],
        compiler_params=pltpu.CompilerParams(vmem_limit_bytes=VMEM_LIMIT),
        cost_estimate=pl.CostEstimate(flops=1000, bytes_accessed=1000, transcendentals=0),
        name="recur_backward",
    )(
        direct,
        state,
        state,
        conv,
        sig_rate,
        sig_input,
        inner,
        inner,
        masks,
        rim,
        state_in,
        after,
        taps,
        vecs,
        rate_dense,
        input_dense,
    )


def dense_blocks(blocks):
    count, rows_in, cols_out = blocks.shape
    tall = blocks.reshape(count * rows_in, cols_out)
    wide = jnp.concatenate([tall] * count, axis=1)
    row = lax.broadcasted_iota(jnp.int32, wide.shape, 0) // rows_in
    col = lax.broadcasted_iota(jnp.int32, wide.shape, 1) // cols_out
    return jnp.where(row == col, wide, jnp.zeros_like(wide))


def diagonal_blocks(full, count):
    rows, cols = full.shape[0] // count, full.shape[1] // count
    return jnp.stack([full[i * rows : (i + 1) * rows, i * cols : (i + 1) * cols] for i in range(count)])


def rms(values):
    return lax.rsqrt(jnp.mean(values * values, axis=-1, keepdims=True) + epsilon)


def norm_back(grad, xhat, scale, root):
    e = grad * scale
    return root * (e - xhat * jnp.mean(e * xhat, axis=-1, keepdims=True)), jnp.sum(grad * xhat, axis=0)


def shards(
    tokens,
    mixer_gain,
    in_proj,
    branch_proj,
    conv_taps,
    conv_bias,
    rate_blocks,
    rate_bias,
    input_blocks,
    input_bias,
    decay_param,
    out_proj,
    dense_gain,
    gate_proj,
    up_proj,
    down_proj,
    segment_ids,
    cotangent,
):
    tp_place = lax.axis_index("tp")
    seq_place = lax.axis_index("seq")
    seq_size = lax.axis_size("seq")
    core = seq_place % 2
    tp_size = lax.axis_size("tp")
    gain_share = mixer_gain.shape[0]
    taps_n, width = conv_taps.shape
    rim_width = taps_n - 1
    length, model = tokens.shape
    group = length * tp_size
    blocks_n = rate_blocks.shape[0]

    in_t, branch_t = in_proj.T, branch_proj.T
    place = tp_place.astype(jnp.int32)[None]

    blocks = [tokens] + [swap(tokens, "tp", r) for r in range(1, tp_size)]
    blocks[1], gains, ids, rate_in, input_in, vec_in = tied(
        blocks[1],
        jnp.stack([mixer_gain, dense_gain]),
        segment_ids,
        rate_blocks,
        input_blocks,
        (conv_bias, rate_bias, input_bias, decay_param),
    )
    gains = gather_rows(gains)
    gains = gains.transpose(1, 0, 2).reshape(2, -1).astype(f32)
    mixer_scale, dense_scale = gains[0], gains[1]
    rim_ids = from_neighbour(ids[-rim_width:], -1)
    ext_ids = jnp.concatenate([rim_ids, ids])
    same = [ext_ids[rim_width - k : rim_width - k + group] == ids for k in range(1, taps_n)]
    masks = jnp.stack([same[0]] + same, axis=1).astype(f32)
    rate_dense = dense_blocks(rate_in)
    input_dense = dense_blocks(input_in)
    vecs = jnp.stack([*vec_in[:3], -8.0 * jax.nn.softplus(-vec_in[3])])
    *blocks, masks, rate_dense, input_dense, vecs = tied(*blocks, masks, rate_dense, input_dense, vecs)
    cot_all = lax.all_gather(cotangent, ("seq", "tp"), axis=0, tiled=True)

    normed, inner = norm_project(blocks, place, mixer_scale[None], in_t)
    rim = from_neighbour(inner[-1, -TILE:], -1)
    conv, conv_low, sig_rate, sig_input, keep_prefix, value_prefix, ends = recur_forward(
        inner, masks, rim, conv_taps, vecs, rate_dense, input_dense
    )
    ends, normed_b = tied(ends, normed)
    state_in = carry_in(ends[0, 0], ends[1, 0], False)
    branch_pre = project_t(normed_b, branch_t).reshape(inner.shape)
    state, mixed, mixer_part = mix_out(value_prefix, keep_prefix, branch_pre, state_in[None], out_proj)
    mixed = mixed.reshape(group, width)
    mixer_out = scatter_rows(mixer_part)
    mid = tokens.astype(f32) + mixer_out
    mid_root = rms(mid)
    xhat_dense = mid * mid_root
    normed_two = (xhat_dense * dense_scale).astype(bf16)

    chips = seq_size // 2
    same_core = [[core_no + 2 * i for i in range(chips)] for core_no in range(2)]
    rows_z = lax.all_gather(normed_two, "seq", axis=0, tiled=True, axis_index_groups=same_core)
    rows_two, cot_all = tied(gather_rows(normed_two).reshape(group, model), cot_all)
    hidden, normed_two_part = dense_rows(
        rows_two, cot_all, seq_place.astype(jnp.int32)[None], gate_proj, up_proj, down_proj
    )
    normed_two_grad = scatter_rows(normed_two_part.reshape(tp_size, length, model))
    dense_part = product(hidden, down_proj).astype(bf16)
    normed_two_grad, dense_part = tied(normed_two_grad, dense_part)
    mid_from_norm, dense_gain_part = norm_back(normed_two_grad, xhat_dense, dense_scale, mid_root)
    mid_grad = cotangent.astype(f32) + mid_from_norm
    mid_blocks = gather_rows(mid_grad.astype(bf16))
    mid_blocks, dense_part, rows_z = tied(mid_blocks, dense_part, rows_z)
    rows_spread = spread(rows_z)

    direct, branch_pre_grad, reach = mix_back(mid_blocks, out_proj, branch_pre, state, keep_prefix)
    branch_pre_grad = branch_pre_grad.reshape(group, width)
    mid_rows = mid_blocks.reshape(group, model)
    reach, direct, branch_pre_grad, mid_rows = tied(reach[0], direct, branch_pre_grad, mid_rows)
    after = carry_in(ends[0, 0], reach, True)
    out_full = product_left_t(mixed, mid_rows).astype(bf16)
    branch_full = product_left_t(branch_pre_grad, normed).astype(bf16)
    after, out_full, branch_full = tied(after, out_full, branch_full)
    out_sum, branch_sum = lax.psum((out_full, branch_full), "seq")
    tile = lambda v: jnp.broadcast_to(v, (TILE, width))
    rate_low, input_low, inner_grad, tail, rim_grad, sums = recur_backward(
        direct,
        state,
        conv,
        sig_rate,
        sig_input,
        inner,
        masks,
        rim,
        tile(state_in),
        tile(after),
        conv_taps,
        vecs,
        rate_dense,
        input_dense,
    )
    rows_mine, rim_grad = rows_spread(rim_grad)
    fixed = tail + from_neighbour(rim_grad, 1)
    low_rows = conv_low.reshape(group, width)
    rate_w = diagonal_blocks(product_left_t(low_rows, rate_low.reshape(group, width)), blocks_n)
    input_w = diagonal_blocks(product_left_t(low_rows, input_low.reshape(group, width)), blocks_n)
    inner_grad = lax.dynamic_update_slice(
        inner_grad, fixed.astype(bf16)[None], (tp_size - 1, length - TILE, 0)
    ).reshape(group, width)
    in_full = product_left_t(inner_grad, normed).astype(bf16)
    block_full = jnp.concatenate([rate_w, input_w]).astype(bf16)
    normed_part = (product(inner_grad, in_t) + product(branch_pre_grad, branch_t)).astype(bf16)
    rows_theirs = swap(rows_mine, "seq", 1)
    normed_part, in_full, block_full, sums = tied(normed_part, in_full, block_full, sums)
    in_sum, block_sum = lax.psum((in_full, block_full), "seq", axis_index_groups=[list(range(seq_size))[::-1]])
    normed_grad = scatter_rows(normed_part.reshape(tp_size, length, model))
    sums = sum_bits(sums, "seq")
    own = tokens.astype(f32)
    own_root = rms(own)
    rows_grad, mixer_gain_part = norm_back(normed_grad, own * own_root, mixer_scale, own_root)
    tokens_grad = mid_grad + rows_grad
    gain_parts = sum_bits(jnp.stack([mixer_gain_part, dense_gain_part]), "tp")
    gain_own = lax.dynamic_slice_in_dim(gain_parts, tp_place * gain_share, gain_share, 1)
    gain_sum = sum_bits(gain_own, "seq")
    decay_sum = 8.0 * jax.nn.sigmoid(-decay_param) * sums[2]
    rows_mine, rows_theirs, tokens_grad, gain_sum, sums, dense_part = tied(
        rows_mine, rows_theirs, tokens_grad, gain_sum, sums, dense_part
    )
    dense_out = scatter_rows(dense_part.reshape(tp_size, length, model))

    places = jnp.stack([core, tp_place]).astype(jnp.int32)
    blocked = lambda rows: rows.reshape(tp_size, chips, length, model)
    hidden_n = gate_proj.shape[1]
    weights = (cot_all, gate_proj, up_proj, down_proj, places)
    big = dense_weight_grads(blocked(rows_mine), blocked(rows_theirs), *weights, hidden_n // 3, 0)
    *big, out_sum, branch_sum, rows_mine, rows_theirs = tied(*big, out_sum, branch_sum, rows_mine, rows_theirs)
    big = [(part, swap(part, "seq", 1)) for part in big]
    small = dense_weight_grads(blocked(rows_mine), blocked(rows_theirs), *weights, hidden_n // 6, 4)
    *small, in_sum, block_sum = tied(*small, in_sum, block_sum)
    small = [(part, swap(part, "seq", 1)) for part in small]
    gate_sum = joined(big[0], small[0], places, 1)
    up_sum = joined(big[1], small[1], places, 1)
    down_sum = joined(big[2], small[2], places, 0)
    output = (mid + dense_out).astype(bf16)
    rate_sum, input_sum = block_sum[:blocks_n].astype(f32), block_sum[blocks_n:].astype(f32)
    return (
        output,
        tokens_grad,
        gain_sum[0],
        in_sum.astype(f32).T,
        branch_sum.astype(f32).T,
        sums[4 : 4 + taps_n],
        sums[3],
        rate_sum,
        sums[0],
        input_sum,
        sums[1],
        decay_sum,
        out_sum.astype(f32),
        gain_sum[1],
        gate_sum,
        up_sum,
        down_sum,
    )


def solution(mesh):
    return jax.shard_map(
        shards,
        mesh=mesh,
        in_specs=(
            P(("seq", "tp"), None),
            P("tp"),
            P(None, "tp"),
            P(None, "tp"),
            P(None, "tp"),
            P("tp"),
            P("tp", None, None),
            P("tp"),
            P("tp", None, None),
            P("tp"),
            P("tp"),
            P("tp", None),
            P("tp"),
            P(None, "tp"),
            P(None, "tp"),
            P("tp", None),
            P("seq"),
            P(("seq", "tp"), None),
        ),
        out_specs=(
            P(("seq", "tp"), None),
            P(("seq", "tp"), None),
            P("tp"),
            P(None, "tp"),
            P(None, "tp"),
            P(None, "tp"),
            P("tp"),
            P("tp", None, None),
            P("tp"),
            P("tp", None, None),
            P("tp"),
            P("tp"),
            P("tp", None),
            P("tp"),
            P(None, "tp"),
            P(None, "tp"),
            P("tp", None),
        ),
        check_vma=False,
    )
```

```python
import math

import jax
import jax.numpy as jnp
from jax import lax
from jax.experimental import pallas as pl
from jax.experimental.pallas import tpu as pltpu
from jax.sharding import PartitionSpec as P

epsilon = 1e-06
f32 = jnp.float32
bf16 = jnp.bfloat16
TILE = 8
VMEM_LIMIT = 50 * 1024 * 1024


def product(left, right):
    return jnp.dot(left, right, preferred_element_type=f32)


def product_left_t(left, right):
    return lax.dot_general(left, right, (((0,), (0,)), ((), ())), preferred_element_type=f32)


def product_right_t(left, right):
    return lax.dot_general(left, right, (((1,), (1,)), ((), ())), preferred_element_type=f32)


def gelu_tanh(values):
    return jax.nn.gelu(values, approximate=True)


def tied(*values):
    return lax.optimization_barrier(values)


def swap(value, axis, bit):
    count = lax.axis_size(axis)
    return lax.ppermute(value, axis, [(i, i ^ bit) for i in range(count)])


def gather_rows(rows):
    count = lax.axis_size("tp")
    place = lax.axis_index("tp")
    whole = jnp.zeros((count,) + rows.shape, rows.dtype)
    for r in range(count):
        block = rows if r == 0 else swap(rows, "tp", r)
        whole = lax.dynamic_update_index_in_dim(whole, block, place ^ r, 0)
    return whole


def spread(rows):
    count = lax.axis_size("tp")
    if count != 4:
        whole = jnp.stack([rows] + [swap(rows, "tp", r) for r in range(1, count)])
        return lambda *after: tied(whole, *after)
    half = rows.shape[0] // 2
    sides = swap(rows, "tp", 1), swap(rows, "tp", 2)

    def finish(*after):
        one, two, *after = tied(*sides, *after)
        far = jnp.concatenate([swap(two[:half], "tp", 1), swap(one[half:], "tp", 2)])
        return (jnp.stack([rows, one, two, far]), *after)

    return finish


def scatter_rows(blocks):
    place = lax.axis_index("tp")
    block = lambda r: lax.dynamic_index_in_dim(blocks, place ^ r, 0, False)
    total = block(0).astype(f32)
    for r in range(1, lax.axis_size("tp")):
        total = total + swap(block(r), "tp", r).astype(f32)
    return total


def carry_in(keep_total, value_total, backward):
    place = lax.axis_index("seq")
    total = jnp.stack([keep_total, value_total])
    before = jnp.stack([jnp.ones_like(keep_total), jnp.zeros_like(value_total)])
    bit = 1
    while bit < lax.axis_size("seq"):
        other = swap(total, "seq", bit)
        upper = (place & bit) != 0
        earlier = jnp.logical_not(upper) if backward else upper
        joined_before = jnp.stack([other[0] * before[0], before[0] * other[1] + before[1]])
        before = jnp.where(earlier, joined_before, before)
        first = jnp.where(earlier, other, total)
        second = jnp.where(earlier, total, other)
        total = jnp.stack([first[0] * second[0], second[0] * first[1] + second[1]])
        bit *= 2
    return before[1]


def from_neighbour(value, step):
    count = lax.axis_size("seq")
    place = lax.axis_index("seq")
    inside = lax.ppermute(value, "seq", [(i, i ^ 1) for i in range(count)])
    pairs = [(i, i + 1) for i in range(1, count - 1, 2)] + [(i + 1, i) for i in range(1, count - 1, 2)]
    across = lax.ppermute(value, "seq", pairs)
    return jnp.where((place % 2 == 0) == (step == 1), inside, across)


def sum_bits(value, axis):
    bit = 1
    while bit < lax.axis_size(axis):
        value = value + swap(value, axis, bit)
        bit *= 2
    return value


def both_halves(mine, theirs, core):
    first = jnp.where(core == 0, mine, theirs)
    second = jnp.where(core == 0, theirs, mine)
    return first, second


def gelu_grads(gate_pre, up_pre, hidden_grad):
    square = gate_pre * gate_pre
    inner = math.sqrt(2.0 / math.pi) * gate_pre * (1.0 + 0.044715 * square)
    half = 0.5 * (1.0 + jnp.tanh(inner))
    act = gate_pre * half
    slope = half + 2.0 * math.sqrt(2.0 / math.pi) * act * (1.0 - half) * (1.0 + 3.0 * 0.044715 * square)
    return act * up_pre, hidden_grad * up_pre * slope, hidden_grad * act


def dense_weight_grads(mine, theirs, cot_all, gate_proj, up_proj, down_proj, places):
    tp_size, chips, block, model = mine.shape
    half = gate_proj.shape[1] // 2
    cot_all = cot_all.reshape(chips, 2, tp_size, block, model)
    part = math.gcd(chips, 4)
    length = part * block
    per_core = tp_size * chips // part
    steps, outs = 2 * per_core, 4
    tile = math.gcd(half, 256)
    left_t = (((0,), (0,)), ((), ()))
    right_t = (((1,), (1,)), ((), ()))

    def kernel(core_ref, mine_ref, theirs_ref, cot_ref, gate_ref, up_ref, down_ref, *rest):
        gate_out, up_out, down_out, acc_g, acc_u, acc_d, hid, gg, ug, x_ref = rest
        i = pl.program_id(0)

        @pl.when(i < per_core)
        def _():
            x_ref[...] = mine_ref[...].reshape(length, model)

        @pl.when(jnp.logical_and(i >= per_core, i < steps))
        def _():
            x_ref[...] = theirs_ref[...].reshape(length, model)

        @pl.when(i == 0)
        def _():
            acc_g[...] = jnp.zeros_like(acc_g)
            acc_u[...] = jnp.zeros_like(acc_u)
            acc_d[...] = jnp.zeros_like(acc_d)

        @pl.when(i < steps)
        def _():
            cots = cot_ref[...].reshape(length, model)
            for n in range(half // tile):
                cols = slice(n * tile, (n + 1) * tile)
                gate_pre = jnp.dot(x_ref[...], gate_ref[:, cols], preferred_element_type=f32)
                up_pre = jnp.dot(x_ref[...], up_ref[:, cols], preferred_element_type=f32)
                hidden_grad = lax.dot_general(cots, down_ref[cols, :], right_t, preferred_element_type=f32)
                a, b, c = gelu_grads(gate_pre, up_pre, hidden_grad)
                hid[:, cols] = a.astype(bf16)
                gg[:, cols] = b.astype(bf16)
                ug[:, cols] = c.astype(bf16)
            acc_g[...] += lax.dot_general(x_ref[...], gg[...], left_t, preferred_element_type=f32)
            acc_u[...] += lax.dot_general(x_ref[...], ug[...], left_t, preferred_element_type=f32)
            acc_d[...] += lax.dot_general(hid[...], cots, left_t, preferred_element_type=f32)

        @pl.when(i >= steps)
        def _():
            wide = pl.ds(pl.multiple_of((i - steps) * (model // outs), model // outs), model // outs)
            low = pl.ds(pl.multiple_of((i - steps) * (half // outs), half // outs), half // outs)
            gate_out[...] = acc_g[wide, :].astype(bf16)
            up_out[...] = acc_u[wide, :].astype(bf16)
            down_out[...] = acc_d[low, :].astype(bf16)

    once = pl.Buffered(1)
    groups = chips // part
    out_index = lambda i, c: (jnp.maximum(i - steps, 0), 0)

    def cot_index(i, c):
        i = jnp.minimum(i, steps - 1)
        n = i % per_core
        return n % groups, c[0] ^ (i // per_core), c[1] ^ (n // groups), 0, 0

    def rows_index(first):
        def index(i, c):
            n = jnp.clip(i - first, 0, per_core - 1)
            return n // groups, n % groups, 0, 0

        return pl.BlockSpec((1, part, block, model), index)

    return pl.pallas_call(
        kernel,
        grid_spec=pltpu.PrefetchScalarGridSpec(
            num_scalar_prefetch=1,
            grid=(steps + outs,),
            in_specs=[
                rows_index(0),
                rows_index(per_core),
                pl.BlockSpec((part, 1, 1, block, model), cot_index),
                pl.BlockSpec((model, half), lambda i, c: (0, c[0]), pipeline_mode=once),
                pl.BlockSpec((model, half), lambda i, c: (0, c[0]), pipeline_mode=once),
                pl.BlockSpec((half, model), lambda i, c: (c[0], 0), pipeline_mode=once),
            ],
            out_specs=[
                pl.BlockSpec((model // outs, half), out_index),
                pl.BlockSpec((model // outs, half), out_index),
                pl.BlockSpec((half // outs, model), out_index),
            ],
            scratch_shapes=[
                pltpu.VMEM((model, half), f32),
                pltpu.VMEM((model, half), f32),
                pltpu.VMEM((half, model), f32),
                pltpu.VMEM((length, half), bf16),
                pltpu.VMEM((length, half), bf16),
                pltpu.VMEM((length, half), bf16),
                pltpu.VMEM((length, model), bf16),
            ],
        ),
        out_shape=[
            jax.ShapeDtypeStruct((model, half), bf16),
            jax.ShapeDtypeStruct((model, half), bf16),
            jax.ShapeDtypeStruct((half, model), bf16),
        ],
        compiler_params=pltpu.CompilerParams(vmem_limit_bytes=60 * 1024 * 1024),
        cost_estimate=pl.CostEstimate(flops=1000, bytes_accessed=1000, transcendentals=0),
        name="dense_weight_grads",
    )(places, mine, theirs, cot_all, gate_proj, up_proj, down_proj)


def joined(mine, theirs, core, axis):
    rows, cols = mine.shape
    block = math.gcd(rows, 256)
    steps = rows // block

    def kernel(core_ref, mine_ref, theirs_ref, out_ref):
        for low in range(2):

            @pl.when(core_ref[0] == low)
            def _(low=low):
                pair = (mine_ref, theirs_ref) if low == 0 else (theirs_ref, mine_ref)
                if axis == 1:
                    out_ref[:, :cols] = pair[0][...].astype(f32)
                    out_ref[:, cols:] = pair[1][...].astype(f32)
                else:
                    out_ref[0] = pair[0][...].astype(f32)
                    out_ref[1] = pair[1][...].astype(f32)

    half = pl.BlockSpec((block, cols), lambda i, c: (i, 0))
    if axis == 1:
        out_spec = pl.BlockSpec((block, 2 * cols), lambda i, c: (i, 0))
        out_shape = jax.ShapeDtypeStruct((rows, 2 * cols), f32)
    else:
        out_spec = pl.BlockSpec((2, block, cols), lambda i, c: (0, i, 0))
        out_shape = jax.ShapeDtypeStruct((2, rows, cols), f32)
    out = pl.pallas_call(
        kernel,
        grid_spec=pltpu.PrefetchScalarGridSpec(
            num_scalar_prefetch=1, grid=(steps,), in_specs=[half, half], out_specs=out_spec
        ),
        out_shape=out_shape,
        compiler_params=pltpu.CompilerParams(vmem_limit_bytes=VMEM_LIMIT),
        cost_estimate=pl.CostEstimate(flops=1000, bytes_accessed=1000, transcendentals=0),
        name="joined",
    )(core, mine, theirs)
    return out if axis == 1 else out.reshape(2 * rows, cols)


def dense_rows(rows, cot_all, group_place, gate_proj, up_proj, down_proj):
    length, model = rows.shape
    width = gate_proj.shape[1]
    tile = math.gcd(width, 256)
    out_tile = math.gcd(model, 256)
    first, second = width // tile, model // out_tile
    right_t = (((1,), (1,)), ((), ()))

    def kernel(place_ref, x_ref, c_ref, gate_ref, up_ref, down_ref, hidden_ref, grad_ref, gates, ups, gate_grads, up_grads):
        j = pl.program_id(0)

        @pl.when(j < first)
        def _():
            gate_pre = jnp.dot(x_ref[...], gate_ref[...], preferred_element_type=f32)
            up_pre = jnp.dot(x_ref[...], up_ref[...], preferred_element_type=f32)
            hidden_grad = lax.dot_general(c_ref[...], down_ref[...], right_t, preferred_element_type=f32)
            hidden, gate_grad, up_grad = gelu_grads(gate_pre, up_pre, hidden_grad)
            hidden_ref[...] = hidden.astype(bf16)
            at = pl.ds(pl.multiple_of(j * tile, tile), tile)
            gates[:, at] = gate_ref[...]
            ups[:, at] = up_ref[...]
            gate_grads[:, at] = gate_grad.astype(bf16)
            up_grads[:, at] = up_grad.astype(bf16)

        @pl.when(j >= first)
        def _():
            at = pl.ds(pl.multiple_of((j - first) * out_tile, out_tile), out_tile)
            part = lax.dot_general(gate_grads[...], gates[at, :], right_t, preferred_element_type=f32)
            part = part + lax.dot_general(up_grads[...], ups[at, :], right_t, preferred_element_type=f32)
            grad_ref[...] = part.astype(bf16)

    clamp = lambda j: jnp.minimum(j, first - 1)
    wide = pl.BlockSpec((model, tile), lambda j, p: (0, clamp(j)))
    return pl.pallas_call(
        kernel,
        grid_spec=pltpu.PrefetchScalarGridSpec(
            num_scalar_prefetch=1,
            grid=(first + second,),
            in_specs=[
                pl.BlockSpec((length, model), lambda j, p: (0, 0)),
                pl.BlockSpec((length, model), lambda j, p: (p[0], 0)),
                wide,
                wide,
                pl.BlockSpec((tile, model), lambda j, p: (clamp(j), 0)),
            ],
            out_specs=[
                pl.BlockSpec((length, tile), lambda j, p: (0, clamp(j))),
                pl.BlockSpec((length, out_tile), lambda j, p: (0, jnp.maximum(j - first, 0))),
            ],
            scratch_shapes=[
                pltpu.VMEM((model, width), bf16),
                pltpu.VMEM((model, width), bf16),
                pltpu.VMEM((length, width), bf16),
                pltpu.VMEM((length, width), bf16),
            ],
        ),
        out_shape=[
            jax.ShapeDtypeStruct((length, width), bf16),
            jax.ShapeDtypeStruct((length, model), bf16),
        ],
        compiler_params=pltpu.CompilerParams(vmem_limit_bytes=VMEM_LIMIT),
        name="dense_rows",
    )(group_place, rows, cot_all, gate_proj, up_proj, down_proj)


def project_t(rows, weight_t):
    total, model = rows.shape
    width = weight_t.shape[0]
    length = math.gcd(total, 256)

    def kernel(rows_ref, weight_ref, out_ref):
        out_ref[...] = lax.dot_general(
            rows_ref[...], weight_ref[...], (((1,), (1,)), ((), ())), preferred_element_type=f32
        )

    return pl.pallas_call(
        kernel,
        grid=(total // length,),
        in_specs=[
            pl.BlockSpec((length, model), lambda j: (j, 0)),
            pl.BlockSpec((width, model), lambda j: (0, 0)),
        ],
        out_specs=pl.BlockSpec((length, width), lambda j: (j, 0)),
        out_shape=jax.ShapeDtypeStruct((total, width), f32),
        compiler_params=pltpu.CompilerParams(vmem_limit_bytes=VMEM_LIMIT),
        name="project_t",
    )(rows, weight_t)


def mix_out(value_prefix, keep_prefix, branch_pre, state_in, out_proj):
    blocks, length, width = value_prefix.shape
    model = out_proj.shape[1]

    def kernel(value_ref, keep_ref, branch_ref, in_ref, out_ref, state_ref, mixed_ref, part_ref):
        state = value_ref[0] + keep_ref[0] * in_ref[...]
        state_ref[0] = state
        mixed = (state * gelu_tanh(branch_ref[0])).astype(bf16)
        mixed_ref[0] = mixed
        part_ref[0] = jnp.dot(mixed, out_ref[...], preferred_element_type=f32).astype(bf16)

    block = pl.BlockSpec((1, length, width), lambda j: (j, 0, 0))
    whole = lambda *shape: pl.BlockSpec(shape, lambda j: (0,) * len(shape))
    return pl.pallas_call(
        kernel,
        grid=(blocks,),
        in_specs=[block, block, block, whole(1, width), whole(width, model)],
        out_specs=[block, block, pl.BlockSpec((1, length, model), lambda j: (j, 0, 0))],
        out_shape=[
            jax.ShapeDtypeStruct((blocks, length, width), f32),
            jax.ShapeDtypeStruct((blocks, length, width), bf16),
            jax.ShapeDtypeStruct((blocks, length, model), bf16),
        ],
        compiler_params=pltpu.CompilerParams(vmem_limit_bytes=VMEM_LIMIT),
        name="mix_out",
    )(value_prefix, keep_prefix, branch_pre, state_in, out_proj)


def mix_back(mid_rows, out_proj, branch_pre, state, keep_prefix):
    blocks, length, width = state.shape
    model = out_proj.shape[1]
    tiles = length // 16

    def kernel(mid_ref, out_ref, branch_ref, state_ref, keep_ref, direct_ref, branch_grad_ref, reach_ref, mixed, acc):
        j = pl.program_id(0)
        mixed[...] = lax.dot_general(
            mid_ref[0], out_ref[...], (((1,), (1,)), ((), ())), preferred_element_type=f32
        )

        @pl.when(j == 0)
        def _():
            acc[...] = jnp.zeros_like(acc)

        def tile(i, total):
            at = pl.ds(pl.multiple_of(i * 16, 16), 16)
            grad = mixed[at, :]
            pre = branch_ref[0, at, :]
            square = pre * pre
            inner = math.sqrt(2.0 / math.pi) * pre * (1.0 + 0.044715 * square)
            half = 0.5 * (1.0 + jnp.tanh(inner))
            act = pre * half
            slope = half + 2.0 * math.sqrt(2.0 / math.pi) * act * (1.0 - half) * (1.0 + 3.0 * 0.044715 * square)
            direct = grad * act
            direct_ref[0, at, :] = direct
            branch_grad_ref[0, at, :] = (grad * state_ref[0, at, :] * slope).astype(bf16)
            return total + direct * keep_ref[0, at, :]

        acc[...] = lax.fori_loop(0, tiles, tile, acc[...])

        @pl.when(j == blocks - 1)
        def _():
            reach_ref[...] = jnp.sum(acc[...], axis=0, keepdims=True)

    block = pl.BlockSpec((1, length, width), lambda j: (j, 0, 0))
    whole = lambda *shape: pl.BlockSpec(shape, lambda j: (0,) * len(shape))
    return pl.pallas_call(
        kernel,
        grid=(blocks,),
        in_specs=[pl.BlockSpec((1, length, model), lambda j: (j, 0, 0)), whole(width, model), block, block, block],
        out_specs=[block, block, whole(1, width)],
        out_shape=[
            jax.ShapeDtypeStruct((blocks, length, width), f32),
            jax.ShapeDtypeStruct((blocks, length, width), bf16),
            jax.ShapeDtypeStruct((1, width), f32),
        ],
        scratch_shapes=[pltpu.VMEM((length, width), f32), pltpu.VMEM((16, width), f32)],
        compiler_params=pltpu.CompilerParams(vmem_limit_bytes=VMEM_LIMIT),
        name="mix_back",
    )(mid_rows, out_proj, branch_pre, state, keep_prefix)


def minus_expm1(x):
    series = 1.0 / 40320.0
    for term in (1.0 / 5040.0, 1.0 / 720.0, 1.0 / 120.0, 1.0 / 24.0, 1.0 / 6.0, 0.5, 1.0):
        series = series * x + term
    return jnp.where(x > -0.35, -x * series, 1.0 - jnp.exp(x))


def rows_of(shape):
    return lax.broadcasted_iota(jnp.int32, shape, 0)


def down(cur, prev, by, row):
    return jnp.where(row >= by, pltpu.roll(cur, by, 0), pltpu.roll(prev, by, 0))


def up(cur, after, by, row):
    return jnp.where(row < TILE - by, pltpu.roll(cur, TILE - by, 0), pltpu.roll(after, TILE - by, 0))


def last_row(tile):
    return jnp.broadcast_to(tile[TILE - 1 :, :], tile.shape)


def first_row(tile):
    return jnp.broadcast_to(tile[:1, :], tile.shape)


def forward_kernel(
    inner_ref,
    mask_ref,
    rim_ref,
    taps_ref,
    vec_ref,
    rate_ref,
    input_ref,
    conv_ref,
    low_ref,
    sig_rate_ref,
    sig_input_ref,
    keep_ref,
    value_ref,
    end_ref,
    prev_ref,
    carry_ref,
    rate_raw_ref,
    input_raw_ref,
):
    step = pl.program_id(0)
    length, width = inner_ref.shape[1:]
    tiles = length // TILE
    taps_n = taps_ref.shape[0]

    @pl.when(step == 0)
    def _():
        prev_ref[...] = rim_ref[...]
        carry_ref[0] = jnp.ones((TILE, width), f32)
        carry_ref[1] = jnp.zeros((TILE, width), f32)

    row = rows_of((TILE, width))

    def conv_tile(i, prev):
        at = pl.ds(pl.multiple_of(i * TILE, TILE), TILE)
        cur = inner_ref[0, at, :]
        masks = mask_ref[at, :]
        total = vec_ref[0:1, :] + taps_ref[0:1, :] * cur
        for k in range(1, taps_n):
            total = total + taps_ref[k : k + 1, :] * (down(cur, prev, k, row) * masks[:, k : k + 1])
        conv_ref[0, at, :] = total
        return cur

    prev_ref[...] = lax.fori_loop(0, tiles, conv_tile, prev_ref[...])
    low = conv_ref[0].astype(bf16)
    low_ref[0] = low
    rate_raw_ref[...] = jnp.dot(low, rate_ref[...], preferred_element_type=f32)
    input_raw_ref[...] = jnp.dot(low, input_ref[...], preferred_element_type=f32)

    def gate_tile(i, carry):
        keep_in, value_in = carry
        at = pl.ds(pl.multiple_of(i * TILE, TILE), TILE)
        sig_rate = jax.nn.sigmoid(rate_raw_ref[at, :] + vec_ref[1:2, :])
        sig_input = jax.nn.sigmoid(input_raw_ref[at, :] + vec_ref[2:3, :])
        sig_rate_ref[0, at, :] = sig_rate
        sig_input_ref[0, at, :] = sig_input
        log_decay = sig_rate * vec_ref[3:4, :]
        a = jnp.exp(log_decay) * mask_ref[at, 0:1]
        b = jnp.sqrt(minus_expm1(2.0 * log_decay)) * sig_input * conv_ref[0, at, :]
        for d in (1, 2, 4):
            a_before = jnp.where(row >= d, pltpu.roll(a, d, 0), 1.0)
            b_before = jnp.where(row >= d, pltpu.roll(b, d, 0), 0.0)
            b = b + a * b_before
            a = a * a_before
        b = b + a * value_in
        a = a * keep_in
        keep_ref[0, at, :] = a
        value_ref[0, at, :] = b
        return last_row(a), last_row(b)

    keep_end, value_end = lax.fori_loop(0, tiles, gate_tile, (carry_ref[0], carry_ref[1]))
    carry_ref[0] = keep_end
    carry_ref[1] = value_end
    end_ref[0] = keep_end
    end_ref[1] = value_end


def backward_kernel(
    direct_ref,
    state_ref,
    state_prev_ref,
    conv_ref,
    sig_rate_ref,
    sig_input_ref,
    inner_ref,
    inner_prev_ref,
    mask_ref,
    rim_ref,
    state_in_ref,
    after_ref,
    taps_ref,
    vec_ref,
    rate_ref,
    input_ref,
    rate_grad_ref,
    input_grad_ref,
    inner_grad_ref,
    tail_ref,
    rim_grad_ref,
    sums_ref,
    carry_ref,
    next_ref,
    acc_ref,
    rate_f_ref,
    input_f_ref,
    conv_f_ref,
):
    step = pl.program_id(0)
    steps = pl.num_programs(0)
    length, width = direct_ref.shape[1:]
    tiles = length // TILE
    taps_n = taps_ref.shape[0]
    row = rows_of((TILE, width))
    is_first_block = step == steps - 1

    @pl.when(step == 0)
    def _():
        carry_ref[...] = after_ref[...]
        next_ref[...] = jnp.zeros_like(next_ref)
        acc_ref[...] = jnp.zeros_like(acc_ref)

    edge_state = jnp.where(is_first_block, state_in_ref[...], state_prev_ref[0])
    edge_inner = jnp.where(is_first_block, rim_ref[...], inner_prev_ref[0])
    neg_rate = vec_ref[3:4, :]

    def gate_tile(n, carry):
        after, acc_rate, acc_input, acc_decay = carry
        i = tiles - 1 - n
        at = pl.ds(pl.multiple_of(i * TILE, TILE), TILE)
        before = pl.ds(pl.multiple_of(jnp.maximum(i - 1, 0) * TILE, TILE), TILE)
        direct = direct_ref[0, at, :]
        sig_rate = sig_rate_ref[0, at, :]
        sig_input = sig_input_ref[0, at, :]
        conv = conv_ref[0, at, :]
        log_decay = sig_rate * neg_rate
        decay = jnp.exp(log_decay)
        keep = decay * mask_ref[at, 0:1]
        room = minus_expm1(2.0 * log_decay)
        root = jnp.sqrt(room)
        a = keep
        b = keep * direct
        for d in (1, 2, 4):
            a_after = jnp.where(row < TILE - d, pltpu.roll(a, TILE - d, 0), 1.0)
            b_after = jnp.where(row < TILE - d, pltpu.roll(b, TILE - d, 0), 0.0)
            b = b + a * b_after
            a = a * a_after
        reach = b + a * after
        grad = direct + up(reach, after, 1, row)
        prev_tile = jnp.where(i == 0, edge_state, state_ref[0, before, :])
        state_prev = down(state_ref[0, at, :], prev_tile, 1, row)
        grad_root = grad * root
        gated = grad_root * sig_input
        decay_grad = grad * (keep * state_prev - sig_input * conv * (decay * decay) / root)
        rate_grad = decay_grad * neg_rate * (sig_rate * (1.0 - sig_rate))
        input_grad = gated * conv * (1.0 - sig_input)
        rate_f_ref[at, :] = rate_grad
        input_f_ref[at, :] = input_grad
        conv_f_ref[at, :] = gated
        return (
            first_row(reach),
            acc_rate + rate_grad,
            acc_input + input_grad,
            acc_decay + decay_grad * sig_rate,
        )

    after, acc_rate, acc_input, acc_decay = lax.fori_loop(
        0, tiles, gate_tile, (carry_ref[...], acc_ref[0], acc_ref[1], acc_ref[2])
    )
    carry_ref[...] = after
    acc_ref[0] = acc_rate
    acc_ref[1] = acc_input
    acc_ref[2] = acc_decay
    rate_low = rate_f_ref[...].astype(bf16)
    input_low = input_f_ref[...].astype(bf16)
    rate_grad_ref[0] = rate_low
    input_grad_ref[0] = input_low
    right_t = (((1,), (1,)), ((), ()))
    conv_f_ref[...] += lax.dot_general(
        rate_low, rate_ref[...], right_t, preferred_element_type=f32
    ) + lax.dot_general(input_low, input_ref[...], right_t, preferred_element_type=f32)

    def conv_tile(n, carry):
        acc_bias, acc_taps, nexts = carry
        i = tiles - 1 - n
        at = pl.ds(pl.multiple_of(i * TILE, TILE), TILE)
        before = pl.ds(pl.multiple_of(jnp.maximum(i - 1, 0) * TILE, TILE), TILE)
        grad = conv_f_ref[at, :]
        masks = mask_ref[at, :]
        cur = inner_ref[0, at, :]
        prev = jnp.where(i == 0, edge_inner, inner_ref[0, before, :])
        total = grad * taps_ref[0:1, :]
        new_taps = [acc_taps[0] + grad * cur]
        new_nexts = []
        for k in range(1, taps_n):
            masked = grad * masks[:, k : k + 1]
            part = masked * taps_ref[k : k + 1, :]
            total = total + up(part, nexts[k - 1], k, row)
            new_taps.append(acc_taps[k] + masked * down(cur, prev, k, row))
            new_nexts.append(part)
        rate_f_ref[at, :] = total
        return acc_bias + grad, tuple(new_taps), tuple(new_nexts)

    acc_bias, acc_taps, nexts = lax.fori_loop(
        0,
        tiles,
        conv_tile,
        (
            acc_ref[3],
            tuple(acc_ref[4 + k] for k in range(taps_n)),
            tuple(next_ref[k] for k in range(taps_n - 1)),
        ),
    )
    acc_ref[3] = acc_bias
    for k in range(taps_n):
        acc_ref[4 + k] = acc_taps[k]
    for k in range(taps_n - 1):
        next_ref[k] = nexts[k]
    inner_grad_ref[0] = rate_f_ref[...].astype(bf16)

    @pl.when(step == 0)
    def _():
        tail_ref[...] = rate_f_ref[length - TILE :, :]

    @pl.when(is_first_block)
    def _():
        zero = jnp.zeros((TILE, width), f32)
        total = zero
        for k in range(1, taps_n):
            total = total + up(zero, nexts[k - 1], k, row)
        rim_grad_ref[...] = total
        sums_ref[...] = jnp.sum(acc_ref[...], axis=1)


def norm_project(blocks, place, gain, weight_t):
    count = len(blocks)
    length, model = blocks[0].shape
    width = weight_t.shape[0]

    def kernel(place_ref, *refs):
        ins, gain_ref, weight_ref, normed_ref, out_ref = refs[:count], *refs[count:]
        j = pl.program_id(0)
        for r in range(count):

            @pl.when((j ^ place_ref[0]) == r)
            def _(source=ins[r]):
                x = source[...].astype(f32)
                root = lax.rsqrt(jnp.mean(x * x, axis=-1, keepdims=True) + epsilon)
                normed_ref[...] = (x * root * gain_ref[...]).astype(bf16)

        out_ref[0] = lax.dot_general(
            normed_ref[...], weight_ref[...], (((1,), (1,)), ((), ())), preferred_element_type=f32
        )

    whole = lambda *shape: pl.BlockSpec(shape, lambda j, p: (0,) * len(shape))
    return pl.pallas_call(
        kernel,
        grid_spec=pltpu.PrefetchScalarGridSpec(
            num_scalar_prefetch=1,
            grid=(count,),
            in_specs=[whole(length, model)] * count + [whole(1, model), whole(width, model)],
            out_specs=[
                pl.BlockSpec((length, model), lambda j, p: (j, 0)),
                pl.BlockSpec((1, length, width), lambda j, p: (j, 0, 0)),
            ],
        ),
        out_shape=[
            jax.ShapeDtypeStruct((count * length, model), bf16),
            jax.ShapeDtypeStruct((count, length, width), f32),
        ],
        compiler_params=pltpu.CompilerParams(vmem_limit_bytes=VMEM_LIMIT),
        name="norm_project",
    )(place, *blocks, gain, weight_t)


def recur_forward(inner, masks, rim, taps, vecs, rate_dense, input_dense):
    blocks, length, width = inner.shape
    whole = lambda *shape: pl.BlockSpec(shape, lambda j: (0,) * len(shape))
    block = pl.BlockSpec((1, length, width), lambda j: (j, 0, 0))
    full = jax.ShapeDtypeStruct((blocks, length, width), f32)
    return pl.pallas_call(
        forward_kernel,
        grid_spec=pltpu.PrefetchScalarGridSpec(
            num_scalar_prefetch=0,
            grid=(blocks,),
            in_specs=[
                block,
                pl.BlockSpec((length, masks.shape[1]), lambda j: (j, 0)),
                whole(*rim.shape),
                whole(*taps.shape),
                whole(*vecs.shape),
                whole(*rate_dense.shape),
                whole(*input_dense.shape),
            ],
            out_specs=[block, block, block, block, block, block, whole(2, TILE, width)],
            scratch_shapes=[
                pltpu.VMEM((TILE, width), f32),
                pltpu.VMEM((2, TILE, width), f32),
                pltpu.VMEM((length, width), f32),
                pltpu.VMEM((length, width), f32),
            ],
        ),
        out_shape=[
            full,
            jax.ShapeDtypeStruct((blocks, length, width), bf16),
            full,
            full,
            full,
            full,
            jax.ShapeDtypeStruct((2, TILE, width), f32),
        ],
        compiler_params=pltpu.CompilerParams(vmem_limit_bytes=VMEM_LIMIT),
        name="recur_forward",
    )(inner, masks, rim, taps, vecs, rate_dense, input_dense)


def recur_backward(
    direct, state, conv, sig_rate, sig_input, inner, masks, rim, state_in, after, taps, vecs, rate_dense, input_dense
):
    blocks, length, width = inner.shape
    last = length // TILE - 1
    whole = lambda *shape: pl.BlockSpec(shape, lambda j: (0,) * len(shape))
    block = pl.BlockSpec((1, length, width), lambda j: (blocks - 1 - j, 0, 0))
    edge = pl.BlockSpec(
        (1, TILE, width), lambda j: (jnp.maximum(blocks - 2 - j, 0), last, 0)
    )
    low = jax.ShapeDtypeStruct((blocks, length, width), bf16)
    tile = jax.ShapeDtypeStruct((TILE, width), f32)
    count = 4 + taps.shape[0]
    return pl.pallas_call(
        backward_kernel,
        grid_spec=pltpu.PrefetchScalarGridSpec(
            num_scalar_prefetch=0,
            grid=(blocks,),
            in_specs=[
                block,
                block,
                edge,
                block,
                block,
                block,
                block,
                edge,
                pl.BlockSpec((length, masks.shape[1]), lambda j: (blocks - 1 - j, 0)),
                whole(*rim.shape),
                whole(*state_in.shape),
                whole(*after.shape),
                whole(*taps.shape),
                whole(*vecs.shape),
                whole(*rate_dense.shape),
                whole(*input_dense.shape),
            ],
            out_specs=[
                block,
                block,
                block,
                whole(TILE, width),
                whole(TILE, width),
                whole(count, width),
            ],
            scratch_shapes=[
                pltpu.VMEM((TILE, width), f32),
                pltpu.VMEM((taps.shape[0] - 1, TILE, width), f32),
                pltpu.VMEM((count, TILE, width), f32),
                pltpu.VMEM((length, width), f32),
                pltpu.VMEM((length, width), f32),
                pltpu.VMEM((length, width), f32),
            ],
        ),
        out_shape=[low, low, low, tile, tile, jax.ShapeDtypeStruct((count, width), f32)],
        compiler_params=pltpu.CompilerParams(vmem_limit_bytes=VMEM_LIMIT),
        cost_estimate=pl.CostEstimate(flops=1000, bytes_accessed=1000, transcendentals=0),
        name="recur_backward",
    )(
        direct,
        state,
        state,
        conv,
        sig_rate,
        sig_input,
        inner,
        inner,
        masks,
        rim,
        state_in,
        after,
        taps,
        vecs,
        rate_dense,
        input_dense,
    )


def dense_blocks(blocks):
    count, rows_in, cols_out = blocks.shape
    tall = blocks.reshape(count * rows_in, cols_out)
    wide = jnp.concatenate([tall] * count, axis=1)
    row = lax.broadcasted_iota(jnp.int32, wide.shape, 0) // rows_in
    col = lax.broadcasted_iota(jnp.int32, wide.shape, 1) // cols_out
    return jnp.where(row == col, wide, jnp.zeros_like(wide))


def diagonal_blocks(full, count):
    rows, cols = full.shape[0] // count, full.shape[1] // count
    return jnp.stack([full[i * rows : (i + 1) * rows, i * cols : (i + 1) * cols] for i in range(count)])


def rms(values):
    return lax.rsqrt(jnp.mean(values * values, axis=-1, keepdims=True) + epsilon)


def norm_back(grad, xhat, scale, root):
    e = grad * scale
    return root * (e - xhat * jnp.mean(e * xhat, axis=-1, keepdims=True)), jnp.sum(grad * xhat, axis=0)


def shards(
    tokens,
    mixer_gain,
    in_proj,
    branch_proj,
    conv_taps,
    conv_bias,
    rate_blocks,
    rate_bias,
    input_blocks,
    input_bias,
    decay_param,
    out_proj,
    dense_gain,
    gate_proj,
    up_proj,
    down_proj,
    segment_ids,
    cotangent,
):
    tp_place = lax.axis_index("tp")
    seq_place = lax.axis_index("seq")
    seq_size = lax.axis_size("seq")
    core = seq_place % 2
    tp_size = lax.axis_size("tp")
    gain_share = mixer_gain.shape[0]
    taps_n, width = conv_taps.shape
    rim_width = taps_n - 1
    length, model = tokens.shape
    group = length * tp_size
    blocks_n = rate_blocks.shape[0]

    in_t, branch_t = in_proj.T, branch_proj.T
    place = tp_place.astype(jnp.int32)[None]

    blocks = [tokens] + [swap(tokens, "tp", r) for r in range(1, tp_size)]
    blocks[1], gains, ids, rate_in, input_in, vec_in = tied(
        blocks[1],
        jnp.stack([mixer_gain, dense_gain]),
        segment_ids,
        rate_blocks,
        input_blocks,
        (conv_bias, rate_bias, input_bias, decay_param),
    )
    gains = gather_rows(gains)
    gains = gains.transpose(1, 0, 2).reshape(2, -1).astype(f32)
    mixer_scale, dense_scale = gains[0], gains[1]
    rim_ids = from_neighbour(ids[-rim_width:], -1)
    ext_ids = jnp.concatenate([rim_ids, ids])
    same = [ext_ids[rim_width - k : rim_width - k + group] == ids for k in range(1, taps_n)]
    masks = jnp.stack([same[0]] + same, axis=1).astype(f32)
    rate_dense = dense_blocks(rate_in)
    input_dense = dense_blocks(input_in)
    vecs = jnp.stack([*vec_in[:3], -8.0 * jax.nn.softplus(-vec_in[3])])
    *blocks, masks, rate_dense, input_dense, vecs = tied(*blocks, masks, rate_dense, input_dense, vecs)
    cot_all = lax.all_gather(cotangent, ("seq", "tp"), axis=0, tiled=True)

    normed, inner = norm_project(blocks, place, mixer_scale[None], in_t)
    rim = from_neighbour(inner[-1, -TILE:], -1)
    conv, conv_low, sig_rate, sig_input, keep_prefix, value_prefix, ends = recur_forward(
        inner, masks, rim, conv_taps, vecs, rate_dense, input_dense
    )
    ends, normed_b = tied(ends, normed)
    state_in = carry_in(ends[0, 0], ends[1, 0], False)
    branch_pre = project_t(normed_b, branch_t).reshape(inner.shape)
    state, mixed, mixer_part = mix_out(value_prefix, keep_prefix, branch_pre, state_in[None], out_proj)
    mixed = mixed.reshape(group, width)
    mixer_out = scatter_rows(mixer_part)
    mid = tokens.astype(f32) + mixer_out
    mid_root = rms(mid)
    xhat_dense = mid * mid_root
    normed_two = (xhat_dense * dense_scale).astype(bf16)

    chips = seq_size // 2
    same_core = [[core_no + 2 * i for i in range(chips)] for core_no in range(2)]
    rows_z = lax.all_gather(normed_two, "seq", axis=0, tiled=True, axis_index_groups=same_core)
    rows_two, cot_all = tied(gather_rows(normed_two).reshape(group, model), cot_all)
    hidden, normed_two_part = dense_rows(
        rows_two, cot_all, seq_place.astype(jnp.int32)[None], gate_proj, up_proj, down_proj
    )
    normed_two_grad = scatter_rows(normed_two_part.reshape(tp_size, length, model))
    dense_part = product(hidden, down_proj).astype(bf16)
    normed_two_grad, dense_part = tied(normed_two_grad, dense_part)
    mid_from_norm, dense_gain_part = norm_back(normed_two_grad, xhat_dense, dense_scale, mid_root)
    mid_grad = cotangent.astype(f32) + mid_from_norm
    mid_blocks = gather_rows(mid_grad.astype(bf16))
    mid_blocks, dense_part, rows_z = tied(mid_blocks, dense_part, rows_z)
    rows_spread = spread(rows_z)

    direct, branch_pre_grad, reach = mix_back(mid_blocks, out_proj, branch_pre, state, keep_prefix)
    branch_pre_grad = branch_pre_grad.reshape(group, width)
    mid_rows = mid_blocks.reshape(group, model)
    reach, direct, branch_pre_grad, mid_rows = tied(reach[0], direct, branch_pre_grad, mid_rows)
    after = carry_in(ends[0, 0], reach, True)
    out_full = product_left_t(mixed, mid_rows).astype(bf16)
    branch_full = product_left_t(branch_pre_grad, normed).astype(bf16)
    after, pair_full = tied(after, jnp.concatenate([out_full, branch_full]))
    pair_part = lax.psum_scatter(pair_full, "seq", scatter_dimension=0, tiled=True)
    tile = lambda v: jnp.broadcast_to(v, (TILE, width))
    rate_low, input_low, inner_grad, tail, rim_grad, sums = recur_backward(
        direct,
        state,
        conv,
        sig_rate,
        sig_input,
        inner,
        masks,
        rim,
        tile(state_in),
        tile(after),
        conv_taps,
        vecs,
        rate_dense,
        input_dense,
    )
    rows_mine, rim_grad = rows_spread(rim_grad)
    fixed = tail + from_neighbour(rim_grad, 1)
    low_rows = conv_low.reshape(group, width)
    rate_w = diagonal_blocks(product_left_t(low_rows, rate_low.reshape(group, width)), blocks_n)
    input_w = diagonal_blocks(product_left_t(low_rows, input_low.reshape(group, width)), blocks_n)
    inner_grad = lax.dynamic_update_slice(
        inner_grad, fixed.astype(bf16)[None], (tp_size - 1, length - TILE, 0)
    ).reshape(group, width)
    in_full = product_left_t(inner_grad, normed).astype(bf16)
    flat = lambda blocks: blocks.astype(bf16).reshape(width, -1)
    in_full = jnp.concatenate([in_full, flat(rate_w), flat(input_w)], axis=1)
    normed_part = (product(inner_grad, in_t) + product(branch_pre_grad, branch_t)).astype(bf16)
    rows_theirs = swap(rows_mine, "seq", 1)
    normed_part, in_full, pair_part, rows_mine, rows_theirs = tied(
        normed_part, in_full, pair_part, rows_mine, rows_theirs
    )
    pair_sum = lax.all_gather(pair_part, "seq", axis=0, tiled=True)
    in_part = lax.psum_scatter(in_full, "seq", scatter_dimension=0, tiled=True)
    normed_grad = scatter_rows(normed_part.reshape(tp_size, length, model))

    places = jnp.stack([core, tp_place]).astype(jnp.int32)
    blocked = lambda rows: rows.reshape(tp_size, chips, length, model)
    gate_w, up_w, down_w = dense_weight_grads(
        blocked(rows_mine), blocked(rows_theirs), cot_all, gate_proj, up_proj, down_proj, places
    )
    gate_w, up_w, down_w, in_part, normed_grad, sums, dense_part = tied(
        gate_w, up_w, down_w, in_part, normed_grad, sums, dense_part
    )
    in_sum = lax.all_gather(in_part, "seq", axis=0, tiled=True)
    gate_sum = joined(gate_w, swap(gate_w, "seq", 1), places, 1)
    up_sum = joined(up_w, swap(up_w, "seq", 1), places, 1)
    down_sum = joined(down_w, swap(down_w, "seq", 1), places, 0)

    own = tokens.astype(f32)
    own_root = rms(own)
    rows_grad, mixer_gain_part = norm_back(normed_grad, own * own_root, mixer_scale, own_root)
    tokens_grad = mid_grad + rows_grad
    gain_parts = sum_bits(jnp.stack([mixer_gain_part, dense_gain_part]), "tp")
    gain_own = lax.dynamic_slice_in_dim(gain_parts, tp_place * gain_share, gain_share, 1)
    gain_sum = sum_bits(gain_own, "seq")
    sums = sum_bits(sums, "seq")
    decay_sum = 8.0 * jax.nn.sigmoid(-decay_param) * sums[2]
    dense_out = scatter_rows(dense_part.reshape(tp_size, length, model))
    output = (mid + dense_out).astype(bf16)
    gate_sum, up_sum, down_sum, in_sum = tied(gate_sum, up_sum, down_sum, in_sum)
    out_sum, branch_sum = pair_sum[:width], pair_sum[width:]
    block_sum = in_sum[:, model:]
    in_sum = in_sum[:, :model]
    block_w = block_sum.shape[1] // 2
    rate_sum = block_sum[:, :block_w].astype(f32).reshape(rate_blocks.shape)
    input_sum = block_sum[:, block_w:].astype(f32).reshape(input_blocks.shape)
    return (
        output,
        tokens_grad,
        gain_sum[0],
        in_sum.astype(f32).T,
        branch_sum.astype(f32).T,
        sums[4 : 4 + taps_n],
        sums[3],
        rate_sum,
        sums[0],
        input_sum,
        sums[1],
        decay_sum,
        out_sum.astype(f32),
        gain_sum[1],
        gate_sum,
        up_sum,
        down_sum,
    )


def solution(mesh):
    return jax.shard_map(
        shards,
        mesh=mesh,
        in_specs=(
            P(("seq", "tp"), None),
            P("tp"),
            P(None, "tp"),
            P(None, "tp"),
            P(None, "tp"),
            P("tp"),
            P("tp", None, None),
            P("tp"),
            P("tp", None, None),
            P("tp"),
            P("tp"),
            P("tp", None),
            P("tp"),
            P(None, "tp"),
            P(None, "tp"),
            P("tp", None),
            P("seq"),
            P(("seq", "tp"), None),
        ),
        out_specs=(
            P(("seq", "tp"), None),
            P(("seq", "tp"), None),
            P("tp"),
            P(None, "tp"),
            P(None, "tp"),
            P(None, "tp"),
            P("tp"),
            P("tp", None, None),
            P("tp"),
            P("tp", None, None),
            P("tp"),
            P("tp"),
            P("tp", None),
            P("tp"),
            P(None, "tp"),
            P(None, "tp"),
            P("tp", None),
        ),
        check_vma=False,
    )
```

```python
import math

import jax
import jax.numpy as jnp
from jax import lax
from jax.experimental import pallas as pl
from jax.experimental.pallas import tpu as pltpu
from jax.sharding import PartitionSpec as P

epsilon = 1e-06
f32 = jnp.float32
bf16 = jnp.bfloat16
TILE = 8
VMEM_LIMIT = 50 * 1024 * 1024


def product(left, right):
    return jnp.dot(left, right, preferred_element_type=f32)


def product_left_t(left, right):
    return lax.dot_general(left, right, (((0,), (0,)), ((), ())), preferred_element_type=f32)


def product_right_t(left, right):
    return lax.dot_general(left, right, (((1,), (1,)), ((), ())), preferred_element_type=f32)


def gelu_tanh(values):
    return jax.nn.gelu(values, approximate=True)


def tied(*values):
    return lax.optimization_barrier(values)


def swap(value, axis, bit):
    count = lax.axis_size(axis)
    return lax.ppermute(value, axis, [(i, i ^ bit) for i in range(count)])


def gather_rows(rows):
    count = lax.axis_size("tp")
    place = lax.axis_index("tp")
    whole = jnp.zeros((count,) + rows.shape, rows.dtype)
    for r in range(count):
        block = rows if r == 0 else swap(rows, "tp", r)
        whole = lax.dynamic_update_index_in_dim(whole, block, place ^ r, 0)
    return whole


def spread(rows):
    count = lax.axis_size("tp")
    if count != 4:
        whole = jnp.stack([rows] + [swap(rows, "tp", r) for r in range(1, count)])
        return lambda *after: tied(whole, *after)
    half = rows.shape[0] // 2
    sides = swap(rows, "tp", 1), swap(rows, "tp", 2)

    def finish(*after):
        one, two, *after = tied(*sides, *after)
        far = jnp.concatenate([swap(two[:half], "tp", 1), swap(one[half:], "tp", 2)])
        return (jnp.stack([rows, one, two, far]), *after)

    return finish


def scatter_rows(blocks):
    place = lax.axis_index("tp")
    block = lambda r: lax.dynamic_index_in_dim(blocks, place ^ r, 0, False)
    total = block(0).astype(f32)
    for r in range(1, lax.axis_size("tp")):
        total = total + swap(block(r), "tp", r).astype(f32)
    return total


def carry_in(keep_total, value_total, backward):
    place = lax.axis_index("seq")
    total = jnp.stack([keep_total, value_total])
    before = jnp.stack([jnp.ones_like(keep_total), jnp.zeros_like(value_total)])
    bit = 1
    while bit < lax.axis_size("seq"):
        other = swap(total, "seq", bit)
        upper = (place & bit) != 0
        earlier = jnp.logical_not(upper) if backward else upper
        joined_before = jnp.stack([other[0] * before[0], before[0] * other[1] + before[1]])
        before = jnp.where(earlier, joined_before, before)
        first = jnp.where(earlier, other, total)
        second = jnp.where(earlier, total, other)
        total = jnp.stack([first[0] * second[0], second[0] * first[1] + second[1]])
        bit *= 2
    return before[1]


def from_neighbour(value, step):
    count = lax.axis_size("seq")
    place = lax.axis_index("seq")
    inside = lax.ppermute(value, "seq", [(i, i ^ 1) for i in range(count)])
    pairs = [(i, i + 1) for i in range(1, count - 1, 2)] + [(i + 1, i) for i in range(1, count - 1, 2)]
    across = lax.ppermute(value, "seq", pairs)
    return jnp.where((place % 2 == 0) == (step == 1), inside, across)


def sum_bits(value, axis):
    bit = 1
    while bit < lax.axis_size(axis):
        value = value + swap(value, axis, bit)
        bit *= 2
    return value


def both_halves(mine, theirs, core):
    first = jnp.where(core == 0, mine, theirs)
    second = jnp.where(core == 0, theirs, mine)
    return first, second


def gelu_grads(gate_pre, up_pre, hidden_grad):
    square = gate_pre * gate_pre
    inner = math.sqrt(2.0 / math.pi) * gate_pre * (1.0 + 0.044715 * square)
    half = 0.5 * (1.0 + jnp.tanh(inner))
    act = gate_pre * half
    slope = half + 2.0 * math.sqrt(2.0 / math.pi) * act * (1.0 - half) * (1.0 + 3.0 * 0.044715 * square)
    return act * up_pre, hidden_grad * up_pre * slope, hidden_grad * act


def dense_weight_grads(mine, theirs, cot_all, gate_proj, up_proj, down_proj, places):
    tp_size, chips, block, model = mine.shape
    half = gate_proj.shape[1] // 2
    cot_all = cot_all.reshape(chips, 2, tp_size, block, model)
    part = math.gcd(chips, 4)
    length = part * block
    per_core = tp_size * chips // part
    steps, outs = 2 * per_core, 4
    tile = math.gcd(half, 256)
    left_t = (((0,), (0,)), ((), ()))
    right_t = (((1,), (1,)), ((), ()))

    def kernel(core_ref, mine_ref, theirs_ref, cot_ref, gate_ref, up_ref, down_ref, *rest):
        gate_out, up_out, down_out, acc_g, acc_u, acc_d, hid, gg, ug, x_ref = rest
        i = pl.program_id(0)

        @pl.when(i < per_core)
        def _():
            x_ref[...] = mine_ref[...].reshape(length, model)

        @pl.when(jnp.logical_and(i >= per_core, i < steps))
        def _():
            x_ref[...] = theirs_ref[...].reshape(length, model)

        @pl.when(i == 0)
        def _():
            acc_g[...] = jnp.zeros_like(acc_g)
            acc_u[...] = jnp.zeros_like(acc_u)
            acc_d[...] = jnp.zeros_like(acc_d)

        @pl.when(i < steps)
        def _():
            cots = cot_ref[...].reshape(length, model)
            for n in range(half // tile):
                cols = slice(n * tile, (n + 1) * tile)
                gate_pre = jnp.dot(x_ref[...], gate_ref[:, cols], preferred_element_type=f32)
                up_pre = jnp.dot(x_ref[...], up_ref[:, cols], preferred_element_type=f32)
                hidden_grad = lax.dot_general(cots, down_ref[cols, :], right_t, preferred_element_type=f32)
                a, b, c = gelu_grads(gate_pre, up_pre, hidden_grad)
                hid[:, cols] = a.astype(bf16)
                gg[:, cols] = b.astype(bf16)
                ug[:, cols] = c.astype(bf16)
            acc_g[...] += lax.dot_general(x_ref[...], gg[...], left_t, preferred_element_type=f32)
            acc_u[...] += lax.dot_general(x_ref[...], ug[...], left_t, preferred_element_type=f32)
            acc_d[...] += lax.dot_general(hid[...], cots, left_t, preferred_element_type=f32)

        @pl.when(i >= steps)
        def _():
            wide = pl.ds(pl.multiple_of((i - steps) * (model // outs), model // outs), model // outs)
            low = pl.ds(pl.multiple_of((i - steps) * (half // outs), half // outs), half // outs)
            gate_out[...] = acc_g[wide, :].astype(bf16)
            up_out[...] = acc_u[wide, :].astype(bf16)
            down_out[...] = acc_d[low, :].astype(bf16)

    once = pl.Buffered(1)
    groups = chips // part
    out_index = lambda i, c: (jnp.maximum(i - steps, 0), 0)

    def cot_index(i, c):
        i = jnp.minimum(i, steps - 1)
        n = i % per_core
        return n % groups, c[0] ^ (i // per_core), c[1] ^ (n // groups), 0, 0

    def rows_index(first):
        def index(i, c):
            n = jnp.clip(i - first, 0, per_core - 1)
            return n // groups, n % groups, 0, 0

        return pl.BlockSpec((1, part, block, model), index)

    return pl.pallas_call(
        kernel,
        grid_spec=pltpu.PrefetchScalarGridSpec(
            num_scalar_prefetch=1,
            grid=(steps + outs,),
            in_specs=[
                rows_index(0),
                rows_index(per_core),
                pl.BlockSpec((part, 1, 1, block, model), cot_index),
                pl.BlockSpec((model, half), lambda i, c: (0, c[0]), pipeline_mode=once),
                pl.BlockSpec((model, half), lambda i, c: (0, c[0]), pipeline_mode=once),
                pl.BlockSpec((half, model), lambda i, c: (c[0], 0), pipeline_mode=once),
            ],
            out_specs=[
                pl.BlockSpec((model // outs, half), out_index),
                pl.BlockSpec((model // outs, half), out_index),
                pl.BlockSpec((half // outs, model), out_index),
            ],
            scratch_shapes=[
                pltpu.VMEM((model, half), f32),
                pltpu.VMEM((model, half), f32),
                pltpu.VMEM((half, model), f32),
                pltpu.VMEM((length, half), bf16),
                pltpu.VMEM((length, half), bf16),
                pltpu.VMEM((length, half), bf16),
                pltpu.VMEM((length, model), bf16),
            ],
        ),
        out_shape=[
            jax.ShapeDtypeStruct((model, half), bf16),
            jax.ShapeDtypeStruct((model, half), bf16),
            jax.ShapeDtypeStruct((half, model), bf16),
        ],
        compiler_params=pltpu.CompilerParams(vmem_limit_bytes=60 * 1024 * 1024),
        cost_estimate=pl.CostEstimate(flops=1000, bytes_accessed=1000, transcendentals=0),
        name="dense_weight_grads",
    )(places, mine, theirs, cot_all, gate_proj, up_proj, down_proj)


def joined(mine, theirs, core, axis):
    rows, cols = mine.shape
    block = math.gcd(rows, 256)
    steps = rows // block

    def kernel(core_ref, mine_ref, theirs_ref, out_ref):
        for low in range(2):

            @pl.when(core_ref[0] == low)
            def _(low=low):
                pair = (mine_ref, theirs_ref) if low == 0 else (theirs_ref, mine_ref)
                if axis == 1:
                    out_ref[:, :cols] = pair[0][...].astype(f32)
                    out_ref[:, cols:] = pair[1][...].astype(f32)
                else:
                    out_ref[0] = pair[0][...].astype(f32)
                    out_ref[1] = pair[1][...].astype(f32)

    half = pl.BlockSpec((block, cols), lambda i, c: (i, 0))
    if axis == 1:
        out_spec = pl.BlockSpec((block, 2 * cols), lambda i, c: (i, 0))
        out_shape = jax.ShapeDtypeStruct((rows, 2 * cols), f32)
    else:
        out_spec = pl.BlockSpec((2, block, cols), lambda i, c: (0, i, 0))
        out_shape = jax.ShapeDtypeStruct((2, rows, cols), f32)
    out = pl.pallas_call(
        kernel,
        grid_spec=pltpu.PrefetchScalarGridSpec(
            num_scalar_prefetch=1, grid=(steps,), in_specs=[half, half], out_specs=out_spec
        ),
        out_shape=out_shape,
        compiler_params=pltpu.CompilerParams(vmem_limit_bytes=VMEM_LIMIT),
        cost_estimate=pl.CostEstimate(flops=0, bytes_accessed=12 * rows * cols, transcendentals=0),
        name="joined",
    )(core, mine, theirs)
    return out if axis == 1 else out.reshape(2 * rows, cols)


def dense_rows(rows, cot_all, group_place, gate_proj, up_proj, down_proj):
    length, model = rows.shape
    width = gate_proj.shape[1]
    tile = math.gcd(width, 256)
    out_tile = math.gcd(model, 256)
    first, second = width // tile, model // out_tile
    right_t = (((1,), (1,)), ((), ()))

    def kernel(place_ref, x_ref, c_ref, gate_ref, up_ref, down_ref, hidden_ref, grad_ref, gates, ups, gate_grads, up_grads):
        j = pl.program_id(0)

        @pl.when(j < first)
        def _():
            gate_pre = jnp.dot(x_ref[...], gate_ref[...], preferred_element_type=f32)
            up_pre = jnp.dot(x_ref[...], up_ref[...], preferred_element_type=f32)
            hidden_grad = lax.dot_general(c_ref[...], down_ref[...], right_t, preferred_element_type=f32)
            hidden, gate_grad, up_grad = gelu_grads(gate_pre, up_pre, hidden_grad)
            hidden_ref[...] = hidden.astype(bf16)
            at = pl.ds(pl.multiple_of(j * tile, tile), tile)
            gates[:, at] = gate_ref[...]
            ups[:, at] = up_ref[...]
            gate_grads[:, at] = gate_grad.astype(bf16)
            up_grads[:, at] = up_grad.astype(bf16)

        @pl.when(j >= first)
        def _():
            at = pl.ds(pl.multiple_of((j - first) * out_tile, out_tile), out_tile)
            part = lax.dot_general(gate_grads[...], gates[at, :], right_t, preferred_element_type=f32)
            part = part + lax.dot_general(up_grads[...], ups[at, :], right_t, preferred_element_type=f32)
            grad_ref[...] = part.astype(bf16)

    clamp = lambda j: jnp.minimum(j, first - 1)
    wide = pl.BlockSpec((model, tile), lambda j, p: (0, clamp(j)))
    return pl.pallas_call(
        kernel,
        grid_spec=pltpu.PrefetchScalarGridSpec(
            num_scalar_prefetch=1,
            grid=(first + second,),
            in_specs=[
                pl.BlockSpec((length, model), lambda j, p: (0, 0)),
                pl.BlockSpec((length, model), lambda j, p: (p[0], 0)),
                wide,
                wide,
                pl.BlockSpec((tile, model), lambda j, p: (clamp(j), 0)),
            ],
            out_specs=[
                pl.BlockSpec((length, tile), lambda j, p: (0, clamp(j))),
                pl.BlockSpec((length, out_tile), lambda j, p: (0, jnp.maximum(j - first, 0))),
            ],
            scratch_shapes=[
                pltpu.VMEM((model, width), bf16),
                pltpu.VMEM((model, width), bf16),
                pltpu.VMEM((length, width), bf16),
                pltpu.VMEM((length, width), bf16),
            ],
        ),
        out_shape=[
            jax.ShapeDtypeStruct((length, width), bf16),
            jax.ShapeDtypeStruct((length, model), bf16),
        ],
        compiler_params=pltpu.CompilerParams(vmem_limit_bytes=VMEM_LIMIT),
        name="dense_rows",
    )(group_place, rows, cot_all, gate_proj, up_proj, down_proj)


def project_t(rows, weight_t):
    total, model = rows.shape
    width = weight_t.shape[0]
    length = math.gcd(total, 256)

    def kernel(rows_ref, weight_ref, out_ref):
        out_ref[...] = lax.dot_general(
            rows_ref[...], weight_ref[...], (((1,), (1,)), ((), ())), preferred_element_type=f32
        )

    return pl.pallas_call(
        kernel,
        grid=(total // length,),
        in_specs=[
            pl.BlockSpec((length, model), lambda j: (j, 0)),
            pl.BlockSpec((width, model), lambda j: (0, 0)),
        ],
        out_specs=pl.BlockSpec((length, width), lambda j: (j, 0)),
        out_shape=jax.ShapeDtypeStruct((total, width), f32),
        compiler_params=pltpu.CompilerParams(vmem_limit_bytes=VMEM_LIMIT),
        name="project_t",
    )(rows, weight_t)


def mix_out(value_prefix, keep_prefix, branch_pre, state_in, out_proj):
    blocks, length, width = value_prefix.shape
    model = out_proj.shape[1]

    def kernel(value_ref, keep_ref, branch_ref, in_ref, out_ref, state_ref, mixed_ref, part_ref):
        state = value_ref[0] + keep_ref[0] * in_ref[...]
        state_ref[0] = state
        mixed = (state * gelu_tanh(branch_ref[0])).astype(bf16)
        mixed_ref[0] = mixed
        part_ref[0] = jnp.dot(mixed, out_ref[...], preferred_element_type=f32).astype(bf16)

    block = pl.BlockSpec((1, length, width), lambda j: (j, 0, 0))
    whole = lambda *shape: pl.BlockSpec(shape, lambda j: (0,) * len(shape))
    return pl.pallas_call(
        kernel,
        grid=(blocks,),
        in_specs=[block, block, block, whole(1, width), whole(width, model)],
        out_specs=[block, block, pl.BlockSpec((1, length, model), lambda j: (j, 0, 0))],
        out_shape=[
            jax.ShapeDtypeStruct((blocks, length, width), f32),
            jax.ShapeDtypeStruct((blocks, length, width), bf16),
            jax.ShapeDtypeStruct((blocks, length, model), bf16),
        ],
        compiler_params=pltpu.CompilerParams(vmem_limit_bytes=VMEM_LIMIT),
        name="mix_out",
    )(value_prefix, keep_prefix, branch_pre, state_in, out_proj)


def mix_back(mid_rows, out_proj, branch_pre, state, keep_prefix):
    blocks, length, width = state.shape
    model = out_proj.shape[1]
    tiles = length // 16

    def kernel(mid_ref, out_ref, branch_ref, state_ref, keep_ref, direct_ref, branch_grad_ref, reach_ref, mixed, acc):
        j = pl.program_id(0)
        mixed[...] = lax.dot_general(
            mid_ref[0], out_ref[...], (((1,), (1,)), ((), ())), preferred_element_type=f32
        )

        @pl.when(j == 0)
        def _():
            acc[...] = jnp.zeros_like(acc)

        def tile(i, total):
            at = pl.ds(pl.multiple_of(i * 16, 16), 16)
            grad = mixed[at, :]
            pre = branch_ref[0, at, :]
            square = pre * pre
            inner = math.sqrt(2.0 / math.pi) * pre * (1.0 + 0.044715 * square)
            half = 0.5 * (1.0 + jnp.tanh(inner))
            act = pre * half
            slope = half + 2.0 * math.sqrt(2.0 / math.pi) * act * (1.0 - half) * (1.0 + 3.0 * 0.044715 * square)
            direct = grad * act
            direct_ref[0, at, :] = direct
            branch_grad_ref[0, at, :] = (grad * state_ref[0, at, :] * slope).astype(bf16)
            return total + direct * keep_ref[0, at, :]

        acc[...] = lax.fori_loop(0, tiles, tile, acc[...])

        @pl.when(j == blocks - 1)
        def _():
            reach_ref[...] = jnp.sum(acc[...], axis=0, keepdims=True)

    block = pl.BlockSpec((1, length, width), lambda j: (j, 0, 0))
    whole = lambda *shape: pl.BlockSpec(shape, lambda j: (0,) * len(shape))
    return pl.pallas_call(
        kernel,
        grid=(blocks,),
        in_specs=[pl.BlockSpec((1, length, model), lambda j: (j, 0, 0)), whole(width, model), block, block, block],
        out_specs=[block, block, whole(1, width)],
        out_shape=[
            jax.ShapeDtypeStruct((blocks, length, width), f32),
            jax.ShapeDtypeStruct((blocks, length, width), bf16),
            jax.ShapeDtypeStruct((1, width), f32),
        ],
        scratch_shapes=[pltpu.VMEM((length, width), f32), pltpu.VMEM((16, width), f32)],
        compiler_params=pltpu.CompilerParams(vmem_limit_bytes=VMEM_LIMIT),
        name="mix_back",
    )(mid_rows, out_proj, branch_pre, state, keep_prefix)


def minus_expm1(x):
    series = 1.0 / 40320.0
    for term in (1.0 / 5040.0, 1.0 / 720.0, 1.0 / 120.0, 1.0 / 24.0, 1.0 / 6.0, 0.5, 1.0):
        series = series * x + term
    return jnp.where(x > -0.35, -x * series, 1.0 - jnp.exp(x))


def rows_of(shape):
    return lax.broadcasted_iota(jnp.int32, shape, 0)


def down(cur, prev, by, row):
    return jnp.where(row >= by, pltpu.roll(cur, by, 0), pltpu.roll(prev, by, 0))


def up(cur, after, by, row):
    return jnp.where(row < TILE - by, pltpu.roll(cur, TILE - by, 0), pltpu.roll(after, TILE - by, 0))


def last_row(tile):
    return jnp.broadcast_to(tile[TILE - 1 :, :], tile.shape)


def first_row(tile):
    return jnp.broadcast_to(tile[:1, :], tile.shape)


def forward_kernel(
    inner_ref,
    mask_ref,
    rim_ref,
    taps_ref,
    vec_ref,
    rate_ref,
    input_ref,
    conv_ref,
    low_ref,
    sig_rate_ref,
    sig_input_ref,
    keep_ref,
    value_ref,
    end_ref,
    prev_ref,
    carry_ref,
    rate_raw_ref,
    input_raw_ref,
):
    step = pl.program_id(0)
    length, width = inner_ref.shape[1:]
    tiles = length // TILE
    taps_n = taps_ref.shape[0]

    @pl.when(step == 0)
    def _():
        prev_ref[...] = rim_ref[...]
        carry_ref[0] = jnp.ones((TILE, width), f32)
        carry_ref[1] = jnp.zeros((TILE, width), f32)

    row = rows_of((TILE, width))

    def conv_tile(i, prev):
        at = pl.ds(pl.multiple_of(i * TILE, TILE), TILE)
        cur = inner_ref[0, at, :]
        masks = mask_ref[at, :]
        total = vec_ref[0:1, :] + taps_ref[0:1, :] * cur
        for k in range(1, taps_n):
            total = total + taps_ref[k : k + 1, :] * (down(cur, prev, k, row) * masks[:, k : k + 1])
        conv_ref[0, at, :] = total
        return cur

    prev_ref[...] = lax.fori_loop(0, tiles, conv_tile, prev_ref[...])
    low = conv_ref[0].astype(bf16)
    low_ref[0] = low
    rate_raw_ref[...] = jnp.dot(low, rate_ref[...], preferred_element_type=f32)
    input_raw_ref[...] = jnp.dot(low, input_ref[...], preferred_element_type=f32)

    def gate_tile(i, carry):
        keep_in, value_in = carry
        at = pl.ds(pl.multiple_of(i * TILE, TILE), TILE)
        sig_rate = jax.nn.sigmoid(rate_raw_ref[at, :] + vec_ref[1:2, :])
        sig_input = jax.nn.sigmoid(input_raw_ref[at, :] + vec_ref[2:3, :])
        sig_rate_ref[0, at, :] = sig_rate
        sig_input_ref[0, at, :] = sig_input
        log_decay = sig_rate * vec_ref[3:4, :]
        a = jnp.exp(log_decay) * mask_ref[at, 0:1]
        b = jnp.sqrt(minus_expm1(2.0 * log_decay)) * sig_input * conv_ref[0, at, :]
        for d in (1, 2, 4):
            a_before = jnp.where(row >= d, pltpu.roll(a, d, 0), 1.0)
            b_before = jnp.where(row >= d, pltpu.roll(b, d, 0), 0.0)
            b = b + a * b_before
            a = a * a_before
        b = b + a * value_in
        a = a * keep_in
        keep_ref[0, at, :] = a
        value_ref[0, at, :] = b
        return last_row(a), last_row(b)

    keep_end, value_end = lax.fori_loop(0, tiles, gate_tile, (carry_ref[0], carry_ref[1]))
    carry_ref[0] = keep_end
    carry_ref[1] = value_end
    end_ref[0] = keep_end
    end_ref[1] = value_end


def backward_kernel(
    direct_ref,
    state_ref,
    state_prev_ref,
    conv_ref,
    sig_rate_ref,
    sig_input_ref,
    inner_ref,
    inner_prev_ref,
    mask_ref,
    rim_ref,
    state_in_ref,
    after_ref,
    taps_ref,
    vec_ref,
    rate_ref,
    input_ref,
    rate_grad_ref,
    input_grad_ref,
    inner_grad_ref,
    tail_ref,
    rim_grad_ref,
    sums_ref,
    carry_ref,
    next_ref,
    acc_ref,
    rate_f_ref,
    input_f_ref,
    conv_f_ref,
):
    step = pl.program_id(0)
    steps = pl.num_programs(0)
    length, width = direct_ref.shape[1:]
    tiles = length // TILE
    taps_n = taps_ref.shape[0]
    row = rows_of((TILE, width))
    is_first_block = step == steps - 1

    @pl.when(step == 0)
    def _():
        carry_ref[...] = after_ref[...]
        next_ref[...] = jnp.zeros_like(next_ref)
        acc_ref[...] = jnp.zeros_like(acc_ref)

    edge_state = jnp.where(is_first_block, state_in_ref[...], state_prev_ref[0])
    edge_inner = jnp.where(is_first_block, rim_ref[...], inner_prev_ref[0])
    neg_rate = vec_ref[3:4, :]

    def gate_tile(n, carry):
        after, acc_rate, acc_input, acc_decay = carry
        i = tiles - 1 - n
        at = pl.ds(pl.multiple_of(i * TILE, TILE), TILE)
        before = pl.ds(pl.multiple_of(jnp.maximum(i - 1, 0) * TILE, TILE), TILE)
        direct = direct_ref[0, at, :]
        sig_rate = sig_rate_ref[0, at, :]
        sig_input = sig_input_ref[0, at, :]
        conv = conv_ref[0, at, :]
        log_decay = sig_rate * neg_rate
        decay = jnp.exp(log_decay)
        keep = decay * mask_ref[at, 0:1]
        room = minus_expm1(2.0 * log_decay)
        root = jnp.sqrt(room)
        a = keep
        b = keep * direct
        for d in (1, 2, 4):
            a_after = jnp.where(row < TILE - d, pltpu.roll(a, TILE - d, 0), 1.0)
            b_after = jnp.where(row < TILE - d, pltpu.roll(b, TILE - d, 0), 0.0)
            b = b + a * b_after
            a = a * a_after
        reach = b + a * after
        grad = direct + up(reach, after, 1, row)
        prev_tile = jnp.where(i == 0, edge_state, state_ref[0, before, :])
        state_prev = down(state_ref[0, at, :], prev_tile, 1, row)
        grad_root = grad * root
        gated = grad_root * sig_input
        decay_grad = grad * (keep * state_prev - sig_input * conv * (decay * decay) / root)
        rate_grad = decay_grad * neg_rate * (sig_rate * (1.0 - sig_rate))
        input_grad = gated * conv * (1.0 - sig_input)
        rate_f_ref[at, :] = rate_grad
        input_f_ref[at, :] = input_grad
        conv_f_ref[at, :] = gated
        return (
            first_row(reach),
            acc_rate + rate_grad,
            acc_input + input_grad,
            acc_decay + decay_grad * sig_rate,
        )

    after, acc_rate, acc_input, acc_decay = lax.fori_loop(
        0, tiles, gate_tile, (carry_ref[...], acc_ref[0], acc_ref[1], acc_ref[2])
    )
    carry_ref[...] = after
    acc_ref[0] = acc_rate
    acc_ref[1] = acc_input
    acc_ref[2] = acc_decay
    rate_low = rate_f_ref[...].astype(bf16)
    input_low = input_f_ref[...].astype(bf16)
    rate_grad_ref[0] = rate_low
    input_grad_ref[0] = input_low
    right_t = (((1,), (1,)), ((), ()))
    conv_f_ref[...] += lax.dot_general(
        rate_low, rate_ref[...], right_t, preferred_element_type=f32
    ) + lax.dot_general(input_low, input_ref[...], right_t, preferred_element_type=f32)

    def conv_tile(n, carry):
        acc_bias, acc_taps, nexts = carry
        i = tiles - 1 - n
        at = pl.ds(pl.multiple_of(i * TILE, TILE), TILE)
        before = pl.ds(pl.multiple_of(jnp.maximum(i - 1, 0) * TILE, TILE), TILE)
        grad = conv_f_ref[at, :]
        masks = mask_ref[at, :]
        cur = inner_ref[0, at, :]
        prev = jnp.where(i == 0, edge_inner, inner_ref[0, before, :])
        total = grad * taps_ref[0:1, :]
        new_taps = [acc_taps[0] + grad * cur]
        new_nexts = []
        for k in range(1, taps_n):
            masked = grad * masks[:, k : k + 1]
            part = masked * taps_ref[k : k + 1, :]
            total = total + up(part, nexts[k - 1], k, row)
            new_taps.append(acc_taps[k] + masked * down(cur, prev, k, row))
            new_nexts.append(part)
        rate_f_ref[at, :] = total
        return acc_bias + grad, tuple(new_taps), tuple(new_nexts)

    acc_bias, acc_taps, nexts = lax.fori_loop(
        0,
        tiles,
        conv_tile,
        (
            acc_ref[3],
            tuple(acc_ref[4 + k] for k in range(taps_n)),
            tuple(next_ref[k] for k in range(taps_n - 1)),
        ),
    )
    acc_ref[3] = acc_bias
    for k in range(taps_n):
        acc_ref[4 + k] = acc_taps[k]
    for k in range(taps_n - 1):
        next_ref[k] = nexts[k]
    inner_grad_ref[0] = rate_f_ref[...].astype(bf16)

    @pl.when(step == 0)
    def _():
        tail_ref[...] = rate_f_ref[length - TILE :, :]

    @pl.when(is_first_block)
    def _():
        zero = jnp.zeros((TILE, width), f32)
        total = zero
        for k in range(1, taps_n):
            total = total + up(zero, nexts[k - 1], k, row)
        rim_grad_ref[...] = total
        sums_ref[...] = jnp.sum(acc_ref[...], axis=1)


def norm_project(blocks, place, gain, weight_t):
    count = len(blocks)
    length, model = blocks[0].shape
    width = weight_t.shape[0]

    def kernel(place_ref, *refs):
        ins, gain_ref, weight_ref, normed_ref, out_ref = refs[:count], *refs[count:]
        j = pl.program_id(0)
        for r in range(count):

            @pl.when((j ^ place_ref[0]) == r)
            def _(source=ins[r]):
                x = source[...].astype(f32)
                root = lax.rsqrt(jnp.mean(x * x, axis=-1, keepdims=True) + epsilon)
                normed_ref[...] = (x * root * gain_ref[...]).astype(bf16)

        out_ref[0] = lax.dot_general(
            normed_ref[...], weight_ref[...], (((1,), (1,)), ((), ())), preferred_element_type=f32
        )

    whole = lambda *shape: pl.BlockSpec(shape, lambda j, p: (0,) * len(shape))
    return pl.pallas_call(
        kernel,
        grid_spec=pltpu.PrefetchScalarGridSpec(
            num_scalar_prefetch=1,
            grid=(count,),
            in_specs=[whole(length, model)] * count + [whole(1, model), whole(width, model)],
            out_specs=[
                pl.BlockSpec((length, model), lambda j, p: (j, 0)),
                pl.BlockSpec((1, length, width), lambda j, p: (j, 0, 0)),
            ],
        ),
        out_shape=[
            jax.ShapeDtypeStruct((count * length, model), bf16),
            jax.ShapeDtypeStruct((count, length, width), f32),
        ],
        compiler_params=pltpu.CompilerParams(vmem_limit_bytes=VMEM_LIMIT),
        name="norm_project",
    )(place, *blocks, gain, weight_t)


def recur_forward(inner, masks, rim, taps, vecs, rate_dense, input_dense):
    blocks, length, width = inner.shape
    whole = lambda *shape: pl.BlockSpec(shape, lambda j: (0,) * len(shape))
    block = pl.BlockSpec((1, length, width), lambda j: (j, 0, 0))
    full = jax.ShapeDtypeStruct((blocks, length, width), f32)
    return pl.pallas_call(
        forward_kernel,
        grid_spec=pltpu.PrefetchScalarGridSpec(
            num_scalar_prefetch=0,
            grid=(blocks,),
            in_specs=[
                block,
                pl.BlockSpec((length, masks.shape[1]), lambda j: (j, 0)),
                whole(*rim.shape),
                whole(*taps.shape),
                whole(*vecs.shape),
                whole(*rate_dense.shape),
                whole(*input_dense.shape),
            ],
            out_specs=[block, block, block, block, block, block, whole(2, TILE, width)],
            scratch_shapes=[
                pltpu.VMEM((TILE, width), f32),
                pltpu.VMEM((2, TILE, width), f32),
                pltpu.VMEM((length, width), f32),
                pltpu.VMEM((length, width), f32),
            ],
        ),
        out_shape=[
            full,
            jax.ShapeDtypeStruct((blocks, length, width), bf16),
            full,
            full,
            full,
            full,
            jax.ShapeDtypeStruct((2, TILE, width), f32),
        ],
        compiler_params=pltpu.CompilerParams(vmem_limit_bytes=VMEM_LIMIT),
        name="recur_forward",
    )(inner, masks, rim, taps, vecs, rate_dense, input_dense)


def recur_backward(
    direct, state, conv, sig_rate, sig_input, inner, masks, rim, state_in, after, taps, vecs, rate_dense, input_dense
):
    blocks, length, width = inner.shape
    last = length // TILE - 1
    whole = lambda *shape: pl.BlockSpec(shape, lambda j: (0,) * len(shape))
    block = pl.BlockSpec((1, length, width), lambda j: (blocks - 1 - j, 0, 0))
    edge = pl.BlockSpec(
        (1, TILE, width), lambda j: (jnp.maximum(blocks - 2 - j, 0), last, 0)
    )
    low = jax.ShapeDtypeStruct((blocks, length, width), bf16)
    tile = jax.ShapeDtypeStruct((TILE, width), f32)
    count = 4 + taps.shape[0]
    return pl.pallas_call(
        backward_kernel,
        grid_spec=pltpu.PrefetchScalarGridSpec(
            num_scalar_prefetch=0,
            grid=(blocks,),
            in_specs=[
                block,
                block,
                edge,
                block,
                block,
                block,
                block,
                edge,
                pl.BlockSpec((length, masks.shape[1]), lambda j: (blocks - 1 - j, 0)),
                whole(*rim.shape),
                whole(*state_in.shape),
                whole(*after.shape),
                whole(*taps.shape),
                whole(*vecs.shape),
                whole(*rate_dense.shape),
                whole(*input_dense.shape),
            ],
            out_specs=[
                block,
                block,
                block,
                whole(TILE, width),
                whole(TILE, width),
                whole(count, width),
            ],
            scratch_shapes=[
                pltpu.VMEM((TILE, width), f32),
                pltpu.VMEM((taps.shape[0] - 1, TILE, width), f32),
                pltpu.VMEM((count, TILE, width), f32),
                pltpu.VMEM((length, width), f32),
                pltpu.VMEM((length, width), f32),
                pltpu.VMEM((length, width), f32),
            ],
        ),
        out_shape=[low, low, low, tile, tile, jax.ShapeDtypeStruct((count, width), f32)],
        compiler_params=pltpu.CompilerParams(vmem_limit_bytes=VMEM_LIMIT),
        cost_estimate=pl.CostEstimate(flops=1000, bytes_accessed=1000, transcendentals=0),
        name="recur_backward",
    )(
        direct,
        state,
        state,
        conv,
        sig_rate,
        sig_input,
        inner,
        inner,
        masks,
        rim,
        state_in,
        after,
        taps,
        vecs,
        rate_dense,
        input_dense,
    )


def dense_blocks(blocks):
    count, rows_in, cols_out = blocks.shape
    tall = blocks.reshape(count * rows_in, cols_out)
    wide = jnp.concatenate([tall] * count, axis=1)
    row = lax.broadcasted_iota(jnp.int32, wide.shape, 0) // rows_in
    col = lax.broadcasted_iota(jnp.int32, wide.shape, 1) // cols_out
    return jnp.where(row == col, wide, jnp.zeros_like(wide))


def diagonal_blocks(full, count):
    rows, cols = full.shape[0] // count, full.shape[1] // count
    return jnp.stack([full[i * rows : (i + 1) * rows, i * cols : (i + 1) * cols] for i in range(count)])


def rms(values):
    return lax.rsqrt(jnp.mean(values * values, axis=-1, keepdims=True) + epsilon)


def norm_back(grad, xhat, scale, root):
    e = grad * scale
    return root * (e - xhat * jnp.mean(e * xhat, axis=-1, keepdims=True)), jnp.sum(grad * xhat, axis=0)


def shards(
    tokens,
    mixer_gain,
    in_proj,
    branch_proj,
    conv_taps,
    conv_bias,
    rate_blocks,
    rate_bias,
    input_blocks,
    input_bias,
    decay_param,
    out_proj,
    dense_gain,
    gate_proj,
    up_proj,
    down_proj,
    segment_ids,
    cotangent,
):
    tp_place = lax.axis_index("tp")
    seq_place = lax.axis_index("seq")
    seq_size = lax.axis_size("seq")
    core = seq_place % 2
    tp_size = lax.axis_size("tp")
    gain_share = mixer_gain.shape[0]
    taps_n, width = conv_taps.shape
    rim_width = taps_n - 1
    length, model = tokens.shape
    group = length * tp_size
    blocks_n = rate_blocks.shape[0]

    in_t, branch_t = in_proj.T, branch_proj.T
    place = tp_place.astype(jnp.int32)[None]

    blocks = [tokens] + [swap(tokens, "tp", r) for r in range(1, tp_size)]
    blocks[1], gains, ids, rate_in, input_in, vec_in = tied(
        blocks[1],
        jnp.stack([mixer_gain, dense_gain]),
        segment_ids,
        rate_blocks,
        input_blocks,
        (conv_bias, rate_bias, input_bias, decay_param),
    )
    gains = gather_rows(gains)
    gains = gains.transpose(1, 0, 2).reshape(2, -1).astype(f32)
    mixer_scale, dense_scale = gains[0], gains[1]
    rim_ids = from_neighbour(ids[-rim_width:], -1)
    ext_ids = jnp.concatenate([rim_ids, ids])
    same = [ext_ids[rim_width - k : rim_width - k + group] == ids for k in range(1, taps_n)]
    masks = jnp.stack([same[0]] + same, axis=1).astype(f32)
    rate_dense = dense_blocks(rate_in)
    input_dense = dense_blocks(input_in)
    vecs = jnp.stack([*vec_in[:3], -8.0 * jax.nn.softplus(-vec_in[3])])
    *blocks, masks, rate_dense, input_dense, vecs = tied(*blocks, masks, rate_dense, input_dense, vecs)
    cot_all = lax.all_gather(cotangent, ("seq", "tp"), axis=0, tiled=True)

    normed, inner = norm_project(blocks, place, mixer_scale[None], in_t)
    rim = from_neighbour(inner[-1, -TILE:], -1)
    conv, conv_low, sig_rate, sig_input, keep_prefix, value_prefix, ends = recur_forward(
        inner, masks, rim, conv_taps, vecs, rate_dense, input_dense
    )
    ends, normed_b = tied(ends, normed)
    state_in = carry_in(ends[0, 0], ends[1, 0], False)
    branch_pre = project_t(normed_b, branch_t).reshape(inner.shape)
    state, mixed, mixer_part = mix_out(value_prefix, keep_prefix, branch_pre, state_in[None], out_proj)
    mixed = mixed.reshape(group, width)
    mixer_out = scatter_rows(mixer_part)
    mid = tokens.astype(f32) + mixer_out
    mid_root = rms(mid)
    xhat_dense = mid * mid_root
    normed_two = (xhat_dense * dense_scale).astype(bf16)

    chips = seq_size // 2
    same_core = [[core_no + 2 * i for i in range(chips)] for core_no in range(2)]
    rows_z = lax.all_gather(normed_two, "seq", axis=0, tiled=True, axis_index_groups=same_core)
    rows_two, cot_all = tied(gather_rows(normed_two).reshape(group, model), cot_all)
    hidden, normed_two_part = dense_rows(
        rows_two, cot_all, seq_place.astype(jnp.int32)[None], gate_proj, up_proj, down_proj
    )
    normed_two_grad = scatter_rows(normed_two_part.reshape(tp_size, length, model))
    dense_part = product(hidden, down_proj).astype(bf16)
    normed_two_grad, dense_part = tied(normed_two_grad, dense_part)
    mid_from_norm, dense_gain_part = norm_back(normed_two_grad, xhat_dense, dense_scale, mid_root)
    mid_grad = cotangent.astype(f32) + mid_from_norm
    mid_blocks = gather_rows(mid_grad.astype(bf16))
    mid_blocks, dense_part, rows_z = tied(mid_blocks, dense_part, rows_z)
    rows_spread = spread(rows_z)

    direct, branch_pre_grad, reach = mix_back(mid_blocks, out_proj, branch_pre, state, keep_prefix)
    branch_pre_grad = branch_pre_grad.reshape(group, width)
    mid_rows = mid_blocks.reshape(group, model)
    reach, direct, branch_pre_grad, mid_rows = tied(reach[0], direct, branch_pre_grad, mid_rows)
    after = carry_in(ends[0, 0], reach, True)
    out_full = product_left_t(mixed, mid_rows).astype(bf16)
    branch_full = product_left_t(branch_pre_grad, normed).astype(bf16)
    after, pair_full = tied(after, jnp.concatenate([out_full, branch_full]))
    pair_part = lax.psum_scatter(pair_full, "seq", scatter_dimension=0, tiled=True)
    tile = lambda v: jnp.broadcast_to(v, (TILE, width))
    rate_low, input_low, inner_grad, tail, rim_grad, sums = recur_backward(
        direct,
        state,
        conv,
        sig_rate,
        sig_input,
        inner,
        masks,
        rim,
        tile(state_in),
        tile(after),
        conv_taps,
        vecs,
        rate_dense,
        input_dense,
    )
    rows_mine, rim_grad = rows_spread(rim_grad)
    fixed = tail + from_neighbour(rim_grad, 1)
    low_rows = conv_low.reshape(group, width)
    rate_w = diagonal_blocks(product_left_t(low_rows, rate_low.reshape(group, width)), blocks_n)
    input_w = diagonal_blocks(product_left_t(low_rows, input_low.reshape(group, width)), blocks_n)
    inner_grad = lax.dynamic_update_slice(
        inner_grad, fixed.astype(bf16)[None], (tp_size - 1, length - TILE, 0)
    ).reshape(group, width)
    in_full = product_left_t(inner_grad, normed).astype(bf16)
    block_full = jnp.concatenate([rate_w, input_w]).astype(bf16)
    block_sum = block_full + swap(block_full, "seq", 1)
    normed_part = (product(inner_grad, in_t) + product(branch_pre_grad, branch_t)).astype(bf16)
    rows_theirs = swap(rows_mine, "seq", 1)
    normed_part, in_full, pair_part, rows_mine, rows_theirs, block_sum, dense_part = tied(
        normed_part, in_full, pair_part, rows_mine, rows_theirs, block_sum, dense_part
    )
    pair_sum = lax.all_gather(pair_part, "seq", axis=0, tiled=True)
    in_part = lax.psum_scatter(in_full, "seq", scatter_dimension=0, tiled=True)
    split = lambda rows: rows.reshape(tp_size, length, model)
    grad_and_out = scatter_rows(jnp.concatenate([split(normed_part), split(dense_part)], axis=1))
    block_other = swap(block_sum, "seq", 2)

    places = jnp.stack([core, tp_place]).astype(jnp.int32)
    blocked = lambda rows: rows.reshape(tp_size, chips, length, model)
    gate_w, up_w, down_w = dense_weight_grads(
        blocked(rows_mine), blocked(rows_theirs), cot_all, gate_proj, up_proj, down_proj, places
    )
    gate_w, up_w, down_w, in_part, grad_and_out, block_other = tied(
        gate_w, up_w, down_w, in_part, grad_and_out, block_other
    )
    normed_grad, dense_out = grad_and_out[:length], grad_and_out[length:]
    block_sum = block_sum + block_other
    bit = 4
    while bit < seq_size:
        block_sum = block_sum + swap(block_sum, "seq", bit)
        bit *= 2
    in_sum = lax.all_gather(in_part, "seq", axis=0, tiled=True)
    halves = [(gate_w, swap(gate_w, "seq", 1), 1), (up_w, swap(up_w, "seq", 1), 1), (down_w, swap(down_w, "seq", 1), 0)]
    output = (mid + dense_out).astype(bf16)
    own = tokens.astype(f32)
    own_root = rms(own)
    rows_grad, mixer_gain_part = norm_back(normed_grad, own * own_root, mixer_scale, own_root)
    tokens_grad = mid_grad + rows_grad
    out_sum, branch_sum = pair_sum[:width].astype(f32), pair_sum[width:].astype(f32)

    small = jnp.stack([mixer_gain_part, dense_gain_part])
    whole = []
    for axis, size in (("tp", tp_size), ("seq", seq_size)):
        if axis == "seq":
            gain_own = lax.dynamic_slice_in_dim(small, tp_place * gain_share, gain_share, 1)
            wide = max(width, gain_share)
            fit = lambda v: jnp.pad(v, ((0, 0), (0, wide - v.shape[1])))
            small = jnp.concatenate([fit(sums), fit(gain_own)])
        bit = 1
        while bit < size:
            other = swap(small, axis, bit)
            if halves:
                mine, theirs, along = halves.pop(0)
                made, other = tied(joined(mine, theirs, places, along), other)
                whole.append(made)
            small = small + other
            bit *= 2
    gate_sum, up_sum, down_sum = whole
    sums, gain_sum = small[:-2, :width], small[-2:, :gain_share]
    decay_sum = 8.0 * jax.nn.sigmoid(-decay_param) * sums[2]
    rate_sum, input_sum = block_sum[:blocks_n].astype(f32), block_sum[blocks_n:].astype(f32)
    return (
        output,
        tokens_grad,
        gain_sum[0],
        in_sum.astype(f32).T,
        branch_sum.astype(f32).T,
        sums[4 : 4 + taps_n],
        sums[3],
        rate_sum,
        sums[0],
        input_sum,
        sums[1],
        decay_sum,
        out_sum.astype(f32),
        gain_sum[1],
        gate_sum,
        up_sum,
        down_sum,
    )


def solution(mesh):
    return jax.shard_map(
        shards,
        mesh=mesh,
        in_specs=(
            P(("seq", "tp"), None),
            P("tp"),
            P(None, "tp"),
            P(None, "tp"),
            P(None, "tp"),
            P("tp"),
            P("tp", None, None),
            P("tp"),
            P("tp", None, None),
            P("tp"),
            P("tp"),
            P("tp", None),
            P("tp"),
            P(None, "tp"),
            P(None, "tp"),
            P("tp", None),
            P("seq"),
            P(("seq", "tp"), None),
        ),
        out_specs=(
            P(("seq", "tp"), None),
            P(("seq", "tp"), None),
            P("tp"),
            P(None, "tp"),
            P(None, "tp"),
            P(None, "tp"),
            P("tp"),
            P("tp", None, None),
            P("tp"),
            P("tp", None, None),
            P("tp"),
            P("tp"),
            P("tp", None),
            P("tp"),
            P(None, "tp"),
            P(None, "tp"),
            P("tp", None),
        ),
        check_vma=False,
    )
```

```python
import math

import jax
import jax.numpy as jnp
from jax import lax
from jax.experimental import pallas as pl
from jax.experimental.pallas import tpu as pltpu
from jax.sharding import PartitionSpec as P

epsilon = 1e-06
f32 = jnp.float32
bf16 = jnp.bfloat16
TILE = 8
VMEM_LIMIT = 50 * 1024 * 1024


def product(left, right):
    return jnp.dot(left, right, preferred_element_type=f32)


def product_left_t(left, right):
    return lax.dot_general(left, right, (((0,), (0,)), ((), ())), preferred_element_type=f32)


def product_right_t(left, right):
    return lax.dot_general(left, right, (((1,), (1,)), ((), ())), preferred_element_type=f32)


def gelu_tanh(values):
    return jax.nn.gelu(values, approximate=True)


def tied(*values):
    return lax.optimization_barrier(values)


def swap(value, axis, bit):
    count = lax.axis_size(axis)
    return lax.ppermute(value, axis, [(i, i ^ bit) for i in range(count)])


def gather_rows(rows):
    count = lax.axis_size("tp")
    place = lax.axis_index("tp")
    whole = jnp.zeros((count,) + rows.shape, rows.dtype)
    for r in range(count):
        block = rows if r == 0 else swap(rows, "tp", r)
        whole = lax.dynamic_update_index_in_dim(whole, block, place ^ r, 0)
    return whole


def spread(rows):
    count = lax.axis_size("tp")
    if count != 4:
        whole = jnp.stack([rows] + [swap(rows, "tp", r) for r in range(1, count)])
        return lambda *after: tied(whole, *after)
    half = rows.shape[0] // 2
    sides = swap(rows, "tp", 1), swap(rows, "tp", 2)

    def finish(*after):
        one, two, *after = tied(*sides, *after)
        far = jnp.concatenate([swap(two[:half], "tp", 1), swap(one[half:], "tp", 2)])
        return (jnp.stack([rows, one, two, far]), *after)

    return finish


def scatter_rows(blocks):
    place = lax.axis_index("tp")
    block = lambda r: lax.dynamic_index_in_dim(blocks, place ^ r, 0, False)
    total = block(0).astype(f32)
    for r in range(1, lax.axis_size("tp")):
        total = total + swap(block(r), "tp", r).astype(f32)
    return total


def carry_in(keep_total, value_total, backward):
    place = lax.axis_index("seq")
    total = jnp.stack([keep_total, value_total])
    before = jnp.stack([jnp.ones_like(keep_total), jnp.zeros_like(value_total)])
    bit = 1
    while bit < lax.axis_size("seq"):
        other = swap(total, "seq", bit)
        upper = (place & bit) != 0
        earlier = jnp.logical_not(upper) if backward else upper
        joined_before = jnp.stack([other[0] * before[0], before[0] * other[1] + before[1]])
        before = jnp.where(earlier, joined_before, before)
        first = jnp.where(earlier, other, total)
        second = jnp.where(earlier, total, other)
        total = jnp.stack([first[0] * second[0], second[0] * first[1] + second[1]])
        bit *= 2
    return before[1]


def from_neighbour(value, step):
    count = lax.axis_size("seq")
    place = lax.axis_index("seq")
    inside = lax.ppermute(value, "seq", [(i, i ^ 1) for i in range(count)])
    pairs = [(i, i + 1) for i in range(1, count - 1, 2)] + [(i + 1, i) for i in range(1, count - 1, 2)]
    across = lax.ppermute(value, "seq", pairs)
    return jnp.where((place % 2 == 0) == (step == 1), inside, across)


def sum_bits(value, axis):
    bit = 1
    while bit < lax.axis_size(axis):
        value = value + swap(value, axis, bit)
        bit *= 2
    return value


def both_halves(mine, theirs, core):
    first = jnp.where(core == 0, mine, theirs)
    second = jnp.where(core == 0, theirs, mine)
    return first, second


def gelu_grads(gate_pre, up_pre, hidden_grad):
    square = gate_pre * gate_pre
    inner = math.sqrt(2.0 / math.pi) * gate_pre * (1.0 + 0.044715 * square)
    half = 0.5 * (1.0 + jnp.tanh(inner))
    act = gate_pre * half
    slope = half + 2.0 * math.sqrt(2.0 / math.pi) * act * (1.0 - half) * (1.0 + 3.0 * 0.044715 * square)
    return act * up_pre, hidden_grad * up_pre * slope, hidden_grad * act


def dense_weight_grads(mine, theirs, cot_all, gate_proj, up_proj, down_proj, places):
    tp_size, chips, block, model = mine.shape
    half = gate_proj.shape[1] // 2
    cot_all = cot_all.reshape(chips, 2, tp_size, block, model)
    part = math.gcd(chips, 4)
    length = part * block
    per_core = tp_size * chips // part
    steps, outs = 2 * per_core, 4
    tile = math.gcd(half, 256)
    left_t = (((0,), (0,)), ((), ()))
    right_t = (((1,), (1,)), ((), ()))

    def kernel(core_ref, mine_ref, theirs_ref, cot_ref, gate_ref, up_ref, down_ref, *rest):
        gate_out, up_out, down_out, acc_g, acc_u, acc_d, hid, gg, ug, x_ref = rest
        i = pl.program_id(0)

        @pl.when(i < per_core)
        def _():
            x_ref[...] = mine_ref[...].reshape(length, model)

        @pl.when(jnp.logical_and(i >= per_core, i < steps))
        def _():
            x_ref[...] = theirs_ref[...].reshape(length, model)

        @pl.when(i == 0)
        def _():
            acc_g[...] = jnp.zeros_like(acc_g)
            acc_u[...] = jnp.zeros_like(acc_u)
            acc_d[...] = jnp.zeros_like(acc_d)

        @pl.when(i < steps)
        def _():
            cots = cot_ref[...].reshape(length, model)
            for n in range(half // tile):
                cols = slice(n * tile, (n + 1) * tile)
                gate_pre = jnp.dot(x_ref[...], gate_ref[:, cols], preferred_element_type=f32)
                up_pre = jnp.dot(x_ref[...], up_ref[:, cols], preferred_element_type=f32)
                hidden_grad = lax.dot_general(cots, down_ref[cols, :], right_t, preferred_element_type=f32)
                a, b, c = gelu_grads(gate_pre, up_pre, hidden_grad)
                hid[:, cols] = a.astype(bf16)
                gg[:, cols] = b.astype(bf16)
                ug[:, cols] = c.astype(bf16)
            acc_g[...] += lax.dot_general(x_ref[...], gg[...], left_t, preferred_element_type=f32)
            acc_u[...] += lax.dot_general(x_ref[...], ug[...], left_t, preferred_element_type=f32)
            acc_d[...] += lax.dot_general(hid[...], cots, left_t, preferred_element_type=f32)

        @pl.when(i >= steps)
        def _():
            wide = pl.ds(pl.multiple_of((i - steps) * (model // outs), model // outs), model // outs)
            low = pl.ds(pl.multiple_of((i - steps) * (half // outs), half // outs), half // outs)
            gate_out[...] = acc_g[wide, :].astype(bf16)
            up_out[...] = acc_u[wide, :].astype(bf16)
            down_out[...] = acc_d[low, :].astype(bf16)

    once = pl.Buffered(1)
    groups = chips // part
    out_index = lambda i, c: (jnp.maximum(i - steps, 0), 0)

    def cot_index(i, c):
        i = jnp.minimum(i, steps - 1)
        n = i % per_core
        return n % groups, c[0] ^ (i // per_core), c[1] ^ (n // groups), 0, 0

    def rows_index(first):
        def index(i, c):
            n = jnp.clip(i - first, 0, per_core - 1)
            return n // groups, n % groups, 0, 0

        return pl.BlockSpec((1, part, block, model), index)

    return pl.pallas_call(
        kernel,
        grid_spec=pltpu.PrefetchScalarGridSpec(
            num_scalar_prefetch=1,
            grid=(steps + outs,),
            in_specs=[
                rows_index(0),
                rows_index(per_core),
                pl.BlockSpec((part, 1, 1, block, model), cot_index),
                pl.BlockSpec((model, half), lambda i, c: (0, c[0]), pipeline_mode=once),
                pl.BlockSpec((model, half), lambda i, c: (0, c[0]), pipeline_mode=once),
                pl.BlockSpec((half, model), lambda i, c: (c[0], 0), pipeline_mode=once),
            ],
            out_specs=[
                pl.BlockSpec((model // outs, half), out_index),
                pl.BlockSpec((model // outs, half), out_index),
                pl.BlockSpec((half // outs, model), out_index),
            ],
            scratch_shapes=[
                pltpu.VMEM((model, half), f32),
                pltpu.VMEM((model, half), f32),
                pltpu.VMEM((half, model), f32),
                pltpu.VMEM((length, half), bf16),
                pltpu.VMEM((length, half), bf16),
                pltpu.VMEM((length, half), bf16),
                pltpu.VMEM((length, model), bf16),
            ],
        ),
        out_shape=[
            jax.ShapeDtypeStruct((model, half), bf16),
            jax.ShapeDtypeStruct((model, half), bf16),
            jax.ShapeDtypeStruct((half, model), bf16),
        ],
        compiler_params=pltpu.CompilerParams(vmem_limit_bytes=60 * 1024 * 1024),
        cost_estimate=pl.CostEstimate(flops=1000, bytes_accessed=1000, transcendentals=0),
        name="dense_weight_grads",
    )(places, mine, theirs, cot_all, gate_proj, up_proj, down_proj)


def joined(mine, theirs, core, axis):
    rows, cols = mine.shape
    block = math.gcd(rows, 256)
    steps = rows // block

    def kernel(core_ref, mine_ref, theirs_ref, out_ref):
        for low in range(2):

            @pl.when(core_ref[0] == low)
            def _(low=low):
                pair = (mine_ref, theirs_ref) if low == 0 else (theirs_ref, mine_ref)
                if axis == 1:
                    out_ref[:, :cols] = pair[0][...].astype(f32)
                    out_ref[:, cols:] = pair[1][...].astype(f32)
                else:
                    out_ref[0] = pair[0][...].astype(f32)
                    out_ref[1] = pair[1][...].astype(f32)

    half = pl.BlockSpec((block, cols), lambda i, c: (i, 0))
    if axis == 1:
        out_spec = pl.BlockSpec((block, 2 * cols), lambda i, c: (i, 0))
        out_shape = jax.ShapeDtypeStruct((rows, 2 * cols), f32)
    else:
        out_spec = pl.BlockSpec((2, block, cols), lambda i, c: (0, i, 0))
        out_shape = jax.ShapeDtypeStruct((2, rows, cols), f32)
    out = pl.pallas_call(
        kernel,
        grid_spec=pltpu.PrefetchScalarGridSpec(
            num_scalar_prefetch=1, grid=(steps,), in_specs=[half, half], out_specs=out_spec
        ),
        out_shape=out_shape,
        compiler_params=pltpu.CompilerParams(vmem_limit_bytes=VMEM_LIMIT),
        cost_estimate=pl.CostEstimate(flops=0, bytes_accessed=12 * rows * cols, transcendentals=0),
        name="joined",
    )(core, mine, theirs)
    return out if axis == 1 else out.reshape(2 * rows, cols)


def dense_rows(rows, cot_all, group_place, gate_proj, up_proj, down_proj):
    length, model = rows.shape
    width = gate_proj.shape[1]
    tile = math.gcd(width, 256)
    out_tile = math.gcd(model, 256)
    first, second = width // tile, model // out_tile
    right_t = (((1,), (1,)), ((), ()))

    def kernel(place_ref, x_ref, c_ref, gate_ref, up_ref, down_ref, hidden_ref, grad_ref, gates, ups, gate_grads, up_grads):
        j = pl.program_id(0)

        @pl.when(j < first)
        def _():
            gate_pre = jnp.dot(x_ref[...], gate_ref[...], preferred_element_type=f32)
            up_pre = jnp.dot(x_ref[...], up_ref[...], preferred_element_type=f32)
            hidden_grad = lax.dot_general(c_ref[...], down_ref[...], right_t, preferred_element_type=f32)
            hidden, gate_grad, up_grad = gelu_grads(gate_pre, up_pre, hidden_grad)
            hidden_ref[...] = hidden.astype(bf16)
            at = pl.ds(pl.multiple_of(j * tile, tile), tile)
            gates[:, at] = gate_ref[...]
            ups[:, at] = up_ref[...]
            gate_grads[:, at] = gate_grad.astype(bf16)
            up_grads[:, at] = up_grad.astype(bf16)

        @pl.when(j >= first)
        def _():
            at = pl.ds(pl.multiple_of((j - first) * out_tile, out_tile), out_tile)
            part = lax.dot_general(gate_grads[...], gates[at, :], right_t, preferred_element_type=f32)
            part = part + lax.dot_general(up_grads[...], ups[at, :], right_t, preferred_element_type=f32)
            grad_ref[...] = part.astype(bf16)

    clamp = lambda j: jnp.minimum(j, first - 1)
    wide = pl.BlockSpec((model, tile), lambda j, p: (0, clamp(j)))
    return pl.pallas_call(
        kernel,
        grid_spec=pltpu.PrefetchScalarGridSpec(
            num_scalar_prefetch=1,
            grid=(first + second,),
            in_specs=[
                pl.BlockSpec((length, model), lambda j, p: (0, 0)),
                pl.BlockSpec((length, model), lambda j, p: (p[0], 0)),
                wide,
                wide,
                pl.BlockSpec((tile, model), lambda j, p: (clamp(j), 0)),
            ],
            out_specs=[
                pl.BlockSpec((length, tile), lambda j, p: (0, clamp(j))),
                pl.BlockSpec((length, out_tile), lambda j, p: (0, jnp.maximum(j - first, 0))),
            ],
            scratch_shapes=[
                pltpu.VMEM((model, width), bf16),
                pltpu.VMEM((model, width), bf16),
                pltpu.VMEM((length, width), bf16),
                pltpu.VMEM((length, width), bf16),
            ],
        ),
        out_shape=[
            jax.ShapeDtypeStruct((length, width), bf16),
            jax.ShapeDtypeStruct((length, model), bf16),
        ],
        compiler_params=pltpu.CompilerParams(vmem_limit_bytes=VMEM_LIMIT),
        name="dense_rows",
    )(group_place, rows, cot_all, gate_proj, up_proj, down_proj)


def project_t(rows, weight_t):
    total, model = rows.shape
    width = weight_t.shape[0]
    length = math.gcd(total, 256)

    def kernel(rows_ref, weight_ref, out_ref):
        out_ref[...] = lax.dot_general(
            rows_ref[...], weight_ref[...], (((1,), (1,)), ((), ())), preferred_element_type=f32
        )

    return pl.pallas_call(
        kernel,
        grid=(total // length,),
        in_specs=[
            pl.BlockSpec((length, model), lambda j: (j, 0)),
            pl.BlockSpec((width, model), lambda j: (0, 0)),
        ],
        out_specs=pl.BlockSpec((length, width), lambda j: (j, 0)),
        out_shape=jax.ShapeDtypeStruct((total, width), f32),
        compiler_params=pltpu.CompilerParams(vmem_limit_bytes=VMEM_LIMIT),
        name="project_t",
    )(rows, weight_t)


def mix_out(value_prefix, keep_prefix, branch_pre, state_in, out_proj):
    blocks, length, width = value_prefix.shape
    model = out_proj.shape[1]

    def kernel(value_ref, keep_ref, branch_ref, in_ref, out_ref, state_ref, mixed_ref, part_ref):
        state = value_ref[0] + keep_ref[0] * in_ref[...]
        state_ref[0] = state
        mixed = (state * gelu_tanh(branch_ref[0])).astype(bf16)
        mixed_ref[0] = mixed
        part_ref[0] = jnp.dot(mixed, out_ref[...], preferred_element_type=f32).astype(bf16)

    block = pl.BlockSpec((1, length, width), lambda j: (j, 0, 0))
    whole = lambda *shape: pl.BlockSpec(shape, lambda j: (0,) * len(shape))
    return pl.pallas_call(
        kernel,
        grid=(blocks,),
        in_specs=[block, block, block, whole(1, width), whole(width, model)],
        out_specs=[block, block, pl.BlockSpec((1, length, model), lambda j: (j, 0, 0))],
        out_shape=[
            jax.ShapeDtypeStruct((blocks, length, width), f32),
            jax.ShapeDtypeStruct((blocks, length, width), bf16),
            jax.ShapeDtypeStruct((blocks, length, model), bf16),
        ],
        compiler_params=pltpu.CompilerParams(vmem_limit_bytes=VMEM_LIMIT),
        name="mix_out",
    )(value_prefix, keep_prefix, branch_pre, state_in, out_proj)


def mix_back(mid_rows, out_proj, branch_pre, state, keep_prefix):
    blocks, length, width = state.shape
    model = out_proj.shape[1]
    tiles = length // 16

    def kernel(mid_ref, out_ref, branch_ref, state_ref, keep_ref, direct_ref, branch_grad_ref, reach_ref, mixed, acc):
        j = pl.program_id(0)
        mixed[...] = lax.dot_general(
            mid_ref[0], out_ref[...], (((1,), (1,)), ((), ())), preferred_element_type=f32
        )

        @pl.when(j == 0)
        def _():
            acc[...] = jnp.zeros_like(acc)

        def tile(i, total):
            at = pl.ds(pl.multiple_of(i * 16, 16), 16)
            grad = mixed[at, :]
            pre = branch_ref[0, at, :]
            square = pre * pre
            inner = math.sqrt(2.0 / math.pi) * pre * (1.0 + 0.044715 * square)
            half = 0.5 * (1.0 + jnp.tanh(inner))
            act = pre * half
            slope = half + 2.0 * math.sqrt(2.0 / math.pi) * act * (1.0 - half) * (1.0 + 3.0 * 0.044715 * square)
            direct = grad * act
            direct_ref[0, at, :] = direct
            branch_grad_ref[0, at, :] = (grad * state_ref[0, at, :] * slope).astype(bf16)
            return total + direct * keep_ref[0, at, :]

        acc[...] = lax.fori_loop(0, tiles, tile, acc[...])

        @pl.when(j == blocks - 1)
        def _():
            reach_ref[...] = jnp.sum(acc[...], axis=0, keepdims=True)

    block = pl.BlockSpec((1, length, width), lambda j: (j, 0, 0))
    whole = lambda *shape: pl.BlockSpec(shape, lambda j: (0,) * len(shape))
    return pl.pallas_call(
        kernel,
        grid=(blocks,),
        in_specs=[pl.BlockSpec((1, length, model), lambda j: (j, 0, 0)), whole(width, model), block, block, block],
        out_specs=[block, block, whole(1, width)],
        out_shape=[
            jax.ShapeDtypeStruct((blocks, length, width), f32),
            jax.ShapeDtypeStruct((blocks, length, width), bf16),
            jax.ShapeDtypeStruct((1, width), f32),
        ],
        scratch_shapes=[pltpu.VMEM((length, width), f32), pltpu.VMEM((16, width), f32)],
        compiler_params=pltpu.CompilerParams(vmem_limit_bytes=VMEM_LIMIT),
        name="mix_back",
    )(mid_rows, out_proj, branch_pre, state, keep_prefix)


def minus_expm1(x):
    series = 1.0 / 40320.0
    for term in (1.0 / 5040.0, 1.0 / 720.0, 1.0 / 120.0, 1.0 / 24.0, 1.0 / 6.0, 0.5, 1.0):
        series = series * x + term
    return jnp.where(x > -0.35, -x * series, 1.0 - jnp.exp(x))


def rows_of(shape):
    return lax.broadcasted_iota(jnp.int32, shape, 0)


def down(cur, prev, by, row):
    return jnp.where(row >= by, pltpu.roll(cur, by, 0), pltpu.roll(prev, by, 0))


def up(cur, after, by, row):
    return jnp.where(row < TILE - by, pltpu.roll(cur, TILE - by, 0), pltpu.roll(after, TILE - by, 0))


def last_row(tile):
    return jnp.broadcast_to(tile[TILE - 1 :, :], tile.shape)


def first_row(tile):
    return jnp.broadcast_to(tile[:1, :], tile.shape)


def forward_kernel(
    inner_ref,
    mask_ref,
    rim_ref,
    taps_ref,
    vec_ref,
    rate_ref,
    input_ref,
    conv_ref,
    low_ref,
    sig_rate_ref,
    sig_input_ref,
    keep_ref,
    value_ref,
    end_ref,
    prev_ref,
    carry_ref,
    rate_raw_ref,
    input_raw_ref,
):
    step = pl.program_id(0)
    length, width = inner_ref.shape[1:]
    tiles = length // TILE
    taps_n = taps_ref.shape[0]

    @pl.when(step == 0)
    def _():
        prev_ref[...] = rim_ref[...]
        carry_ref[0] = jnp.ones((TILE, width), f32)
        carry_ref[1] = jnp.zeros((TILE, width), f32)

    row = rows_of((TILE, width))

    def conv_tile(i, prev):
        at = pl.ds(pl.multiple_of(i * TILE, TILE), TILE)
        cur = inner_ref[0, at, :]
        masks = mask_ref[at, :]
        total = vec_ref[0:1, :] + taps_ref[0:1, :] * cur
        for k in range(1, taps_n):
            total = total + taps_ref[k : k + 1, :] * (down(cur, prev, k, row) * masks[:, k : k + 1])
        conv_ref[0, at, :] = total
        return cur

    prev_ref[...] = lax.fori_loop(0, tiles, conv_tile, prev_ref[...])
    low = conv_ref[0].astype(bf16)
    low_ref[0] = low
    rate_raw_ref[...] = jnp.dot(low, rate_ref[...], preferred_element_type=f32)
    input_raw_ref[...] = jnp.dot(low, input_ref[...], preferred_element_type=f32)

    def gate_tile(i, carry):
        keep_in, value_in = carry
        at = pl.ds(pl.multiple_of(i * TILE, TILE), TILE)
        sig_rate = jax.nn.sigmoid(rate_raw_ref[at, :] + vec_ref[1:2, :])
        sig_input = jax.nn.sigmoid(input_raw_ref[at, :] + vec_ref[2:3, :])
        sig_rate_ref[0, at, :] = sig_rate
        sig_input_ref[0, at, :] = sig_input
        log_decay = sig_rate * vec_ref[3:4, :]
        a = jnp.exp(log_decay) * mask_ref[at, 0:1]
        b = jnp.sqrt(minus_expm1(2.0 * log_decay)) * sig_input * conv_ref[0, at, :]
        for d in (1, 2, 4):
            a_before = jnp.where(row >= d, pltpu.roll(a, d, 0), 1.0)
            b_before = jnp.where(row >= d, pltpu.roll(b, d, 0), 0.0)
            b = b + a * b_before
            a = a * a_before
        b = b + a * value_in
        a = a * keep_in
        keep_ref[0, at, :] = a
        value_ref[0, at, :] = b
        return last_row(a), last_row(b)

    keep_end, value_end = lax.fori_loop(0, tiles, gate_tile, (carry_ref[0], carry_ref[1]))
    carry_ref[0] = keep_end
    carry_ref[1] = value_end
    end_ref[0] = keep_end
    end_ref[1] = value_end


def backward_kernel(
    direct_ref,
    state_ref,
    state_prev_ref,
    conv_ref,
    sig_rate_ref,
    sig_input_ref,
    inner_ref,
    inner_prev_ref,
    mask_ref,
    rim_ref,
    state_in_ref,
    after_ref,
    taps_ref,
    vec_ref,
    rate_ref,
    input_ref,
    rate_grad_ref,
    input_grad_ref,
    inner_grad_ref,
    tail_ref,
    rim_grad_ref,
    sums_ref,
    carry_ref,
    next_ref,
    acc_ref,
    rate_f_ref,
    input_f_ref,
    conv_f_ref,
):
    step = pl.program_id(0)
    steps = pl.num_programs(0)
    length, width = direct_ref.shape[1:]
    tiles = length // TILE
    taps_n = taps_ref.shape[0]
    row = rows_of((TILE, width))
    is_first_block = step == steps - 1

    @pl.when(step == 0)
    def _():
        carry_ref[...] = after_ref[...]
        next_ref[...] = jnp.zeros_like(next_ref)
        acc_ref[...] = jnp.zeros_like(acc_ref)

    edge_state = jnp.where(is_first_block, state_in_ref[...], state_prev_ref[0])
    edge_inner = jnp.where(is_first_block, rim_ref[...], inner_prev_ref[0])
    neg_rate = vec_ref[3:4, :]

    def gate_tile(n, carry):
        after, acc_rate, acc_input, acc_decay = carry
        i = tiles - 1 - n
        at = pl.ds(pl.multiple_of(i * TILE, TILE), TILE)
        before = pl.ds(pl.multiple_of(jnp.maximum(i - 1, 0) * TILE, TILE), TILE)
        direct = direct_ref[0, at, :]
        sig_rate = sig_rate_ref[0, at, :]
        sig_input = sig_input_ref[0, at, :]
        conv = conv_ref[0, at, :]
        log_decay = sig_rate * neg_rate
        decay = jnp.exp(log_decay)
        keep = decay * mask_ref[at, 0:1]
        room = minus_expm1(2.0 * log_decay)
        root = jnp.sqrt(room)
        a = keep
        b = keep * direct
        for d in (1, 2, 4):
            a_after = jnp.where(row < TILE - d, pltpu.roll(a, TILE - d, 0), 1.0)
            b_after = jnp.where(row < TILE - d, pltpu.roll(b, TILE - d, 0), 0.0)
            b = b + a * b_after
            a = a * a_after
        reach = b + a * after
        grad = direct + up(reach, after, 1, row)
        prev_tile = jnp.where(i == 0, edge_state, state_ref[0, before, :])
        state_prev = down(state_ref[0, at, :], prev_tile, 1, row)
        grad_root = grad * root
        gated = grad_root * sig_input
        decay_grad = grad * (keep * state_prev - sig_input * conv * (decay * decay) / root)
        rate_grad = decay_grad * neg_rate * (sig_rate * (1.0 - sig_rate))
        input_grad = gated * conv * (1.0 - sig_input)
        rate_f_ref[at, :] = rate_grad
        input_f_ref[at, :] = input_grad
        conv_f_ref[at, :] = gated
        return (
            first_row(reach),
            acc_rate + rate_grad,
            acc_input + input_grad,
            acc_decay + decay_grad * sig_rate,
        )

    after, acc_rate, acc_input, acc_decay = lax.fori_loop(
        0, tiles, gate_tile, (carry_ref[...], acc_ref[0], acc_ref[1], acc_ref[2])
    )
    carry_ref[...] = after
    acc_ref[0] = acc_rate
    acc_ref[1] = acc_input
    acc_ref[2] = acc_decay
    rate_low = rate_f_ref[...].astype(bf16)
    input_low = input_f_ref[...].astype(bf16)
    rate_grad_ref[0] = rate_low
    input_grad_ref[0] = input_low
    right_t = (((1,), (1,)), ((), ()))
    conv_f_ref[...] += lax.dot_general(
        rate_low, rate_ref[...], right_t, preferred_element_type=f32
    ) + lax.dot_general(input_low, input_ref[...], right_t, preferred_element_type=f32)

    def conv_tile(n, carry):
        acc_bias, acc_taps, nexts = carry
        i = tiles - 1 - n
        at = pl.ds(pl.multiple_of(i * TILE, TILE), TILE)
        before = pl.ds(pl.multiple_of(jnp.maximum(i - 1, 0) * TILE, TILE), TILE)
        grad = conv_f_ref[at, :]
        masks = mask_ref[at, :]
        cur = inner_ref[0, at, :]
        prev = jnp.where(i == 0, edge_inner, inner_ref[0, before, :])
        total = grad * taps_ref[0:1, :]
        new_taps = [acc_taps[0] + grad * cur]
        new_nexts = []
        for k in range(1, taps_n):
            masked = grad * masks[:, k : k + 1]
            part = masked * taps_ref[k : k + 1, :]
            total = total + up(part, nexts[k - 1], k, row)
            new_taps.append(acc_taps[k] + masked * down(cur, prev, k, row))
            new_nexts.append(part)
        rate_f_ref[at, :] = total
        return acc_bias + grad, tuple(new_taps), tuple(new_nexts)

    acc_bias, acc_taps, nexts = lax.fori_loop(
        0,
        tiles,
        conv_tile,
        (
            acc_ref[3],
            tuple(acc_ref[4 + k] for k in range(taps_n)),
            tuple(next_ref[k] for k in range(taps_n - 1)),
        ),
    )
    acc_ref[3] = acc_bias
    for k in range(taps_n):
        acc_ref[4 + k] = acc_taps[k]
    for k in range(taps_n - 1):
        next_ref[k] = nexts[k]
    inner_grad_ref[0] = rate_f_ref[...].astype(bf16)

    @pl.when(step == 0)
    def _():
        tail_ref[...] = rate_f_ref[length - TILE :, :]

    @pl.when(is_first_block)
    def _():
        zero = jnp.zeros((TILE, width), f32)
        total = zero
        for k in range(1, taps_n):
            total = total + up(zero, nexts[k - 1], k, row)
        rim_grad_ref[...] = total
        sums_ref[...] = jnp.sum(acc_ref[...], axis=1)


def norm_project(blocks, place, gain, weight_t):
    count = len(blocks)
    length, model = blocks[0].shape
    width = weight_t.shape[0]

    def kernel(place_ref, *refs):
        ins, gain_ref, weight_ref, normed_ref, out_ref = refs[:count], *refs[count:]
        j = pl.program_id(0)
        for r in range(count):

            @pl.when((j ^ place_ref[0]) == r)
            def _(source=ins[r]):
                x = source[...].astype(f32)
                root = lax.rsqrt(jnp.mean(x * x, axis=-1, keepdims=True) + epsilon)
                normed_ref[...] = (x * root * gain_ref[...]).astype(bf16)

        out_ref[0] = lax.dot_general(
            normed_ref[...], weight_ref[...], (((1,), (1,)), ((), ())), preferred_element_type=f32
        )

    whole = lambda *shape: pl.BlockSpec(shape, lambda j, p: (0,) * len(shape))
    return pl.pallas_call(
        kernel,
        grid_spec=pltpu.PrefetchScalarGridSpec(
            num_scalar_prefetch=1,
            grid=(count,),
            in_specs=[whole(length, model)] * count + [whole(1, model), whole(width, model)],
            out_specs=[
                pl.BlockSpec((length, model), lambda j, p: (j, 0)),
                pl.BlockSpec((1, length, width), lambda j, p: (j, 0, 0)),
            ],
        ),
        out_shape=[
            jax.ShapeDtypeStruct((count * length, model), bf16),
            jax.ShapeDtypeStruct((count, length, width), f32),
        ],
        compiler_params=pltpu.CompilerParams(vmem_limit_bytes=VMEM_LIMIT),
        name="norm_project",
    )(place, *blocks, gain, weight_t)


def recur_forward(inner, masks, rim, taps, vecs, rate_dense, input_dense):
    blocks, length, width = inner.shape
    whole = lambda *shape: pl.BlockSpec(shape, lambda j: (0,) * len(shape))
    block = pl.BlockSpec((1, length, width), lambda j: (j, 0, 0))
    full = jax.ShapeDtypeStruct((blocks, length, width), f32)
    return pl.pallas_call(
        forward_kernel,
        grid_spec=pltpu.PrefetchScalarGridSpec(
            num_scalar_prefetch=0,
            grid=(blocks,),
            in_specs=[
                block,
                pl.BlockSpec((length, masks.shape[1]), lambda j: (j, 0)),
                whole(*rim.shape),
                whole(*taps.shape),
                whole(*vecs.shape),
                whole(*rate_dense.shape),
                whole(*input_dense.shape),
            ],
            out_specs=[block, block, block, block, block, block, whole(2, TILE, width)],
            scratch_shapes=[
                pltpu.VMEM((TILE, width), f32),
                pltpu.VMEM((2, TILE, width), f32),
                pltpu.VMEM((length, width), f32),
                pltpu.VMEM((length, width), f32),
            ],
        ),
        out_shape=[
            full,
            jax.ShapeDtypeStruct((blocks, length, width), bf16),
            full,
            full,
            full,
            full,
            jax.ShapeDtypeStruct((2, TILE, width), f32),
        ],
        compiler_params=pltpu.CompilerParams(vmem_limit_bytes=VMEM_LIMIT),
        name="recur_forward",
    )(inner, masks, rim, taps, vecs, rate_dense, input_dense)


def recur_backward(
    direct, state, conv, sig_rate, sig_input, inner, masks, rim, state_in, after, taps, vecs, rate_dense, input_dense
):
    blocks, length, width = inner.shape
    last = length // TILE - 1
    whole = lambda *shape: pl.BlockSpec(shape, lambda j: (0,) * len(shape))
    block = pl.BlockSpec((1, length, width), lambda j: (blocks - 1 - j, 0, 0))
    edge = pl.BlockSpec(
        (1, TILE, width), lambda j: (jnp.maximum(blocks - 2 - j, 0), last, 0)
    )
    low = jax.ShapeDtypeStruct((blocks, length, width), bf16)
    tile = jax.ShapeDtypeStruct((TILE, width), f32)
    count = 4 + taps.shape[0]
    return pl.pallas_call(
        backward_kernel,
        grid_spec=pltpu.PrefetchScalarGridSpec(
            num_scalar_prefetch=0,
            grid=(blocks,),
            in_specs=[
                block,
                block,
                edge,
                block,
                block,
                block,
                block,
                edge,
                pl.BlockSpec((length, masks.shape[1]), lambda j: (blocks - 1 - j, 0)),
                whole(*rim.shape),
                whole(*state_in.shape),
                whole(*after.shape),
                whole(*taps.shape),
                whole(*vecs.shape),
                whole(*rate_dense.shape),
                whole(*input_dense.shape),
            ],
            out_specs=[
                block,
                block,
                block,
                whole(TILE, width),
                whole(TILE, width),
                whole(count, width),
            ],
            scratch_shapes=[
                pltpu.VMEM((TILE, width), f32),
                pltpu.VMEM((taps.shape[0] - 1, TILE, width), f32),
                pltpu.VMEM((count, TILE, width), f32),
                pltpu.VMEM((length, width), f32),
                pltpu.VMEM((length, width), f32),
                pltpu.VMEM((length, width), f32),
            ],
        ),
        out_shape=[low, low, low, tile, tile, jax.ShapeDtypeStruct((count, width), f32)],
        compiler_params=pltpu.CompilerParams(vmem_limit_bytes=VMEM_LIMIT),
        cost_estimate=pl.CostEstimate(flops=1000, bytes_accessed=1000, transcendentals=0),
        name="recur_backward",
    )(
        direct,
        state,
        state,
        conv,
        sig_rate,
        sig_input,
        inner,
        inner,
        masks,
        rim,
        state_in,
        after,
        taps,
        vecs,
        rate_dense,
        input_dense,
    )


def dense_blocks(blocks):
    count, rows_in, cols_out = blocks.shape
    tall = blocks.reshape(count * rows_in, cols_out)
    wide = jnp.concatenate([tall] * count, axis=1)
    row = lax.broadcasted_iota(jnp.int32, wide.shape, 0) // rows_in
    col = lax.broadcasted_iota(jnp.int32, wide.shape, 1) // cols_out
    return jnp.where(row == col, wide, jnp.zeros_like(wide))


def diagonal_blocks(full, count):
    rows, cols = full.shape[0] // count, full.shape[1] // count
    return jnp.stack([full[i * rows : (i + 1) * rows, i * cols : (i + 1) * cols] for i in range(count)])


def rms(values):
    return lax.rsqrt(jnp.mean(values * values, axis=-1, keepdims=True) + epsilon)


def norm_back(grad, xhat, scale, root):
    e = grad * scale
    return root * (e - xhat * jnp.mean(e * xhat, axis=-1, keepdims=True)), jnp.sum(grad * xhat, axis=0)


def shards(
    tokens,
    mixer_gain,
    in_proj,
    branch_proj,
    conv_taps,
    conv_bias,
    rate_blocks,
    rate_bias,
    input_blocks,
    input_bias,
    decay_param,
    out_proj,
    dense_gain,
    gate_proj,
    up_proj,
    down_proj,
    segment_ids,
    cotangent,
):
    tp_place = lax.axis_index("tp")
    seq_place = lax.axis_index("seq")
    seq_size = lax.axis_size("seq")
    core = seq_place % 2
    tp_size = lax.axis_size("tp")
    gain_share = mixer_gain.shape[0]
    taps_n, width = conv_taps.shape
    rim_width = taps_n - 1
    length, model = tokens.shape
    group = length * tp_size
    blocks_n = rate_blocks.shape[0]

    in_t, branch_t = in_proj.T, branch_proj.T
    place = tp_place.astype(jnp.int32)[None]

    blocks = [tokens] + [swap(tokens, "tp", r) for r in range(1, tp_size)]
    blocks[1], gains, ids, rate_in, input_in, vec_in = tied(
        blocks[1],
        jnp.stack([mixer_gain, dense_gain]),
        segment_ids,
        rate_blocks,
        input_blocks,
        (conv_bias, rate_bias, input_bias, decay_param),
    )
    gains = gather_rows(gains)
    gains = gains.transpose(1, 0, 2).reshape(2, -1).astype(f32)
    mixer_scale, dense_scale = gains[0], gains[1]
    rim_ids = from_neighbour(ids[-rim_width:], -1)
    ext_ids = jnp.concatenate([rim_ids, ids])
    same = [ext_ids[rim_width - k : rim_width - k + group] == ids for k in range(1, taps_n)]
    masks = jnp.stack([same[0]] + same, axis=1).astype(f32)
    rate_dense = dense_blocks(rate_in)
    input_dense = dense_blocks(input_in)
    vecs = jnp.stack([*vec_in[:3], -8.0 * jax.nn.softplus(-vec_in[3])])
    *blocks, masks, rate_dense, input_dense, vecs = tied(*blocks, masks, rate_dense, input_dense, vecs)
    cot_all = lax.all_gather(cotangent, ("seq", "tp"), axis=0, tiled=True)

    normed, inner = norm_project(blocks, place, mixer_scale[None], in_t)
    rim = from_neighbour(inner[-1, -TILE:], -1)
    conv, conv_low, sig_rate, sig_input, keep_prefix, value_prefix, ends = recur_forward(
        inner, masks, rim, conv_taps, vecs, rate_dense, input_dense
    )
    ends, normed_b = tied(ends, normed)
    state_in = carry_in(ends[0, 0], ends[1, 0], False)
    branch_pre = project_t(normed_b, branch_t).reshape(inner.shape)
    state, mixed, mixer_part = mix_out(value_prefix, keep_prefix, branch_pre, state_in[None], out_proj)
    mixed = mixed.reshape(group, width)
    mixer_out = scatter_rows(mixer_part)
    mid = tokens.astype(f32) + mixer_out
    mid_root = rms(mid)
    xhat_dense = mid * mid_root
    normed_two = (xhat_dense * dense_scale).astype(bf16)

    chips = seq_size // 2
    same_core = [[core_no + 2 * i for i in range(chips)] for core_no in range(2)]
    rows_z = lax.all_gather(normed_two, "seq", axis=0, tiled=True, axis_index_groups=same_core)
    rows_two, cot_all = tied(gather_rows(normed_two).reshape(group, model), cot_all)
    hidden, normed_two_part = dense_rows(
        rows_two, cot_all, seq_place.astype(jnp.int32)[None], gate_proj, up_proj, down_proj
    )
    normed_two_grad = scatter_rows(normed_two_part.reshape(tp_size, length, model))
    dense_part = product(hidden, down_proj).astype(bf16)
    normed_two_grad, dense_part = tied(normed_two_grad, dense_part)
    mid_from_norm, dense_gain_part = norm_back(normed_two_grad, xhat_dense, dense_scale, mid_root)
    mid_grad = cotangent.astype(f32) + mid_from_norm
    mid_blocks = gather_rows(mid_grad.astype(bf16))
    mid_blocks, dense_part, rows_z = tied(mid_blocks, dense_part, rows_z)
    rows_spread = spread(rows_z)

    direct, branch_pre_grad, reach = mix_back(mid_blocks, out_proj, branch_pre, state, keep_prefix)
    branch_pre_grad = branch_pre_grad.reshape(group, width)
    mid_rows = mid_blocks.reshape(group, model)
    reach, direct, branch_pre_grad, mid_rows = tied(reach[0], direct, branch_pre_grad, mid_rows)
    after = carry_in(ends[0, 0], reach, True)
    out_full = product_left_t(mixed, mid_rows).astype(bf16)
    branch_full = product_left_t(branch_pre_grad, normed).astype(bf16)
    after, pair_full = tied(after, jnp.concatenate([out_full, branch_full]))
    pair_part = lax.psum_scatter(pair_full, "seq", scatter_dimension=0, tiled=True)
    tile = lambda v: jnp.broadcast_to(v, (TILE, width))
    rate_low, input_low, inner_grad, tail, rim_grad, sums = recur_backward(
        direct,
        state,
        conv,
        sig_rate,
        sig_input,
        inner,
        masks,
        rim,
        tile(state_in),
        tile(after),
        conv_taps,
        vecs,
        rate_dense,
        input_dense,
    )
    fixed = tail + from_neighbour(rim_grad, 1)
    low_rows = conv_low.reshape(group, width)
    rate_w = diagonal_blocks(product_left_t(low_rows, rate_low.reshape(group, width)), blocks_n)
    input_w = diagonal_blocks(product_left_t(low_rows, input_low.reshape(group, width)), blocks_n)
    inner_grad = lax.dynamic_update_slice(
        inner_grad, fixed.astype(bf16)[None], (tp_size - 1, length - TILE, 0)
    ).reshape(group, width)
    in_full = product_left_t(inner_grad, normed).astype(bf16)
    ours, theirs = both_halves(rate_w.astype(bf16), input_w.astype(bf16), core)
    block_sum = ours + swap(theirs, "seq", 1)
    normed_part = (product(inner_grad, in_t) + product(branch_pre_grad, branch_t)).astype(bf16)
    rows_mine, normed_part, in_full = rows_spread(normed_part, in_full)
    rows_theirs = swap(rows_mine, "seq", 1)
    normed_part, in_full, pair_part, rows_mine, rows_theirs, block_sum, dense_part = tied(
        normed_part, in_full, pair_part, rows_mine, rows_theirs, block_sum, dense_part
    )
    pair_sum = lax.all_gather(pair_part, "seq", axis=0, tiled=True)
    in_part = lax.psum_scatter(in_full, "seq", scatter_dimension=0, tiled=True)
    split = lambda rows: rows.reshape(tp_size, length, model)
    grad_and_out = scatter_rows(jnp.concatenate([split(normed_part), split(dense_part)], axis=1))
    block_other = swap(block_sum, "seq", 2)

    places = jnp.stack([core, tp_place]).astype(jnp.int32)
    blocked = lambda rows: rows.reshape(tp_size, chips, length, model)
    gate_w, up_w, down_w = dense_weight_grads(
        blocked(rows_mine), blocked(rows_theirs), cot_all, gate_proj, up_proj, down_proj, places
    )
    gate_w, up_w, down_w, in_part, grad_and_out, block_other = tied(
        gate_w, up_w, down_w, in_part, grad_and_out, block_other
    )
    normed_grad, dense_out = grad_and_out[:length], grad_and_out[length:]
    block_sum = block_sum + block_other
    bit = 4
    while bit < seq_size:
        block_sum = block_sum + swap(block_sum, "seq", bit)
        bit *= 2
    in_sum = lax.all_gather(in_part, "seq", axis=0, tiled=True)
    halves = [(gate_w, swap(gate_w, "seq", 1), 1), (up_w, swap(up_w, "seq", 1), 1), (down_w, swap(down_w, "seq", 1), 0)]
    output = (mid + dense_out).astype(bf16)
    own = tokens.astype(f32)
    own_root = rms(own)
    rows_grad, mixer_gain_part = norm_back(normed_grad, own * own_root, mixer_scale, own_root)
    tokens_grad = mid_grad + rows_grad
    out_sum, branch_sum = pair_sum[:width].astype(f32), pair_sum[width:].astype(f32)

    small = jnp.stack([mixer_gain_part, dense_gain_part])
    whole = []
    for axis, size in (("tp", tp_size), ("seq", seq_size)):
        if axis == "seq":
            gain_own = lax.dynamic_slice_in_dim(small, tp_place * gain_share, gain_share, 1)
            wide = max(width, gain_share)
            fit = lambda v: jnp.pad(v, ((0, 0), (0, wide - v.shape[1])))
            small = jnp.concatenate([fit(sums), fit(gain_own)])
        bit = 1
        while bit < size:
            other = swap(small, axis, bit)
            if halves:
                mine, theirs, along = halves.pop(0)
                made, other = tied(joined(mine, theirs, places, along), other)
                whole.append(made)
            small = small + other
            bit *= 2
    gate_sum, up_sum, down_sum = whole
    sums, gain_sum = small[:-2, :width], small[-2:, :gain_share]
    decay_sum = 8.0 * jax.nn.sigmoid(-decay_param) * sums[2]
    rate_sum, input_sum = both_halves(block_sum, swap(block_sum, "seq", 1), core)
    rate_sum, input_sum = rate_sum.astype(f32), input_sum.astype(f32)
    in_sum, out_sum, branch_sum = tied(in_sum, out_sum, branch_sum)
    return (
        output,
        tokens_grad,
        gain_sum[0],
        in_sum.astype(f32).T,
        branch_sum.astype(f32).T,
        sums[4 : 4 + taps_n],
        sums[3],
        rate_sum,
        sums[0],
        input_sum,
        sums[1],
        decay_sum,
        out_sum.astype(f32),
        gain_sum[1],
        gate_sum,
        up_sum,
        down_sum,
    )


def solution(mesh):
    return jax.shard_map(
        shards,
        mesh=mesh,
        in_specs=(
            P(("seq", "tp"), None),
            P("tp"),
            P(None, "tp"),
            P(None, "tp"),
            P(None, "tp"),
            P("tp"),
            P("tp", None, None),
            P("tp"),
            P("tp", None, None),
            P("tp"),
            P("tp"),
            P("tp", None),
            P("tp"),
            P(None, "tp"),
            P(None, "tp"),
            P("tp", None),
            P("seq"),
            P(("seq", "tp"), None),
        ),
        out_specs=(
            P(("seq", "tp"), None),
            P(("seq", "tp"), None),
            P("tp"),
            P(None, "tp"),
            P(None, "tp"),
            P(None, "tp"),
            P("tp"),
            P("tp", None, None),
            P("tp"),
            P("tp", None, None),
            P("tp"),
            P("tp"),
            P("tp", None),
            P("tp"),
            P(None, "tp"),
            P(None, "tp"),
            P("tp", None),
        ),
        check_vma=False,
    )
```

```python
import math

import jax
import jax.numpy as jnp
from jax import lax
from jax.experimental import pallas as pl
from jax.experimental.pallas import tpu as pltpu
from jax.sharding import PartitionSpec as P

epsilon = 1e-06
f32 = jnp.float32
bf16 = jnp.bfloat16
TILE = 8
VMEM_LIMIT = 50 * 1024 * 1024


def product(left, right):
    return jnp.dot(left, right, preferred_element_type=f32)


def product_left_t(left, right):
    return lax.dot_general(left, right, (((0,), (0,)), ((), ())), preferred_element_type=f32)


def product_right_t(left, right):
    return lax.dot_general(left, right, (((1,), (1,)), ((), ())), preferred_element_type=f32)


def gelu_tanh(values):
    return jax.nn.gelu(values, approximate=True)


def tied(*values):
    return lax.optimization_barrier(values)


def swap(value, axis, bit):
    count = lax.axis_size(axis)
    return lax.ppermute(value, axis, [(i, i ^ bit) for i in range(count)])


def gather_rows(rows):
    count = lax.axis_size("tp")
    place = lax.axis_index("tp")
    whole = jnp.zeros((count,) + rows.shape, rows.dtype)
    for r in range(count):
        block = rows if r == 0 else swap(rows, "tp", r)
        whole = lax.dynamic_update_index_in_dim(whole, block, place ^ r, 0)
    return whole


def spread(rows):
    count = lax.axis_size("tp")
    if count != 4:
        whole = jnp.stack([rows] + [swap(rows, "tp", r) for r in range(1, count)])
        return lambda *after: after, lambda *after: tied(whole, *after)
    half = rows.shape[0] // 2
    parts = []

    def first(*after):
        one, two, rest, *after = tied(swap(rows[:half], "tp", 1), swap(rows[:half], "tp", 2), rows[half:], *after)
        parts.extend([one, two, swap(rest, "tp", 1), swap(rest, "tp", 2)])
        return after

    def finish(*after):
        one, two, one_rest, two_rest, *after = tied(*parts, *after)
        far, far_rest = swap(two, "tp", 1), swap(one_rest, "tp", 2)
        whole = jnp.concatenate([rows, one, one_rest, two, two_rest, far, far_rest])
        return (whole.reshape((count,) + rows.shape), *after)

    return first, finish


def scatter_rows(blocks):
    place = lax.axis_index("tp")
    block = lambda r: lax.dynamic_index_in_dim(blocks, place ^ r, 0, False)
    total = block(0).astype(f32)
    for r in range(1, lax.axis_size("tp")):
        total = total + swap(block(r), "tp", r).astype(f32)
    return total


def carry_in(keep_total, value_total, backward):
    place = lax.axis_index("seq")
    total = jnp.stack([keep_total, value_total])
    before = jnp.stack([jnp.ones_like(keep_total), jnp.zeros_like(value_total)])
    bit = 1
    while bit < lax.axis_size("seq"):
        other = swap(total, "seq", bit)
        upper = (place & bit) != 0
        earlier = jnp.logical_not(upper) if backward else upper
        joined_before = jnp.stack([other[0] * before[0], before[0] * other[1] + before[1]])
        before = jnp.where(earlier, joined_before, before)
        first = jnp.where(earlier, other, total)
        second = jnp.where(earlier, total, other)
        total = jnp.stack([first[0] * second[0], second[0] * first[1] + second[1]])
        bit *= 2
    return before[1]


def from_neighbour(value, step):
    count = lax.axis_size("seq")
    place = lax.axis_index("seq")
    inside = lax.ppermute(value, "seq", [(i, i ^ 1) for i in range(count)])
    pairs = [(i, i + 1) for i in range(1, count - 1, 2)] + [(i + 1, i) for i in range(1, count - 1, 2)]
    across = lax.ppermute(value, "seq", pairs)
    return jnp.where((place % 2 == 0) == (step == 1), inside, across)


def sum_bits(value, axis):
    bit = 1
    while bit < lax.axis_size(axis):
        value = value + swap(value, axis, bit)
        bit *= 2
    return value


def both_halves(mine, theirs, core):
    first = jnp.where(core == 0, mine, theirs)
    second = jnp.where(core == 0, theirs, mine)
    return first, second


def gelu_grads(gate_pre, up_pre, hidden_grad):
    square = gate_pre * gate_pre
    inner = math.sqrt(2.0 / math.pi) * gate_pre * (1.0 + 0.044715 * square)
    half = 0.5 * (1.0 + jnp.tanh(inner))
    act = gate_pre * half
    slope = half + 2.0 * math.sqrt(2.0 / math.pi) * act * (1.0 - half) * (1.0 + 3.0 * 0.044715 * square)
    return act * up_pre, hidden_grad * up_pre * slope, hidden_grad * act


def dense_weight_grads(mine, theirs, cot_all, gate_proj, up_proj, down_proj, places):
    tp_size, chips, block, model = mine.shape
    half = gate_proj.shape[1] // 2
    cot_all = cot_all.reshape(chips, 2, tp_size, block, model)
    part = math.gcd(chips, 4)
    length = part * block
    per_core = tp_size * chips // part
    steps, outs = 2 * per_core, 4
    tile = math.gcd(half, 256)
    left_t = (((0,), (0,)), ((), ()))
    right_t = (((1,), (1,)), ((), ()))

    def kernel(core_ref, mine_ref, theirs_ref, cot_ref, gate_ref, up_ref, down_ref, *rest):
        gate_out, up_out, down_out, acc_g, acc_u, acc_d, hid, gg, ug, x_ref = rest
        i = pl.program_id(0)

        @pl.when(i < per_core)
        def _():
            x_ref[...] = mine_ref[...].reshape(length, model)

        @pl.when(jnp.logical_and(i >= per_core, i < steps))
        def _():
            x_ref[...] = theirs_ref[...].reshape(length, model)

        @pl.when(i == 0)
        def _():
            acc_g[...] = jnp.zeros_like(acc_g)
            acc_u[...] = jnp.zeros_like(acc_u)
            acc_d[...] = jnp.zeros_like(acc_d)

        @pl.when(i < steps)
        def _():
            cots = cot_ref[...].reshape(length, model)
            for n in range(half // tile):
                cols = slice(n * tile, (n + 1) * tile)
                gate_pre = jnp.dot(x_ref[...], gate_ref[:, cols], preferred_element_type=f32)
                up_pre = jnp.dot(x_ref[...], up_ref[:, cols], preferred_element_type=f32)
                hidden_grad = lax.dot_general(cots, down_ref[cols, :], right_t, preferred_element_type=f32)
                a, b, c = gelu_grads(gate_pre, up_pre, hidden_grad)
                hid[:, cols] = a.astype(bf16)
                gg[:, cols] = b.astype(bf16)
                ug[:, cols] = c.astype(bf16)
            acc_g[...] += lax.dot_general(x_ref[...], gg[...], left_t, preferred_element_type=f32)
            acc_u[...] += lax.dot_general(x_ref[...], ug[...], left_t, preferred_element_type=f32)
            acc_d[...] += lax.dot_general(hid[...], cots, left_t, preferred_element_type=f32)

        @pl.when(i >= steps)
        def _():
            wide = pl.ds(pl.multiple_of((i - steps) * (model // outs), model // outs), model // outs)
            low = pl.ds(pl.multiple_of((i - steps) * (half // outs), half // outs), half // outs)
            gate_out[...] = acc_g[wide, :].astype(bf16)
            up_out[...] = acc_u[wide, :].astype(bf16)
            down_out[...] = acc_d[low, :].astype(bf16)

    once = pl.Buffered(1)
    groups = chips // part
    out_index = lambda i, c: (jnp.maximum(i - steps, 0), 0)

    def cot_index(i, c):
        i = jnp.minimum(i, steps - 1)
        n = i % per_core
        return n % groups, c[0] ^ (i // per_core), c[1] ^ (n // groups), 0, 0

    def rows_index(first):
        def index(i, c):
            n = jnp.clip(i - first, 0, per_core - 1)
            return n // groups, n % groups, 0, 0

        return pl.BlockSpec((1, part, block, model), index)

    return pl.pallas_call(
        kernel,
        grid_spec=pltpu.PrefetchScalarGridSpec(
            num_scalar_prefetch=1,
            grid=(steps + outs,),
            in_specs=[
                rows_index(0),
                rows_index(per_core),
                pl.BlockSpec((part, 1, 1, block, model), cot_index),
                pl.BlockSpec((model, half), lambda i, c: (0, c[0]), pipeline_mode=once),
                pl.BlockSpec((model, half), lambda i, c: (0, c[0]), pipeline_mode=once),
                pl.BlockSpec((half, model), lambda i, c: (c[0], 0), pipeline_mode=once),
            ],
            out_specs=[
                pl.BlockSpec((model // outs, half), out_index),
                pl.BlockSpec((model // outs, half), out_index),
                pl.BlockSpec((half // outs, model), out_index),
            ],
            scratch_shapes=[
                pltpu.VMEM((model, half), f32),
                pltpu.VMEM((model, half), f32),
                pltpu.VMEM((half, model), f32),
                pltpu.VMEM((length, half), bf16),
                pltpu.VMEM((length, half), bf16),
                pltpu.VMEM((length, half), bf16),
                pltpu.VMEM((length, model), bf16),
            ],
        ),
        out_shape=[
            jax.ShapeDtypeStruct((model, half), bf16),
            jax.ShapeDtypeStruct((model, half), bf16),
            jax.ShapeDtypeStruct((half, model), bf16),
        ],
        compiler_params=pltpu.CompilerParams(vmem_limit_bytes=60 * 1024 * 1024),
        cost_estimate=pl.CostEstimate(flops=1000, bytes_accessed=1000, transcendentals=0),
        name="dense_weight_grads",
    )(places, mine, theirs, cot_all, gate_proj, up_proj, down_proj)


def joined(mine, theirs, core, axis):
    rows, cols = mine.shape
    block = math.gcd(rows, 256)
    steps = rows // block

    def kernel(core_ref, mine_ref, theirs_ref, out_ref):
        for low in range(2):

            @pl.when(core_ref[0] == low)
            def _(low=low):
                pair = (mine_ref, theirs_ref) if low == 0 else (theirs_ref, mine_ref)
                if axis == 1:
                    out_ref[:, :cols] = pair[0][...].astype(f32)
                    out_ref[:, cols:] = pair[1][...].astype(f32)
                else:
                    out_ref[0] = pair[0][...].astype(f32)
                    out_ref[1] = pair[1][...].astype(f32)

    half = pl.BlockSpec((block, cols), lambda i, c: (i, 0))
    if axis == 1:
        out_spec = pl.BlockSpec((block, 2 * cols), lambda i, c: (i, 0))
        out_shape = jax.ShapeDtypeStruct((rows, 2 * cols), f32)
    else:
        out_spec = pl.BlockSpec((2, block, cols), lambda i, c: (0, i, 0))
        out_shape = jax.ShapeDtypeStruct((2, rows, cols), f32)
    out = pl.pallas_call(
        kernel,
        grid_spec=pltpu.PrefetchScalarGridSpec(
            num_scalar_prefetch=1, grid=(steps,), in_specs=[half, half], out_specs=out_spec
        ),
        out_shape=out_shape,
        compiler_params=pltpu.CompilerParams(vmem_limit_bytes=VMEM_LIMIT),
        cost_estimate=pl.CostEstimate(flops=0, bytes_accessed=12 * rows * cols, transcendentals=0),
        name="joined",
    )(core, mine, theirs)
    return out if axis == 1 else out.reshape(2 * rows, cols)


def dense_rows(rows, cot_all, group_place, gate_proj, up_proj, down_proj):
    length, model = rows.shape
    width = gate_proj.shape[1]
    tile = math.gcd(width, 256)
    out_tile = math.gcd(model, 256)
    first, second = width // tile, model // out_tile
    right_t = (((1,), (1,)), ((), ()))

    def kernel(place_ref, x_ref, c_ref, gate_ref, up_ref, down_ref, hidden_ref, grad_ref, gates, ups, gate_grads, up_grads):
        j = pl.program_id(0)

        @pl.when(j < first)
        def _():
            gate_pre = jnp.dot(x_ref[...], gate_ref[...], preferred_element_type=f32)
            up_pre = jnp.dot(x_ref[...], up_ref[...], preferred_element_type=f32)
            hidden_grad = lax.dot_general(c_ref[...], down_ref[...], right_t, preferred_element_type=f32)
            hidden, gate_grad, up_grad = gelu_grads(gate_pre, up_pre, hidden_grad)
            hidden_ref[...] = hidden.astype(bf16)
            at = pl.ds(pl.multiple_of(j * tile, tile), tile)
            gates[:, at] = gate_ref[...]
            ups[:, at] = up_ref[...]
            gate_grads[:, at] = gate_grad.astype(bf16)
            up_grads[:, at] = up_grad.astype(bf16)

        @pl.when(j >= first)
        def _():
            at = pl.ds(pl.multiple_of((j - first) * out_tile, out_tile), out_tile)
            part = lax.dot_general(gate_grads[...], gates[at, :], right_t, preferred_element_type=f32)
            part = part + lax.dot_general(up_grads[...], ups[at, :], right_t, preferred_element_type=f32)
            grad_ref[...] = part.astype(bf16)

    clamp = lambda j: jnp.minimum(j, first - 1)
    wide = pl.BlockSpec((model, tile), lambda j, p: (0, clamp(j)))
    return pl.pallas_call(
        kernel,
        grid_spec=pltpu.PrefetchScalarGridSpec(
            num_scalar_prefetch=1,
            grid=(first + second,),
            in_specs=[
                pl.BlockSpec((length, model), lambda j, p: (0, 0)),
                pl.BlockSpec((length, model), lambda j, p: (p[0], 0)),
                wide,
                wide,
                pl.BlockSpec((tile, model), lambda j, p: (clamp(j), 0)),
            ],
            out_specs=[
                pl.BlockSpec((length, tile), lambda j, p: (0, clamp(j))),
                pl.BlockSpec((length, out_tile), lambda j, p: (0, jnp.maximum(j - first, 0))),
            ],
            scratch_shapes=[
                pltpu.VMEM((model, width), bf16),
                pltpu.VMEM((model, width), bf16),
                pltpu.VMEM((length, width), bf16),
                pltpu.VMEM((length, width), bf16),
            ],
        ),
        out_shape=[
            jax.ShapeDtypeStruct((length, width), bf16),
            jax.ShapeDtypeStruct((length, model), bf16),
        ],
        compiler_params=pltpu.CompilerParams(vmem_limit_bytes=VMEM_LIMIT),
        name="dense_rows",
    )(group_place, rows, cot_all, gate_proj, up_proj, down_proj)


def project_t(rows, weight_t):
    total, model = rows.shape
    width = weight_t.shape[0]
    length = math.gcd(total, 256)

    def kernel(rows_ref, weight_ref, out_ref):
        out_ref[...] = lax.dot_general(
            rows_ref[...], weight_ref[...], (((1,), (1,)), ((), ())), preferred_element_type=f32
        )

    return pl.pallas_call(
        kernel,
        grid=(total // length,),
        in_specs=[
            pl.BlockSpec((length, model), lambda j: (j, 0)),
            pl.BlockSpec((width, model), lambda j: (0, 0)),
        ],
        out_specs=pl.BlockSpec((length, width), lambda j: (j, 0)),
        out_shape=jax.ShapeDtypeStruct((total, width), f32),
        compiler_params=pltpu.CompilerParams(vmem_limit_bytes=VMEM_LIMIT),
        name="project_t",
    )(rows, weight_t)


def mix_out(value_prefix, keep_prefix, branch_pre, state_in, out_proj):
    blocks, length, width = value_prefix.shape
    model = out_proj.shape[1]

    def kernel(value_ref, keep_ref, branch_ref, in_ref, out_ref, state_ref, mixed_ref, part_ref):
        state = value_ref[0] + keep_ref[0] * in_ref[...]
        state_ref[0] = state
        mixed = (state * gelu_tanh(branch_ref[0])).astype(bf16)
        mixed_ref[0] = mixed
        part_ref[0] = jnp.dot(mixed, out_ref[...], preferred_element_type=f32).astype(bf16)

    block = pl.BlockSpec((1, length, width), lambda j: (j, 0, 0))
    whole = lambda *shape: pl.BlockSpec(shape, lambda j: (0,) * len(shape))
    return pl.pallas_call(
        kernel,
        grid=(blocks,),
        in_specs=[block, block, block, whole(1, width), whole(width, model)],
        out_specs=[block, block, pl.BlockSpec((1, length, model), lambda j: (j, 0, 0))],
        out_shape=[
            jax.ShapeDtypeStruct((blocks, length, width), f32),
            jax.ShapeDtypeStruct((blocks, length, width), bf16),
            jax.ShapeDtypeStruct((blocks, length, model), bf16),
        ],
        compiler_params=pltpu.CompilerParams(vmem_limit_bytes=VMEM_LIMIT),
        name="mix_out",
    )(value_prefix, keep_prefix, branch_pre, state_in, out_proj)


def mix_back(mid_rows, out_proj, branch_pre, state, keep_prefix):
    blocks, length, width = state.shape
    model = out_proj.shape[1]
    tiles = length // 16

    def kernel(mid_ref, out_ref, branch_ref, state_ref, keep_ref, direct_ref, branch_grad_ref, reach_ref, mixed, acc):
        j = pl.program_id(0)
        mixed[...] = lax.dot_general(
            mid_ref[0], out_ref[...], (((1,), (1,)), ((), ())), preferred_element_type=f32
        )

        @pl.when(j == 0)
        def _():
            acc[...] = jnp.zeros_like(acc)

        def tile(i, total):
            at = pl.ds(pl.multiple_of(i * 16, 16), 16)
            grad = mixed[at, :]
            pre = branch_ref[0, at, :]
            square = pre * pre
            inner = math.sqrt(2.0 / math.pi) * pre * (1.0 + 0.044715 * square)
            half = 0.5 * (1.0 + jnp.tanh(inner))
            act = pre * half
            slope = half + 2.0 * math.sqrt(2.0 / math.pi) * act * (1.0 - half) * (1.0 + 3.0 * 0.044715 * square)
            direct = grad * act
            direct_ref[0, at, :] = direct
            branch_grad_ref[0, at, :] = (grad * state_ref[0, at, :] * slope).astype(bf16)
            return total + direct * keep_ref[0, at, :]

        acc[...] = lax.fori_loop(0, tiles, tile, acc[...])

        @pl.when(j == blocks - 1)
        def _():
            reach_ref[...] = jnp.sum(acc[...], axis=0, keepdims=True)

    block = pl.BlockSpec((1, length, width), lambda j: (j, 0, 0))
    whole = lambda *shape: pl.BlockSpec(shape, lambda j: (0,) * len(shape))
    return pl.pallas_call(
        kernel,
        grid=(blocks,),
        in_specs=[pl.BlockSpec((1, length, model), lambda j: (j, 0, 0)), whole(width, model), block, block, block],
        out_specs=[block, block, whole(1, width)],
        out_shape=[
            jax.ShapeDtypeStruct((blocks, length, width), f32),
            jax.ShapeDtypeStruct((blocks, length, width), bf16),
            jax.ShapeDtypeStruct((1, width), f32),
        ],
        scratch_shapes=[pltpu.VMEM((length, width), f32), pltpu.VMEM((16, width), f32)],
        compiler_params=pltpu.CompilerParams(vmem_limit_bytes=VMEM_LIMIT),
        name="mix_back",
    )(mid_rows, out_proj, branch_pre, state, keep_prefix)


def minus_expm1(x):
    series = 1.0 / 40320.0
    for term in (1.0 / 5040.0, 1.0 / 720.0, 1.0 / 120.0, 1.0 / 24.0, 1.0 / 6.0, 0.5, 1.0):
        series = series * x + term
    return jnp.where(x > -0.35, -x * series, 1.0 - jnp.exp(x))


def rows_of(shape):
    return lax.broadcasted_iota(jnp.int32, shape, 0)


def down(cur, prev, by, row):
    return jnp.where(row >= by, pltpu.roll(cur, by, 0), pltpu.roll(prev, by, 0))


def up(cur, after, by, row):
    return jnp.where(row < TILE - by, pltpu.roll(cur, TILE - by, 0), pltpu.roll(after, TILE - by, 0))


def last_row(tile):
    return jnp.broadcast_to(tile[TILE - 1 :, :], tile.shape)


def first_row(tile):
    return jnp.broadcast_to(tile[:1, :], tile.shape)


def forward_kernel(
    inner_ref,
    mask_ref,
    rim_ref,
    taps_ref,
    vec_ref,
    rate_ref,
    input_ref,
    conv_ref,
    low_ref,
    sig_rate_ref,
    sig_input_ref,
    keep_ref,
    value_ref,
    end_ref,
    prev_ref,
    carry_ref,
    rate_raw_ref,
    input_raw_ref,
):
    step = pl.program_id(0)
    length, width = inner_ref.shape[1:]
    tiles = length // TILE
    taps_n = taps_ref.shape[0]

    @pl.when(step == 0)
    def _():
        prev_ref[...] = rim_ref[...]
        carry_ref[0] = jnp.ones((TILE, width), f32)
        carry_ref[1] = jnp.zeros((TILE, width), f32)

    row = rows_of((TILE, width))

    def conv_tile(i, prev):
        at = pl.ds(pl.multiple_of(i * TILE, TILE), TILE)
        cur = inner_ref[0, at, :]
        masks = mask_ref[at, :]
        total = vec_ref[0:1, :] + taps_ref[0:1, :] * cur
        for k in range(1, taps_n):
            total = total + taps_ref[k : k + 1, :] * (down(cur, prev, k, row) * masks[:, k : k + 1])
        conv_ref[0, at, :] = total
        return cur

    prev_ref[...] = lax.fori_loop(0, tiles, conv_tile, prev_ref[...])
    low = conv_ref[0].astype(bf16)
    low_ref[0] = low
    rate_raw_ref[...] = jnp.dot(low, rate_ref[...], preferred_element_type=f32)
    input_raw_ref[...] = jnp.dot(low, input_ref[...], preferred_element_type=f32)

    def gate_tile(i, carry):
        keep_in, value_in = carry
        at = pl.ds(pl.multiple_of(i * TILE, TILE), TILE)
        sig_rate = jax.nn.sigmoid(rate_raw_ref[at, :] + vec_ref[1:2, :])
        sig_input = jax.nn.sigmoid(input_raw_ref[at, :] + vec_ref[2:3, :])
        sig_rate_ref[0, at, :] = sig_rate
        sig_input_ref[0, at, :] = sig_input
        log_decay = sig_rate * vec_ref[3:4, :]
        a = jnp.exp(log_decay) * mask_ref[at, 0:1]
        b = jnp.sqrt(minus_expm1(2.0 * log_decay)) * sig_input * conv_ref[0, at, :]
        for d in (1, 2, 4):
            a_before = jnp.where(row >= d, pltpu.roll(a, d, 0), 1.0)
            b_before = jnp.where(row >= d, pltpu.roll(b, d, 0), 0.0)
            b = b + a * b_before
            a = a * a_before
        b = b + a * value_in
        a = a * keep_in
        keep_ref[0, at, :] = a
        value_ref[0, at, :] = b
        return last_row(a), last_row(b)

    keep_end, value_end = lax.fori_loop(0, tiles, gate_tile, (carry_ref[0], carry_ref[1]))
    carry_ref[0] = keep_end
    carry_ref[1] = value_end
    end_ref[0] = keep_end
    end_ref[1] = value_end


def backward_kernel(
    direct_ref,
    state_ref,
    state_prev_ref,
    conv_ref,
    sig_rate_ref,
    sig_input_ref,
    inner_ref,
    inner_prev_ref,
    mask_ref,
    rim_ref,
    state_in_ref,
    after_ref,
    taps_ref,
    vec_ref,
    rate_ref,
    input_ref,
    rate_grad_ref,
    input_grad_ref,
    inner_grad_ref,
    tail_ref,
    rim_grad_ref,
    sums_ref,
    carry_ref,
    next_ref,
    acc_ref,
    rate_f_ref,
    input_f_ref,
    conv_f_ref,
):
    step = pl.program_id(0)
    steps = pl.num_programs(0)
    length, width = direct_ref.shape[1:]
    tiles = length // TILE
    taps_n = taps_ref.shape[0]
    row = rows_of((TILE, width))
    is_first_block = step == steps - 1

    @pl.when(step == 0)
    def _():
        carry_ref[...] = after_ref[...]
        next_ref[...] = jnp.zeros_like(next_ref)
        acc_ref[...] = jnp.zeros_like(acc_ref)

    edge_state = jnp.where(is_first_block, state_in_ref[...], state_prev_ref[0])
    edge_inner = jnp.where(is_first_block, rim_ref[...], inner_prev_ref[0])
    neg_rate = vec_ref[3:4, :]

    def gate_tile(n, carry):
        after, acc_rate, acc_input, acc_decay = carry
        i = tiles - 1 - n
        at = pl.ds(pl.multiple_of(i * TILE, TILE), TILE)
        before = pl.ds(pl.multiple_of(jnp.maximum(i - 1, 0) * TILE, TILE), TILE)
        direct = direct_ref[0, at, :]
        sig_rate = sig_rate_ref[0, at, :]
        sig_input = sig_input_ref[0, at, :]
        conv = conv_ref[0, at, :]
        log_decay = sig_rate * neg_rate
        decay = jnp.exp(log_decay)
        keep = decay * mask_ref[at, 0:1]
        room = minus_expm1(2.0 * log_decay)
        root = jnp.sqrt(room)
        a = keep
        b = keep * direct
        for d in (1, 2, 4):
            a_after = jnp.where(row < TILE - d, pltpu.roll(a, TILE - d, 0), 1.0)
            b_after = jnp.where(row < TILE - d, pltpu.roll(b, TILE - d, 0), 0.0)
            b = b + a * b_after
            a = a * a_after
        reach = b + a * after
        grad = direct + up(reach, after, 1, row)
        prev_tile = jnp.where(i == 0, edge_state, state_ref[0, before, :])
        state_prev = down(state_ref[0, at, :], prev_tile, 1, row)
        grad_root = grad * root
        gated = grad_root * sig_input
        decay_grad = grad * (keep * state_prev - sig_input * conv * (decay * decay) / root)
        rate_grad = decay_grad * neg_rate * (sig_rate * (1.0 - sig_rate))
        input_grad = gated * conv * (1.0 - sig_input)
        rate_f_ref[at, :] = rate_grad
        input_f_ref[at, :] = input_grad
        conv_f_ref[at, :] = gated
        return (
            first_row(reach),
            acc_rate + rate_grad,
            acc_input + input_grad,
            acc_decay + decay_grad * sig_rate,
        )

    after, acc_rate, acc_input, acc_decay = lax.fori_loop(
        0, tiles, gate_tile, (carry_ref[...], acc_ref[0], acc_ref[1], acc_ref[2])
    )
    carry_ref[...] = after
    acc_ref[0] = acc_rate
    acc_ref[1] = acc_input
    acc_ref[2] = acc_decay
    rate_low = rate_f_ref[...].astype(bf16)
    input_low = input_f_ref[...].astype(bf16)
    rate_grad_ref[0] = rate_low
    input_grad_ref[0] = input_low
    right_t = (((1,), (1,)), ((), ()))
    conv_f_ref[...] += lax.dot_general(
        rate_low, rate_ref[...], right_t, preferred_element_type=f32
    ) + lax.dot_general(input_low, input_ref[...], right_t, preferred_element_type=f32)

    def conv_tile(n, carry):
        acc_bias, acc_taps, nexts = carry
        i = tiles - 1 - n
        at = pl.ds(pl.multiple_of(i * TILE, TILE), TILE)
        before = pl.ds(pl.multiple_of(jnp.maximum(i - 1, 0) * TILE, TILE), TILE)
        grad = conv_f_ref[at, :]
        masks = mask_ref[at, :]
        cur = inner_ref[0, at, :]
        prev = jnp.where(i == 0, edge_inner, inner_ref[0, before, :])
        total = grad * taps_ref[0:1, :]
        new_taps = [acc_taps[0] + grad * cur]
        new_nexts = []
        for k in range(1, taps_n):
            masked = grad * masks[:, k : k + 1]
            part = masked * taps_ref[k : k + 1, :]
            total = total + up(part, nexts[k - 1], k, row)
            new_taps.append(acc_taps[k] + masked * down(cur, prev, k, row))
            new_nexts.append(part)
        rate_f_ref[at, :] = total
        return acc_bias + grad, tuple(new_taps), tuple(new_nexts)

    acc_bias, acc_taps, nexts = lax.fori_loop(
        0,
        tiles,
        conv_tile,
        (
            acc_ref[3],
            tuple(acc_ref[4 + k] for k in range(taps_n)),
            tuple(next_ref[k] for k in range(taps_n - 1)),
        ),
    )
    acc_ref[3] = acc_bias
    for k in range(taps_n):
        acc_ref[4 + k] = acc_taps[k]
    for k in range(taps_n - 1):
        next_ref[k] = nexts[k]
    inner_grad_ref[0] = rate_f_ref[...].astype(bf16)

    @pl.when(step == 0)
    def _():
        tail_ref[...] = rate_f_ref[length - TILE :, :]

    @pl.when(is_first_block)
    def _():
        zero = jnp.zeros((TILE, width), f32)
        total = zero
        for k in range(1, taps_n):
            total = total + up(zero, nexts[k - 1], k, row)
        rim_grad_ref[...] = total
        sums_ref[...] = jnp.sum(acc_ref[...], axis=1)


def norm_project(blocks, place, gain, weight_t):
    count = len(blocks)
    length, model = blocks[0].shape
    width = weight_t.shape[0]

    def kernel(place_ref, *refs):
        ins, gain_ref, weight_ref, normed_ref, out_ref = refs[:count], *refs[count:]
        j = pl.program_id(0)
        for r in range(count):

            @pl.when((j ^ place_ref[0]) == r)
            def _(source=ins[r]):
                x = source[...].astype(f32)
                root = lax.rsqrt(jnp.mean(x * x, axis=-1, keepdims=True) + epsilon)
                normed_ref[...] = (x * root * gain_ref[...]).astype(bf16)

        out_ref[0] = lax.dot_general(
            normed_ref[...], weight_ref[...], (((1,), (1,)), ((), ())), preferred_element_type=f32
        )

    whole = lambda *shape: pl.BlockSpec(shape, lambda j, p: (0,) * len(shape))
    return pl.pallas_call(
        kernel,
        grid_spec=pltpu.PrefetchScalarGridSpec(
            num_scalar_prefetch=1,
            grid=(count,),
            in_specs=[whole(length, model)] * count + [whole(1, model), whole(width, model)],
            out_specs=[
                pl.BlockSpec((length, model), lambda j, p: (j, 0)),
                pl.BlockSpec((1, length, width), lambda j, p: (j, 0, 0)),
            ],
        ),
        out_shape=[
            jax.ShapeDtypeStruct((count * length, model), bf16),
            jax.ShapeDtypeStruct((count, length, width), f32),
        ],
        compiler_params=pltpu.CompilerParams(vmem_limit_bytes=VMEM_LIMIT),
        name="norm_project",
    )(place, *blocks, gain, weight_t)


def recur_forward(inner, masks, rim, taps, vecs, rate_dense, input_dense):
    blocks, length, width = inner.shape
    whole = lambda *shape: pl.BlockSpec(shape, lambda j: (0,) * len(shape))
    block = pl.BlockSpec((1, length, width), lambda j: (j, 0, 0))
    full = jax.ShapeDtypeStruct((blocks, length, width), f32)
    return pl.pallas_call(
        forward_kernel,
        grid_spec=pltpu.PrefetchScalarGridSpec(
            num_scalar_prefetch=0,
            grid=(blocks,),
            in_specs=[
                block,
                pl.BlockSpec((length, masks.shape[1]), lambda j: (j, 0)),
                whole(*rim.shape),
                whole(*taps.shape),
                whole(*vecs.shape),
                whole(*rate_dense.shape),
                whole(*input_dense.shape),
            ],
            out_specs=[block, block, block, block, block, block, whole(2, TILE, width)],
            scratch_shapes=[
                pltpu.VMEM((TILE, width), f32),
                pltpu.VMEM((2, TILE, width), f32),
                pltpu.VMEM((length, width), f32),
                pltpu.VMEM((length, width), f32),
            ],
        ),
        out_shape=[
            full,
            jax.ShapeDtypeStruct((blocks, length, width), bf16),
            full,
            full,
            full,
            full,
            jax.ShapeDtypeStruct((2, TILE, width), f32),
        ],
        compiler_params=pltpu.CompilerParams(vmem_limit_bytes=VMEM_LIMIT),
        name="recur_forward",
    )(inner, masks, rim, taps, vecs, rate_dense, input_dense)


def recur_backward(
    direct, state, conv, sig_rate, sig_input, inner, masks, rim, state_in, after, taps, vecs, rate_dense, input_dense
):
    blocks, length, width = inner.shape
    last = length // TILE - 1
    whole = lambda *shape: pl.BlockSpec(shape, lambda j: (0,) * len(shape))
    block = pl.BlockSpec((1, length, width), lambda j: (blocks - 1 - j, 0, 0))
    edge = pl.BlockSpec(
        (1, TILE, width), lambda j: (jnp.maximum(blocks - 2 - j, 0), last, 0)
    )
    low = jax.ShapeDtypeStruct((blocks, length, width), bf16)
    tile = jax.ShapeDtypeStruct((TILE, width), f32)
    count = 4 + taps.shape[0]
    return pl.pallas_call(
        backward_kernel,
        grid_spec=pltpu.PrefetchScalarGridSpec(
            num_scalar_prefetch=0,
            grid=(blocks,),
            in_specs=[
                block,
                block,
                edge,
                block,
                block,
                block,
                block,
                edge,
                pl.BlockSpec((length, masks.shape[1]), lambda j: (blocks - 1 - j, 0)),
                whole(*rim.shape),
                whole(*state_in.shape),
                whole(*after.shape),
                whole(*taps.shape),
                whole(*vecs.shape),
                whole(*rate_dense.shape),
                whole(*input_dense.shape),
            ],
            out_specs=[
                block,
                block,
                block,
                whole(TILE, width),
                whole(TILE, width),
                whole(count, width),
            ],
            scratch_shapes=[
                pltpu.VMEM((TILE, width), f32),
                pltpu.VMEM((taps.shape[0] - 1, TILE, width), f32),
                pltpu.VMEM((count, TILE, width), f32),
                pltpu.VMEM((length, width), f32),
                pltpu.VMEM((length, width), f32),
                pltpu.VMEM((length, width), f32),
            ],
        ),
        out_shape=[low, low, low, tile, tile, jax.ShapeDtypeStruct((count, width), f32)],
        compiler_params=pltpu.CompilerParams(vmem_limit_bytes=VMEM_LIMIT),
        cost_estimate=pl.CostEstimate(flops=1000, bytes_accessed=1000, transcendentals=0),
        name="recur_backward",
    )(
        direct,
        state,
        state,
        conv,
        sig_rate,
        sig_input,
        inner,
        inner,
        masks,
        rim,
        state_in,
        after,
        taps,
        vecs,
        rate_dense,
        input_dense,
    )


def dense_blocks(blocks):
    count, rows_in, cols_out = blocks.shape
    tall = blocks.reshape(count * rows_in, cols_out)
    wide = jnp.concatenate([tall] * count, axis=1)
    row = lax.broadcasted_iota(jnp.int32, wide.shape, 0) // rows_in
    col = lax.broadcasted_iota(jnp.int32, wide.shape, 1) // cols_out
    return jnp.where(row == col, wide, jnp.zeros_like(wide))


def diagonal_blocks(full, count):
    rows, cols = full.shape[0] // count, full.shape[1] // count
    return jnp.stack([full[i * rows : (i + 1) * rows, i * cols : (i + 1) * cols] for i in range(count)])


def rms(values):
    return lax.rsqrt(jnp.mean(values * values, axis=-1, keepdims=True) + epsilon)


def norm_back(grad, xhat, scale, root):
    e = grad * scale
    return root * (e - xhat * jnp.mean(e * xhat, axis=-1, keepdims=True)), jnp.sum(grad * xhat, axis=0)


def shards(
    tokens,
    mixer_gain,
    in_proj,
    branch_proj,
    conv_taps,
    conv_bias,
    rate_blocks,
    rate_bias,
    input_blocks,
    input_bias,
    decay_param,
    out_proj,
    dense_gain,
    gate_proj,
    up_proj,
    down_proj,
    segment_ids,
    cotangent,
):
    tp_place = lax.axis_index("tp")
    seq_place = lax.axis_index("seq")
    seq_size = lax.axis_size("seq")
    core = seq_place % 2
    tp_size = lax.axis_size("tp")
    gain_share = mixer_gain.shape[0]
    taps_n, width = conv_taps.shape
    rim_width = taps_n - 1
    length, model = tokens.shape
    group = length * tp_size
    blocks_n = rate_blocks.shape[0]

    in_t, branch_t = in_proj.T, branch_proj.T
    place = tp_place.astype(jnp.int32)[None]

    blocks = [tokens] + [swap(tokens, "tp", r) for r in range(1, tp_size)]
    blocks[1], gains, ids, rate_in, input_in, vec_in = tied(
        blocks[1],
        jnp.stack([mixer_gain, dense_gain]),
        segment_ids,
        rate_blocks,
        input_blocks,
        (conv_bias, rate_bias, input_bias, decay_param),
    )
    gains = gather_rows(gains)
    gains = gains.transpose(1, 0, 2).reshape(2, -1).astype(f32)
    mixer_scale, dense_scale = gains[0], gains[1]
    rim_ids = from_neighbour(ids[-rim_width:], -1)
    ext_ids = jnp.concatenate([rim_ids, ids])
    same = [ext_ids[rim_width - k : rim_width - k + group] == ids for k in range(1, taps_n)]
    masks = jnp.stack([same[0]] + same, axis=1).astype(f32)
    rate_dense = dense_blocks(rate_in)
    input_dense = dense_blocks(input_in)
    vecs = jnp.stack([*vec_in[:3], -8.0 * jax.nn.softplus(-vec_in[3])])
    *blocks, masks, rate_dense, input_dense, vecs = tied(*blocks, masks, rate_dense, input_dense, vecs)
    cot_all = lax.all_gather(cotangent, ("seq", "tp"), axis=0, tiled=True)

    normed, inner = norm_project(blocks, place, mixer_scale[None], in_t)
    rim = from_neighbour(inner[-1, -TILE:], -1)
    conv, conv_low, sig_rate, sig_input, keep_prefix, value_prefix, ends = recur_forward(
        inner, masks, rim, conv_taps, vecs, rate_dense, input_dense
    )
    ends, normed_b = tied(ends, normed)
    state_in = carry_in(ends[0, 0], ends[1, 0], False)
    branch_pre = project_t(normed_b, branch_t).reshape(inner.shape)
    state, mixed, mixer_part = mix_out(value_prefix, keep_prefix, branch_pre, state_in[None], out_proj)
    mixed = mixed.reshape(group, width)
    mixer_out = scatter_rows(mixer_part)
    mid = tokens.astype(f32) + mixer_out
    mid_root = rms(mid)
    xhat_dense = mid * mid_root
    normed_two = (xhat_dense * dense_scale).astype(bf16)

    chips = seq_size // 2
    same_core = [[core_no + 2 * i for i in range(chips)] for core_no in range(2)]
    rows_z = lax.all_gather(normed_two, "seq", axis=0, tiled=True, axis_index_groups=same_core)
    rows_two, cot_all = tied(gather_rows(normed_two).reshape(group, model), cot_all)
    hidden, normed_two_part = dense_rows(
        rows_two, cot_all, seq_place.astype(jnp.int32)[None], gate_proj, up_proj, down_proj
    )
    normed_two_grad = scatter_rows(normed_two_part.reshape(tp_size, length, model))
    dense_part = product(hidden, down_proj).astype(bf16)
    normed_two_grad, dense_part = tied(normed_two_grad, dense_part)
    mid_from_norm, dense_gain_part = norm_back(normed_two_grad, xhat_dense, dense_scale, mid_root)
    mid_grad = cotangent.astype(f32) + mid_from_norm
    mid_blocks = gather_rows(mid_grad.astype(bf16))
    mid_blocks, dense_part, rows_z = tied(mid_blocks, dense_part, rows_z)
    spread_first, spread_finish = spread(rows_z)

    direct, branch_pre_grad, reach = mix_back(mid_blocks, out_proj, branch_pre, state, keep_prefix)
    branch_pre_grad = branch_pre_grad.reshape(group, width)
    mid_rows = mid_blocks.reshape(group, model)
    reach, direct, branch_pre_grad, mid_rows = tied(reach[0], direct, branch_pre_grad, mid_rows)
    after = carry_in(ends[0, 0], reach, True)
    out_full = product_left_t(mixed, mid_rows).astype(bf16)
    branch_full = product_left_t(branch_pre_grad, normed).astype(bf16)
    after, pair_full = spread_first(*tied(after, jnp.concatenate([out_full, branch_full])))
    pair_part = lax.psum_scatter(pair_full, "seq", scatter_dimension=0, tiled=True)
    tile = lambda v: jnp.broadcast_to(v, (TILE, width))
    rate_low, input_low, inner_grad, tail, rim_grad, sums = recur_backward(
        direct,
        state,
        conv,
        sig_rate,
        sig_input,
        inner,
        masks,
        rim,
        tile(state_in),
        tile(after),
        conv_taps,
        vecs,
        rate_dense,
        input_dense,
    )
    fixed = tail + from_neighbour(rim_grad, 1)
    rows_mine, fixed = spread_finish(fixed)
    low_rows = conv_low.reshape(group, width)
    rate_w = diagonal_blocks(product_left_t(low_rows, rate_low.reshape(group, width)), blocks_n)
    input_w = diagonal_blocks(product_left_t(low_rows, input_low.reshape(group, width)), blocks_n)
    inner_grad = lax.dynamic_update_slice(
        inner_grad, fixed.astype(bf16)[None], (tp_size - 1, length - TILE, 0)
    ).reshape(group, width)
    in_full = product_left_t(inner_grad, normed).astype(bf16)
    ours, theirs = both_halves(rate_w.astype(bf16), input_w.astype(bf16), core)
    block_sum = ours + swap(theirs, "seq", 1)
    normed_part = (product(inner_grad, in_t) + product(branch_pre_grad, branch_t)).astype(bf16)
    block_other = swap(block_sum, "seq", 2)
    rows_mine, pair_part = tied(rows_mine, pair_part)
    rows_theirs = swap(rows_mine, "seq", 1)
    normed_part, in_full, pair_part, rows_mine, rows_theirs, block_other, dense_part = tied(
        normed_part, in_full, pair_part, rows_mine, rows_theirs, block_other, dense_part
    )
    block_sum = block_sum + block_other
    pair_sum = lax.all_gather(pair_part, "seq", axis=0, tiled=True)
    in_part = lax.psum_scatter(in_full, "seq", scatter_dimension=0, tiled=True)
    split = lambda rows: rows.reshape(tp_size, length, model)
    grad_and_out = scatter_rows(jnp.concatenate([split(normed_part), split(dense_part)], axis=1))
    block_other = swap(block_sum, "seq", 4)

    places = jnp.stack([core, tp_place]).astype(jnp.int32)
    blocked = lambda rows: rows.reshape(tp_size, chips, length, model)
    gate_w, up_w, down_w = dense_weight_grads(
        blocked(rows_mine), blocked(rows_theirs), cot_all, gate_proj, up_proj, down_proj, places
    )
    gate_w, up_w, down_w, in_part, grad_and_out, block_other = tied(
        gate_w, up_w, down_w, in_part, grad_and_out, block_other
    )
    normed_grad, dense_out = grad_and_out[:length], grad_and_out[length:]
    block_sum = block_sum + block_other
    bit = 8
    while bit < seq_size:
        block_sum = block_sum + swap(block_sum, "seq", bit)
        bit *= 2
    in_sum = lax.all_gather(in_part, "seq", axis=0, tiled=True)
    halves = [(gate_w, swap(gate_w, "seq", 1), 1), (up_w, swap(up_w, "seq", 1), 1), (down_w, swap(down_w, "seq", 1), 0)]
    output = (mid + dense_out).astype(bf16)
    own = tokens.astype(f32)
    own_root = rms(own)
    rows_grad, mixer_gain_part = norm_back(normed_grad, own * own_root, mixer_scale, own_root)
    tokens_grad = mid_grad + rows_grad
    out_sum, branch_sum = pair_sum[:width].astype(f32), pair_sum[width:].astype(f32)

    small = jnp.stack([mixer_gain_part, dense_gain_part])
    whole = []
    for axis, size in (("tp", tp_size), ("seq", seq_size)):
        if axis == "seq":
            gain_own = lax.dynamic_slice_in_dim(small, tp_place * gain_share, gain_share, 1)
            wide = max(width, gain_share)
            fit = lambda v: jnp.pad(v, ((0, 0), (0, wide - v.shape[1])))
            small = jnp.concatenate([fit(sums), fit(gain_own)])
        bit = 1
        while bit < size:
            other = swap(small, axis, bit)
            if halves:
                mine, theirs, along = halves.pop(0)
                made, other = tied(joined(mine, theirs, places, along), other)
                whole.append(made)
            small = small + other
            bit *= 2
    gate_sum, up_sum, down_sum = whole
    sums, gain_sum = small[:-2, :width], small[-2:, :gain_share]
    decay_sum = 8.0 * jax.nn.sigmoid(-decay_param) * sums[2]
    rate_sum, input_sum = both_halves(block_sum, swap(block_sum, "seq", 1), core)
    rate_sum, input_sum = rate_sum.astype(f32), input_sum.astype(f32)
    in_sum, out_sum, branch_sum = tied(in_sum, out_sum, branch_sum)
    return (
        output,
        tokens_grad,
        gain_sum[0],
        in_sum.astype(f32).T,
        branch_sum.astype(f32).T,
        sums[4 : 4 + taps_n],
        sums[3],
        rate_sum,
        sums[0],
        input_sum,
        sums[1],
        decay_sum,
        out_sum.astype(f32),
        gain_sum[1],
        gate_sum,
        up_sum,
        down_sum,
    )


def solution(mesh):
    return jax.shard_map(
        shards,
        mesh=mesh,
        in_specs=(
            P(("seq", "tp"), None),
            P("tp"),
            P(None, "tp"),
            P(None, "tp"),
            P(None, "tp"),
            P("tp"),
            P("tp", None, None),
            P("tp"),
            P("tp", None, None),
            P("tp"),
            P("tp"),
            P("tp", None),
            P("tp"),
            P(None, "tp"),
            P(None, "tp"),
            P("tp", None),
            P("seq"),
            P(("seq", "tp"), None),
        ),
        out_specs=(
            P(("seq", "tp"), None),
            P(("seq", "tp"), None),
            P("tp"),
            P(None, "tp"),
            P(None, "tp"),
            P(None, "tp"),
            P("tp"),
            P("tp", None, None),
            P("tp"),
            P("tp", None, None),
            P("tp"),
            P("tp"),
            P("tp", None),
            P("tp"),
            P(None, "tp"),
            P(None, "tp"),
            P("tp", None),
        ),
        check_vma=False,
    )
```

```python
import math

import jax
import jax.numpy as jnp
from jax import lax
from jax.experimental import pallas as pl
from jax.experimental.pallas import tpu as pltpu
from jax.sharding import PartitionSpec as P

epsilon = 1e-06
f32 = jnp.float32
bf16 = jnp.bfloat16
TILE = 8
VMEM_LIMIT = 50 * 1024 * 1024


def product(left, right):
    return jnp.dot(left, right, preferred_element_type=f32)


def product_left_t(left, right):
    return lax.dot_general(left, right, (((0,), (0,)), ((), ())), preferred_element_type=f32)


def product_right_t(left, right):
    return lax.dot_general(left, right, (((1,), (1,)), ((), ())), preferred_element_type=f32)


def gelu_tanh(values):
    return jax.nn.gelu(values, approximate=True)


def tied(*values):
    return lax.optimization_barrier(values)


def swap(value, axis, bit):
    count = lax.axis_size(axis)
    return lax.ppermute(value, axis, [(i, i ^ bit) for i in range(count)])


def gather_rows(rows):
    count = lax.axis_size("tp")
    place = lax.axis_index("tp")
    whole = jnp.zeros((count,) + rows.shape, rows.dtype)
    for r in range(count):
        block = rows if r == 0 else swap(rows, "tp", r)
        whole = lax.dynamic_update_index_in_dim(whole, block, place ^ r, 0)
    return whole


def spread(rows):
    count = lax.axis_size("tp")
    if count != 4:
        whole = jnp.stack([rows] + [swap(rows, "tp", r) for r in range(1, count)])
        return lambda *after: after, lambda *after: tied(whole, *after)
    half = rows.shape[0] // 2
    parts = []

    def first(*after):
        one, two, rest, *after = tied(swap(rows[:half], "tp", 1), swap(rows[:half], "tp", 2), rows[half:], *after)
        parts.extend([one, two, swap(rest, "tp", 1), swap(rest, "tp", 2)])
        return after

    def finish(*after):
        one, two, one_rest, two_rest, *after = tied(*parts, *after)
        far, far_rest = swap(two, "tp", 1), swap(one_rest, "tp", 2)
        whole = jnp.concatenate([rows, one, one_rest, two, two_rest, far, far_rest])
        return (whole.reshape((count,) + rows.shape), *after)

    return first, finish


def scatter_rows(blocks):
    place = lax.axis_index("tp")
    block = lambda r: lax.dynamic_index_in_dim(blocks, place ^ r, 0, False)
    total = block(0).astype(f32)
    for r in range(1, lax.axis_size("tp")):
        total = total + swap(block(r), "tp", r).astype(f32)
    return total


def carry_in(keep_total, value_total, backward):
    place = lax.axis_index("seq")
    total = jnp.stack([keep_total, value_total])
    before = jnp.stack([jnp.ones_like(keep_total), jnp.zeros_like(value_total)])
    bit = 1
    while bit < lax.axis_size("seq"):
        other = swap(total, "seq", bit)
        upper = (place & bit) != 0
        earlier = jnp.logical_not(upper) if backward else upper
        joined_before = jnp.stack([other[0] * before[0], before[0] * other[1] + before[1]])
        before = jnp.where(earlier, joined_before, before)
        first = jnp.where(earlier, other, total)
        second = jnp.where(earlier, total, other)
        total = jnp.stack([first[0] * second[0], second[0] * first[1] + second[1]])
        bit *= 2
    return before[1]


def from_neighbour(value, step):
    count = lax.axis_size("seq")
    place = lax.axis_index("seq")
    inside = lax.ppermute(value, "seq", [(i, i ^ 1) for i in range(count)])
    pairs = [(i, i + 1) for i in range(1, count - 1, 2)] + [(i + 1, i) for i in range(1, count - 1, 2)]
    across = lax.ppermute(value, "seq", pairs)
    return jnp.where((place % 2 == 0) == (step == 1), inside, across)


def sum_bits(value, axis):
    bit = 1
    while bit < lax.axis_size(axis):
        value = value + swap(value, axis, bit)
        bit *= 2
    return value


def both_halves(mine, theirs, core):
    first = jnp.where(core == 0, mine, theirs)
    second = jnp.where(core == 0, theirs, mine)
    return first, second


def gelu_grads(gate_pre, up_pre, hidden_grad):
    square = gate_pre * gate_pre
    inner = math.sqrt(2.0 / math.pi) * gate_pre * (1.0 + 0.044715 * square)
    half = 0.5 * (1.0 + jnp.tanh(inner))
    act = gate_pre * half
    slope = half + 2.0 * math.sqrt(2.0 / math.pi) * act * (1.0 - half) * (1.0 + 3.0 * 0.044715 * square)
    return act * up_pre, hidden_grad * up_pre * slope, hidden_grad * act


def dense_weight_grads(mine, theirs, cot_all, gate_proj, up_proj, down_proj, places):
    tp_size, chips, block, model = mine.shape
    half = gate_proj.shape[1] // 2
    cot_all = cot_all.reshape(chips, 2, tp_size, block, model)
    part = math.gcd(chips, 4)
    length = part * block
    per_core = tp_size * chips // part
    steps, outs = 2 * per_core, 4
    tile = math.gcd(half, 256)
    left_t = (((0,), (0,)), ((), ()))
    right_t = (((1,), (1,)), ((), ()))

    def kernel(core_ref, mine_ref, theirs_ref, cot_ref, gate_ref, up_ref, down_ref, *rest):
        gate_out, up_out, down_out, acc_g, acc_u, acc_d, hid, gg, ug, x_ref = rest
        i = pl.program_id(0)

        @pl.when(i < per_core)
        def _():
            x_ref[...] = mine_ref[...].reshape(length, model)

        @pl.when(jnp.logical_and(i >= per_core, i < steps))
        def _():
            x_ref[...] = theirs_ref[...].reshape(length, model)

        @pl.when(i == 0)
        def _():
            acc_g[...] = jnp.zeros_like(acc_g)
            acc_u[...] = jnp.zeros_like(acc_u)
            acc_d[...] = jnp.zeros_like(acc_d)

        @pl.when(i < steps)
        def _():
            cots = cot_ref[...].reshape(length, model)
            for n in range(half // tile):
                cols = slice(n * tile, (n + 1) * tile)
                gate_pre = jnp.dot(x_ref[...], gate_ref[:, cols], preferred_element_type=f32)
                up_pre = jnp.dot(x_ref[...], up_ref[:, cols], preferred_element_type=f32)
                hidden_grad = lax.dot_general(cots, down_ref[cols, :], right_t, preferred_element_type=f32)
                a, b, c = gelu_grads(gate_pre, up_pre, hidden_grad)
                hid[:, cols] = a.astype(bf16)
                gg[:, cols] = b.astype(bf16)
                ug[:, cols] = c.astype(bf16)
            acc_g[...] += lax.dot_general(x_ref[...], gg[...], left_t, preferred_element_type=f32)
            acc_u[...] += lax.dot_general(x_ref[...], ug[...], left_t, preferred_element_type=f32)
            acc_d[...] += lax.dot_general(hid[...], cots, left_t, preferred_element_type=f32)

        @pl.when(i >= steps)
        def _():
            wide = pl.ds(pl.multiple_of((i - steps) * (model // outs), model // outs), model // outs)
            low = pl.ds(pl.multiple_of((i - steps) * (half // outs), half // outs), half // outs)
            gate_out[...] = acc_g[wide, :].astype(bf16)
            up_out[...] = acc_u[wide, :].astype(bf16)
            down_out[...] = acc_d[low, :].astype(bf16)

    once = pl.Buffered(1)
    groups = chips // part
    out_index = lambda i, c: (jnp.maximum(i - steps, 0), 0)

    def cot_index(i, c):
        i = jnp.minimum(i, steps - 1)
        n = i % per_core
        return n % groups, c[0] ^ (i // per_core), c[1] ^ (n // groups), 0, 0

    def rows_index(first):
        def index(i, c):
            n = jnp.clip(i - first, 0, per_core - 1)
            return n // groups, n % groups, 0, 0

        return pl.BlockSpec((1, part, block, model), index)

    return pl.pallas_call(
        kernel,
        grid_spec=pltpu.PrefetchScalarGridSpec(
            num_scalar_prefetch=1,
            grid=(steps + outs,),
            in_specs=[
                rows_index(0),
                rows_index(per_core),
                pl.BlockSpec((part, 1, 1, block, model), cot_index),
                pl.BlockSpec((model, half), lambda i, c: (0, c[0]), pipeline_mode=once),
                pl.BlockSpec((model, half), lambda i, c: (0, c[0]), pipeline_mode=once),
                pl.BlockSpec((half, model), lambda i, c: (c[0], 0), pipeline_mode=once),
            ],
            out_specs=[
                pl.BlockSpec((model // outs, half), out_index),
                pl.BlockSpec((model // outs, half), out_index),
                pl.BlockSpec((half // outs, model), out_index),
            ],
            scratch_shapes=[
                pltpu.VMEM((model, half), f32),
                pltpu.VMEM((model, half), f32),
                pltpu.VMEM((half, model), f32),
                pltpu.VMEM((length, half), bf16),
                pltpu.VMEM((length, half), bf16),
                pltpu.VMEM((length, half), bf16),
                pltpu.VMEM((length, model), bf16),
            ],
        ),
        out_shape=[
            jax.ShapeDtypeStruct((model, half), bf16),
            jax.ShapeDtypeStruct((model, half), bf16),
            jax.ShapeDtypeStruct((half, model), bf16),
        ],
        compiler_params=pltpu.CompilerParams(vmem_limit_bytes=60 * 1024 * 1024),
        cost_estimate=pl.CostEstimate(flops=1000, bytes_accessed=1000, transcendentals=0),
        name="dense_weight_grads",
    )(places, mine, theirs, cot_all, gate_proj, up_proj, down_proj)


def joined(mine, theirs, core, axis):
    rows, cols = mine.shape
    block = math.gcd(rows, 256)
    steps = rows // block

    def kernel(core_ref, mine_ref, theirs_ref, out_ref):
        for low in range(2):

            @pl.when(core_ref[0] == low)
            def _(low=low):
                pair = (mine_ref, theirs_ref) if low == 0 else (theirs_ref, mine_ref)
                if axis == 1:
                    out_ref[:, :cols] = pair[0][...].astype(f32)
                    out_ref[:, cols:] = pair[1][...].astype(f32)
                else:
                    out_ref[0] = pair[0][...].astype(f32)
                    out_ref[1] = pair[1][...].astype(f32)

    half = pl.BlockSpec((block, cols), lambda i, c: (i, 0))
    if axis == 1:
        out_spec = pl.BlockSpec((block, 2 * cols), lambda i, c: (i, 0))
        out_shape = jax.ShapeDtypeStruct((rows, 2 * cols), f32)
    else:
        out_spec = pl.BlockSpec((2, block, cols), lambda i, c: (0, i, 0))
        out_shape = jax.ShapeDtypeStruct((2, rows, cols), f32)
    out = pl.pallas_call(
        kernel,
        grid_spec=pltpu.PrefetchScalarGridSpec(
            num_scalar_prefetch=1, grid=(steps,), in_specs=[half, half], out_specs=out_spec
        ),
        out_shape=out_shape,
        compiler_params=pltpu.CompilerParams(vmem_limit_bytes=VMEM_LIMIT),
        cost_estimate=pl.CostEstimate(flops=0, bytes_accessed=12 * rows * cols, transcendentals=0),
        name="joined",
    )(core, mine, theirs)
    return out if axis == 1 else out.reshape(2 * rows, cols)


def dense_rows(rows, cot_all, group_place, gate_proj, up_proj, down_proj):
    length, model = rows.shape
    width = gate_proj.shape[1]
    tile = math.gcd(width, 256)
    out_tile = math.gcd(model, 256)
    first, second = width // tile, model // out_tile
    right_t = (((1,), (1,)), ((), ()))

    def kernel(place_ref, x_ref, c_ref, gate_ref, up_ref, down_ref, hidden_ref, grad_ref, gates, ups, gate_grads, up_grads):
        j = pl.program_id(0)

        @pl.when(j < first)
        def _():
            gate_pre = jnp.dot(x_ref[...], gate_ref[...], preferred_element_type=f32)
            up_pre = jnp.dot(x_ref[...], up_ref[...], preferred_element_type=f32)
            hidden_grad = lax.dot_general(c_ref[...], down_ref[...], right_t, preferred_element_type=f32)
            hidden, gate_grad, up_grad = gelu_grads(gate_pre, up_pre, hidden_grad)
            hidden_ref[...] = hidden.astype(bf16)
            at = pl.ds(pl.multiple_of(j * tile, tile), tile)
            gates[:, at] = gate_ref[...]
            ups[:, at] = up_ref[...]
            gate_grads[:, at] = gate_grad.astype(bf16)
            up_grads[:, at] = up_grad.astype(bf16)

        @pl.when(j >= first)
        def _():
            at = pl.ds(pl.multiple_of((j - first) * out_tile, out_tile), out_tile)
            part = lax.dot_general(gate_grads[...], gates[at, :], right_t, preferred_element_type=f32)
            part = part + lax.dot_general(up_grads[...], ups[at, :], right_t, preferred_element_type=f32)
            grad_ref[...] = part.astype(bf16)

    clamp = lambda j: jnp.minimum(j, first - 1)
    wide = pl.BlockSpec((model, tile), lambda j, p: (0, clamp(j)))
    return pl.pallas_call(
        kernel,
        grid_spec=pltpu.PrefetchScalarGridSpec(
            num_scalar_prefetch=1,
            grid=(first + second,),
            in_specs=[
                pl.BlockSpec((length, model), lambda j, p: (0, 0)),
                pl.BlockSpec((length, model), lambda j, p: (p[0], 0)),
                wide,
                wide,
                pl.BlockSpec((tile, model), lambda j, p: (clamp(j), 0)),
            ],
            out_specs=[
                pl.BlockSpec((length, tile), lambda j, p: (0, clamp(j))),
                pl.BlockSpec((length, out_tile), lambda j, p: (0, jnp.maximum(j - first, 0))),
            ],
            scratch_shapes=[
                pltpu.VMEM((model, width), bf16),
                pltpu.VMEM((model, width), bf16),
                pltpu.VMEM((length, width), bf16),
                pltpu.VMEM((length, width), bf16),
            ],
        ),
        out_shape=[
            jax.ShapeDtypeStruct((length, width), bf16),
            jax.ShapeDtypeStruct((length, model), bf16),
        ],
        compiler_params=pltpu.CompilerParams(vmem_limit_bytes=VMEM_LIMIT),
        name="dense_rows",
    )(group_place, rows, cot_all, gate_proj, up_proj, down_proj)


def project_t(rows, weight_t):
    total, model = rows.shape
    width = weight_t.shape[0]
    length = math.gcd(total, 256)

    def kernel(rows_ref, weight_ref, out_ref):
        out_ref[...] = lax.dot_general(
            rows_ref[...], weight_ref[...], (((1,), (1,)), ((), ())), preferred_element_type=f32
        )

    return pl.pallas_call(
        kernel,
        grid=(total // length,),
        in_specs=[
            pl.BlockSpec((length, model), lambda j: (j, 0)),
            pl.BlockSpec((width, model), lambda j: (0, 0)),
        ],
        out_specs=pl.BlockSpec((length, width), lambda j: (j, 0)),
        out_shape=jax.ShapeDtypeStruct((total, width), f32),
        compiler_params=pltpu.CompilerParams(vmem_limit_bytes=VMEM_LIMIT),
        name="project_t",
    )(rows, weight_t)


def mix_out(value_prefix, keep_prefix, branch_pre, state_in, out_proj):
    blocks, length, width = value_prefix.shape
    model = out_proj.shape[1]

    def kernel(value_ref, keep_ref, branch_ref, in_ref, out_ref, state_ref, mixed_ref, part_ref):
        state = value_ref[0] + keep_ref[0] * in_ref[...]
        state_ref[0] = state
        mixed = (state * gelu_tanh(branch_ref[0])).astype(bf16)
        mixed_ref[0] = mixed
        part_ref[0] = jnp.dot(mixed, out_ref[...], preferred_element_type=f32).astype(bf16)

    block = pl.BlockSpec((1, length, width), lambda j: (j, 0, 0))
    whole = lambda *shape: pl.BlockSpec(shape, lambda j: (0,) * len(shape))
    return pl.pallas_call(
        kernel,
        grid=(blocks,),
        in_specs=[block, block, block, whole(1, width), whole(width, model)],
        out_specs=[block, block, pl.BlockSpec((1, length, model), lambda j: (j, 0, 0))],
        out_shape=[
            jax.ShapeDtypeStruct((blocks, length, width), f32),
            jax.ShapeDtypeStruct((blocks, length, width), bf16),
            jax.ShapeDtypeStruct((blocks, length, model), bf16),
        ],
        compiler_params=pltpu.CompilerParams(vmem_limit_bytes=VMEM_LIMIT),
        name="mix_out",
    )(value_prefix, keep_prefix, branch_pre, state_in, out_proj)


def mix_back(mid_rows, out_proj, branch_pre, state, keep_prefix):
    blocks, length, width = state.shape
    model = out_proj.shape[1]
    tiles = length // 16

    def kernel(mid_ref, out_ref, branch_ref, state_ref, keep_ref, direct_ref, branch_grad_ref, reach_ref, mixed, acc):
        j = pl.program_id(0)
        mixed[...] = lax.dot_general(
            mid_ref[0], out_ref[...], (((1,), (1,)), ((), ())), preferred_element_type=f32
        )

        @pl.when(j == 0)
        def _():
            acc[...] = jnp.zeros_like(acc)

        def tile(i, total):
            at = pl.ds(pl.multiple_of(i * 16, 16), 16)
            grad = mixed[at, :]
            pre = branch_ref[0, at, :]
            square = pre * pre
            inner = math.sqrt(2.0 / math.pi) * pre * (1.0 + 0.044715 * square)
            half = 0.5 * (1.0 + jnp.tanh(inner))
            act = pre * half
            slope = half + 2.0 * math.sqrt(2.0 / math.pi) * act * (1.0 - half) * (1.0 + 3.0 * 0.044715 * square)
            direct = grad * act
            direct_ref[0, at, :] = direct
            branch_grad_ref[0, at, :] = (grad * state_ref[0, at, :] * slope).astype(bf16)
            return total + direct * keep_ref[0, at, :]

        acc[...] = lax.fori_loop(0, tiles, tile, acc[...])

        @pl.when(j == blocks - 1)
        def _():
            reach_ref[...] = jnp.sum(acc[...], axis=0, keepdims=True)

    block = pl.BlockSpec((1, length, width), lambda j: (j, 0, 0))
    whole = lambda *shape: pl.BlockSpec(shape, lambda j: (0,) * len(shape))
    return pl.pallas_call(
        kernel,
        grid=(blocks,),
        in_specs=[pl.BlockSpec((1, length, model), lambda j: (j, 0, 0)), whole(width, model), block, block, block],
        out_specs=[block, block, whole(1, width)],
        out_shape=[
            jax.ShapeDtypeStruct((blocks, length, width), f32),
            jax.ShapeDtypeStruct((blocks, length, width), bf16),
            jax.ShapeDtypeStruct((1, width), f32),
        ],
        scratch_shapes=[pltpu.VMEM((length, width), f32), pltpu.VMEM((16, width), f32)],
        compiler_params=pltpu.CompilerParams(vmem_limit_bytes=VMEM_LIMIT),
        name="mix_back",
    )(mid_rows, out_proj, branch_pre, state, keep_prefix)


def minus_expm1(x):
    series = 1.0 / 40320.0
    for term in (1.0 / 5040.0, 1.0 / 720.0, 1.0 / 120.0, 1.0 / 24.0, 1.0 / 6.0, 0.5, 1.0):
        series = series * x + term
    return jnp.where(x > -0.35, -x * series, 1.0 - jnp.exp(x))


def rows_of(shape):
    return lax.broadcasted_iota(jnp.int32, shape, 0)


def down(cur, prev, by, row):
    return jnp.where(row >= by, pltpu.roll(cur, by, 0), pltpu.roll(prev, by, 0))


def up(cur, after, by, row):
    return jnp.where(row < TILE - by, pltpu.roll(cur, TILE - by, 0), pltpu.roll(after, TILE - by, 0))


def last_row(tile):
    return jnp.broadcast_to(tile[TILE - 1 :, :], tile.shape)


def first_row(tile):
    return jnp.broadcast_to(tile[:1, :], tile.shape)


def forward_kernel(
    inner_ref,
    mask_ref,
    rim_ref,
    taps_ref,
    vec_ref,
    rate_ref,
    input_ref,
    conv_ref,
    low_ref,
    sig_rate_ref,
    sig_input_ref,
    keep_ref,
    value_ref,
    end_ref,
    prev_ref,
    carry_ref,
    rate_raw_ref,
    input_raw_ref,
):
    step = pl.program_id(0)
    length, width = inner_ref.shape[1:]
    tiles = length // TILE
    taps_n = taps_ref.shape[0]

    @pl.when(step == 0)
    def _():
        prev_ref[...] = rim_ref[...]
        carry_ref[0] = jnp.ones((TILE, width), f32)
        carry_ref[1] = jnp.zeros((TILE, width), f32)

    row = rows_of((TILE, width))

    def conv_tile(i, prev):
        at = pl.ds(pl.multiple_of(i * TILE, TILE), TILE)
        cur = inner_ref[0, at, :]
        masks = mask_ref[at, :]
        total = vec_ref[0:1, :] + taps_ref[0:1, :] * cur
        for k in range(1, taps_n):
            total = total + taps_ref[k : k + 1, :] * (down(cur, prev, k, row) * masks[:, k : k + 1])
        conv_ref[0, at, :] = total
        return cur

    prev_ref[...] = lax.fori_loop(0, tiles, conv_tile, prev_ref[...])
    low = conv_ref[0].astype(bf16)
    low_ref[0] = low
    rate_raw_ref[...] = jnp.dot(low, rate_ref[...], preferred_element_type=f32)
    input_raw_ref[...] = jnp.dot(low, input_ref[...], preferred_element_type=f32)

    def gate_tile(i, carry):
        keep_in, value_in = carry
        at = pl.ds(pl.multiple_of(i * TILE, TILE), TILE)
        sig_rate = jax.nn.sigmoid(rate_raw_ref[at, :] + vec_ref[1:2, :])
        sig_input = jax.nn.sigmoid(input_raw_ref[at, :] + vec_ref[2:3, :])
        sig_rate_ref[0, at, :] = sig_rate
        sig_input_ref[0, at, :] = sig_input
        log_decay = sig_rate * vec_ref[3:4, :]
        a = jnp.exp(log_decay) * mask_ref[at, 0:1]
        b = jnp.sqrt(minus_expm1(2.0 * log_decay)) * sig_input * conv_ref[0, at, :]
        for d in (1, 2, 4):
            a_before = jnp.where(row >= d, pltpu.roll(a, d, 0), 1.0)
            b_before = jnp.where(row >= d, pltpu.roll(b, d, 0), 0.0)
            b = b + a * b_before
            a = a * a_before
        b = b + a * value_in
        a = a * keep_in
        keep_ref[0, at, :] = a
        value_ref[0, at, :] = b
        return last_row(a), last_row(b)

    keep_end, value_end = lax.fori_loop(0, tiles, gate_tile, (carry_ref[0], carry_ref[1]))
    carry_ref[0] = keep_end
    carry_ref[1] = value_end
    end_ref[0] = keep_end
    end_ref[1] = value_end


def backward_kernel(
    direct_ref,
    state_ref,
    state_prev_ref,
    conv_ref,
    sig_rate_ref,
    sig_input_ref,
    inner_ref,
    inner_prev_ref,
    mask_ref,
    rim_ref,
    state_in_ref,
    after_ref,
    taps_ref,
    vec_ref,
    rate_ref,
    input_ref,
    rate_grad_ref,
    input_grad_ref,
    inner_grad_ref,
    tail_ref,
    rim_grad_ref,
    sums_ref,
    carry_ref,
    next_ref,
    acc_ref,
    rate_f_ref,
    input_f_ref,
    conv_f_ref,
):
    step = pl.program_id(0)
    steps = pl.num_programs(0)
    length, width = direct_ref.shape[1:]
    tiles = length // TILE
    taps_n = taps_ref.shape[0]
    row = rows_of((TILE, width))
    is_first_block = step == steps - 1

    @pl.when(step == 0)
    def _():
        carry_ref[...] = after_ref[...]
        next_ref[...] = jnp.zeros_like(next_ref)
        acc_ref[...] = jnp.zeros_like(acc_ref)

    edge_state = jnp.where(is_first_block, state_in_ref[...], state_prev_ref[0])
    edge_inner = jnp.where(is_first_block, rim_ref[...], inner_prev_ref[0])
    neg_rate = vec_ref[3:4, :]

    def gate_tile(n, carry):
        after, acc_rate, acc_input, acc_decay = carry
        i = tiles - 1 - n
        at = pl.ds(pl.multiple_of(i * TILE, TILE), TILE)
        before = pl.ds(pl.multiple_of(jnp.maximum(i - 1, 0) * TILE, TILE), TILE)
        direct = direct_ref[0, at, :]
        sig_rate = sig_rate_ref[0, at, :]
        sig_input = sig_input_ref[0, at, :]
        conv = conv_ref[0, at, :]
        log_decay = sig_rate * neg_rate
        decay = jnp.exp(log_decay)
        keep = decay * mask_ref[at, 0:1]
        room = minus_expm1(2.0 * log_decay)
        root = jnp.sqrt(room)
        a = keep
        b = keep * direct
        for d in (1, 2, 4):
            a_after = jnp.where(row < TILE - d, pltpu.roll(a, TILE - d, 0), 1.0)
            b_after = jnp.where(row < TILE - d, pltpu.roll(b, TILE - d, 0), 0.0)
            b = b + a * b_after
            a = a * a_after
        reach = b + a * after
        grad = direct + up(reach, after, 1, row)
        prev_tile = jnp.where(i == 0, edge_state, state_ref[0, before, :])
        state_prev = down(state_ref[0, at, :], prev_tile, 1, row)
        grad_root = grad * root
        gated = grad_root * sig_input
        decay_grad = grad * (keep * state_prev - sig_input * conv * (decay * decay) / root)
        rate_grad = decay_grad * neg_rate * (sig_rate * (1.0 - sig_rate))
        input_grad = gated * conv * (1.0 - sig_input)
        rate_f_ref[at, :] = rate_grad
        input_f_ref[at, :] = input_grad
        conv_f_ref[at, :] = gated
        return (
            first_row(reach),
            acc_rate + rate_grad,
            acc_input + input_grad,
            acc_decay + decay_grad * sig_rate,
        )

    after, acc_rate, acc_input, acc_decay = lax.fori_loop(
        0, tiles, gate_tile, (carry_ref[...], acc_ref[0], acc_ref[1], acc_ref[2])
    )
    carry_ref[...] = after
    acc_ref[0] = acc_rate
    acc_ref[1] = acc_input
    acc_ref[2] = acc_decay
    rate_low = rate_f_ref[...].astype(bf16)
    input_low = input_f_ref[...].astype(bf16)
    rate_grad_ref[0] = rate_low
    input_grad_ref[0] = input_low
    right_t = (((1,), (1,)), ((), ()))
    conv_f_ref[...] += lax.dot_general(
        rate_low, rate_ref[...], right_t, preferred_element_type=f32
    ) + lax.dot_general(input_low, input_ref[...], right_t, preferred_element_type=f32)

    def conv_tile(n, carry):
        acc_bias, acc_taps, nexts = carry
        i = tiles - 1 - n
        at = pl.ds(pl.multiple_of(i * TILE, TILE), TILE)
        before = pl.ds(pl.multiple_of(jnp.maximum(i - 1, 0) * TILE, TILE), TILE)
        grad = conv_f_ref[at, :]
        masks = mask_ref[at, :]
        cur = inner_ref[0, at, :]
        prev = jnp.where(i == 0, edge_inner, inner_ref[0, before, :])
        total = grad * taps_ref[0:1, :]
        new_taps = [acc_taps[0] + grad * cur]
        new_nexts = []
        for k in range(1, taps_n):
            masked = grad * masks[:, k : k + 1]
            part = masked * taps_ref[k : k + 1, :]
            total = total + up(part, nexts[k - 1], k, row)
            new_taps.append(acc_taps[k] + masked * down(cur, prev, k, row))
            new_nexts.append(part)
        rate_f_ref[at, :] = total
        return acc_bias + grad, tuple(new_taps), tuple(new_nexts)

    acc_bias, acc_taps, nexts = lax.fori_loop(
        0,
        tiles,
        conv_tile,
        (
            acc_ref[3],
            tuple(acc_ref[4 + k] for k in range(taps_n)),
            tuple(next_ref[k] for k in range(taps_n - 1)),
        ),
    )
    acc_ref[3] = acc_bias
    for k in range(taps_n):
        acc_ref[4 + k] = acc_taps[k]
    for k in range(taps_n - 1):
        next_ref[k] = nexts[k]
    inner_grad_ref[0] = rate_f_ref[...].astype(bf16)

    @pl.when(step == 0)
    def _():
        tail_ref[...] = rate_f_ref[length - TILE :, :]

    @pl.when(is_first_block)
    def _():
        zero = jnp.zeros((TILE, width), f32)
        total = zero
        for k in range(1, taps_n):
            total = total + up(zero, nexts[k - 1], k, row)
        rim_grad_ref[...] = total
        sums_ref[...] = jnp.sum(acc_ref[...], axis=1)


def norm_project(blocks, place, gain, weight_t):
    count = len(blocks)
    length, model = blocks[0].shape
    width = weight_t.shape[0]

    def kernel(place_ref, *refs):
        ins, gain_ref, weight_ref, normed_ref, out_ref = refs[:count], *refs[count:]
        j = pl.program_id(0)
        for r in range(count):

            @pl.when((j ^ place_ref[0]) == r)
            def _(source=ins[r]):
                x = source[...].astype(f32)
                root = lax.rsqrt(jnp.mean(x * x, axis=-1, keepdims=True) + epsilon)
                normed_ref[...] = (x * root * gain_ref[...]).astype(bf16)

        out_ref[0] = lax.dot_general(
            normed_ref[...], weight_ref[...], (((1,), (1,)), ((), ())), preferred_element_type=f32
        )

    whole = lambda *shape: pl.BlockSpec(shape, lambda j, p: (0,) * len(shape))
    return pl.pallas_call(
        kernel,
        grid_spec=pltpu.PrefetchScalarGridSpec(
            num_scalar_prefetch=1,
            grid=(count,),
            in_specs=[whole(length, model)] * count + [whole(1, model), whole(width, model)],
            out_specs=[
                pl.BlockSpec((length, model), lambda j, p: (j, 0)),
                pl.BlockSpec((1, length, width), lambda j, p: (j, 0, 0)),
            ],
        ),
        out_shape=[
            jax.ShapeDtypeStruct((count * length, model), bf16),
            jax.ShapeDtypeStruct((count, length, width), f32),
        ],
        compiler_params=pltpu.CompilerParams(vmem_limit_bytes=VMEM_LIMIT),
        name="norm_project",
    )(place, *blocks, gain, weight_t)


def recur_forward(inner, masks, rim, taps, vecs, rate_dense, input_dense):
    blocks, length, width = inner.shape
    whole = lambda *shape: pl.BlockSpec(shape, lambda j: (0,) * len(shape))
    block = pl.BlockSpec((1, length, width), lambda j: (j, 0, 0))
    full = jax.ShapeDtypeStruct((blocks, length, width), f32)
    return pl.pallas_call(
        forward_kernel,
        grid_spec=pltpu.PrefetchScalarGridSpec(
            num_scalar_prefetch=0,
            grid=(blocks,),
            in_specs=[
                block,
                pl.BlockSpec((length, masks.shape[1]), lambda j: (j, 0)),
                whole(*rim.shape),
                whole(*taps.shape),
                whole(*vecs.shape),
                whole(*rate_dense.shape),
                whole(*input_dense.shape),
            ],
            out_specs=[block, block, block, block, block, block, whole(2, TILE, width)],
            scratch_shapes=[
                pltpu.VMEM((TILE, width), f32),
                pltpu.VMEM((2, TILE, width), f32),
                pltpu.VMEM((length, width), f32),
                pltpu.VMEM((length, width), f32),
            ],
        ),
        out_shape=[
            full,
            jax.ShapeDtypeStruct((blocks, length, width), bf16),
            full,
            full,
            full,
            full,
            jax.ShapeDtypeStruct((2, TILE, width), f32),
        ],
        compiler_params=pltpu.CompilerParams(vmem_limit_bytes=VMEM_LIMIT),
        name="recur_forward",
    )(inner, masks, rim, taps, vecs, rate_dense, input_dense)


def recur_backward(
    direct, state, conv, sig_rate, sig_input, inner, masks, rim, state_in, after, taps, vecs, rate_dense, input_dense
):
    blocks, length, width = inner.shape
    last = length // TILE - 1
    whole = lambda *shape: pl.BlockSpec(shape, lambda j: (0,) * len(shape))
    block = pl.BlockSpec((1, length, width), lambda j: (blocks - 1 - j, 0, 0))
    edge = pl.BlockSpec(
        (1, TILE, width), lambda j: (jnp.maximum(blocks - 2 - j, 0), last, 0)
    )
    low = jax.ShapeDtypeStruct((blocks, length, width), bf16)
    tile = jax.ShapeDtypeStruct((TILE, width), f32)
    count = 4 + taps.shape[0]
    return pl.pallas_call(
        backward_kernel,
        grid_spec=pltpu.PrefetchScalarGridSpec(
            num_scalar_prefetch=0,
            grid=(blocks,),
            in_specs=[
                block,
                block,
                edge,
                block,
                block,
                block,
                block,
                edge,
                pl.BlockSpec((length, masks.shape[1]), lambda j: (blocks - 1 - j, 0)),
                whole(*rim.shape),
                whole(*state_in.shape),
                whole(*after.shape),
                whole(*taps.shape),
                whole(*vecs.shape),
                whole(*rate_dense.shape),
                whole(*input_dense.shape),
            ],
            out_specs=[
                block,
                block,
                block,
                whole(TILE, width),
                whole(TILE, width),
                whole(count, width),
            ],
            scratch_shapes=[
                pltpu.VMEM((TILE, width), f32),
                pltpu.VMEM((taps.shape[0] - 1, TILE, width), f32),
                pltpu.VMEM((count, TILE, width), f32),
                pltpu.VMEM((length, width), f32),
                pltpu.VMEM((length, width), f32),
                pltpu.VMEM((length, width), f32),
            ],
        ),
        out_shape=[low, low, low, tile, tile, jax.ShapeDtypeStruct((count, width), f32)],
        compiler_params=pltpu.CompilerParams(vmem_limit_bytes=VMEM_LIMIT),
        cost_estimate=pl.CostEstimate(flops=1000, bytes_accessed=1000, transcendentals=0),
        name="recur_backward",
    )(
        direct,
        state,
        state,
        conv,
        sig_rate,
        sig_input,
        inner,
        inner,
        masks,
        rim,
        state_in,
        after,
        taps,
        vecs,
        rate_dense,
        input_dense,
    )


def dense_blocks(blocks):
    count, rows_in, cols_out = blocks.shape
    tall = blocks.reshape(count * rows_in, cols_out)
    wide = jnp.concatenate([tall] * count, axis=1)
    row = lax.broadcasted_iota(jnp.int32, wide.shape, 0) // rows_in
    col = lax.broadcasted_iota(jnp.int32, wide.shape, 1) // cols_out
    return jnp.where(row == col, wide, jnp.zeros_like(wide))


def diagonal_blocks(full, count):
    rows, cols = full.shape[0] // count, full.shape[1] // count
    return jnp.stack([full[i * rows : (i + 1) * rows, i * cols : (i + 1) * cols] for i in range(count)])


def rms(values):
    return lax.rsqrt(jnp.mean(values * values, axis=-1, keepdims=True) + epsilon)


def norm_back(grad, xhat, scale, root):
    e = grad * scale
    return root * (e - xhat * jnp.mean(e * xhat, axis=-1, keepdims=True)), jnp.sum(grad * xhat, axis=0)


def shards(
    tokens,
    mixer_gain,
    in_proj,
    branch_proj,
    conv_taps,
    conv_bias,
    rate_blocks,
    rate_bias,
    input_blocks,
    input_bias,
    decay_param,
    out_proj,
    dense_gain,
    gate_proj,
    up_proj,
    down_proj,
    segment_ids,
    cotangent,
):
    tp_place = lax.axis_index("tp")
    seq_place = lax.axis_index("seq")
    seq_size = lax.axis_size("seq")
    core = seq_place % 2
    tp_size = lax.axis_size("tp")
    gain_share = mixer_gain.shape[0]
    taps_n, width = conv_taps.shape
    rim_width = taps_n - 1
    length, model = tokens.shape
    group = length * tp_size
    blocks_n = rate_blocks.shape[0]

    in_t, branch_t = in_proj.T, branch_proj.T
    place = tp_place.astype(jnp.int32)[None]

    blocks = [tokens] + [swap(tokens, "tp", r) for r in range(1, tp_size)]
    blocks[1], gains, ids, rate_in, input_in, vec_in = tied(
        blocks[1],
        jnp.stack([mixer_gain, dense_gain]),
        segment_ids,
        rate_blocks,
        input_blocks,
        (conv_bias, rate_bias, input_bias, decay_param),
    )
    gains = gather_rows(gains)
    gains = gains.transpose(1, 0, 2).reshape(2, -1).astype(f32)
    mixer_scale, dense_scale = gains[0], gains[1]
    rim_ids = from_neighbour(ids[-rim_width:], -1)
    ext_ids = jnp.concatenate([rim_ids, ids])
    same = [ext_ids[rim_width - k : rim_width - k + group] == ids for k in range(1, taps_n)]
    masks = jnp.stack([same[0]] + same, axis=1).astype(f32)
    rate_dense = dense_blocks(rate_in)
    input_dense = dense_blocks(input_in)
    vecs = jnp.stack([*vec_in[:3], -8.0 * jax.nn.softplus(-vec_in[3])])
    *blocks, masks, rate_dense, input_dense, vecs = tied(*blocks, masks, rate_dense, input_dense, vecs)
    cot_all = lax.all_gather(cotangent, ("seq", "tp"), axis=0, tiled=True)

    normed, inner = norm_project(blocks, place, mixer_scale[None], in_t)
    rim = from_neighbour(inner[-1, -TILE:], -1)
    conv, conv_low, sig_rate, sig_input, keep_prefix, value_prefix, ends = recur_forward(
        inner, masks, rim, conv_taps, vecs, rate_dense, input_dense
    )
    ends, normed_b = tied(ends, normed)
    state_in = carry_in(ends[0, 0], ends[1, 0], False)
    branch_pre = project_t(normed_b, branch_t).reshape(inner.shape)
    state, mixed, mixer_part = mix_out(value_prefix, keep_prefix, branch_pre, state_in[None], out_proj)
    mixed = mixed.reshape(group, width)
    mixer_out = scatter_rows(mixer_part)
    mid = tokens.astype(f32) + mixer_out
    mid_root = rms(mid)
    xhat_dense = mid * mid_root
    normed_two = (xhat_dense * dense_scale).astype(bf16)

    chips = seq_size // 2
    same_core = [[core_no + 2 * i for i in range(chips)] for core_no in range(2)]
    rows_z = lax.all_gather(normed_two, "seq", axis=0, tiled=True, axis_index_groups=same_core)
    rows_two, cot_all = tied(gather_rows(normed_two).reshape(group, model), cot_all)
    hidden, normed_two_part = dense_rows(
        rows_two, cot_all, seq_place.astype(jnp.int32)[None], gate_proj, up_proj, down_proj
    )
    normed_two_grad = scatter_rows(normed_two_part.reshape(tp_size, length, model))
    dense_part = product(hidden, down_proj).astype(bf16)
    normed_two_grad, dense_part = tied(normed_two_grad, dense_part)
    mid_from_norm, dense_gain_part = norm_back(normed_two_grad, xhat_dense, dense_scale, mid_root)
    mid_grad = cotangent.astype(f32) + mid_from_norm
    mid_blocks = gather_rows(mid_grad.astype(bf16))
    mid_blocks, dense_part, rows_z = tied(mid_blocks, dense_part, rows_z)
    spread_first, spread_finish = spread(rows_z)

    direct, branch_pre_grad, reach = mix_back(mid_blocks, out_proj, branch_pre, state, keep_prefix)
    branch_pre_grad = branch_pre_grad.reshape(group, width)
    mid_rows = mid_blocks.reshape(group, model)
    reach, direct, branch_pre_grad, mid_rows = tied(reach[0], direct, branch_pre_grad, mid_rows)
    after = carry_in(ends[0, 0], reach, True)
    out_full = product_left_t(mixed, mid_rows).astype(bf16)
    branch_full = product_left_t(branch_pre_grad, normed).astype(bf16)
    after, pair_full = spread_first(*tied(after, jnp.concatenate([out_full, branch_full])))
    pair_part = lax.psum_scatter(pair_full, "seq", scatter_dimension=0, tiled=True)
    tile = lambda v: jnp.broadcast_to(v, (TILE, width))
    rate_low, input_low, inner_grad, tail, rim_grad, sums = recur_backward(
        direct,
        state,
        conv,
        sig_rate,
        sig_input,
        inner,
        masks,
        rim,
        tile(state_in),
        tile(after),
        conv_taps,
        vecs,
        rate_dense,
        input_dense,
    )
    fixed = tail + from_neighbour(rim_grad, 1)
    rows_mine, fixed = spread_finish(fixed)
    low_rows = conv_low.reshape(group, width)
    rate_w = diagonal_blocks(product_left_t(low_rows, rate_low.reshape(group, width)), blocks_n)
    input_w = diagonal_blocks(product_left_t(low_rows, input_low.reshape(group, width)), blocks_n)
    inner_grad = lax.dynamic_update_slice(
        inner_grad, fixed.astype(bf16)[None], (tp_size - 1, length - TILE, 0)
    ).reshape(group, width)
    in_full = product_left_t(inner_grad, normed).astype(bf16)
    ours, theirs = both_halves(rate_w.astype(bf16), input_w.astype(bf16), core)
    block_sum = ours + swap(theirs, "seq", 1)
    normed_part = (product(inner_grad, in_t) + product(branch_pre_grad, branch_t)).astype(bf16)
    in_full, normed_part, block_sum, pair_part = tied(in_full, normed_part, block_sum, pair_part)
    block_other = swap(block_sum, "seq", 2)
    rows_theirs = swap(rows_mine, "seq", 1)
    normed_part, in_full, pair_part, rows_mine, rows_theirs, block_other, dense_part = tied(
        normed_part, in_full, pair_part, rows_mine, rows_theirs, block_other, dense_part
    )
    block_sum = block_sum + block_other
    pair_sum = lax.all_gather(pair_part, "seq", axis=0, tiled=True)
    in_part = lax.psum_scatter(in_full, "seq", scatter_dimension=0, tiled=True)
    split = lambda rows: rows.reshape(tp_size, length, model)
    grad_and_out = scatter_rows(jnp.concatenate([split(normed_part), split(dense_part)], axis=1))
    block_other = swap(block_sum, "seq", 4)

    places = jnp.stack([core, tp_place]).astype(jnp.int32)
    blocked = lambda rows: rows.reshape(tp_size, chips, length, model)
    gate_w, up_w, down_w = dense_weight_grads(
        blocked(rows_mine), blocked(rows_theirs), cot_all, gate_proj, up_proj, down_proj, places
    )
    gate_w, up_w, down_w, in_part, grad_and_out, block_other = tied(
        gate_w, up_w, down_w, in_part, grad_and_out, block_other
    )
    normed_grad, dense_out = grad_and_out[:length], grad_and_out[length:]
    block_sum = block_sum + block_other
    bit = 8
    while bit < seq_size:
        block_sum = block_sum + swap(block_sum, "seq", bit)
        bit *= 2
    in_sum = lax.all_gather(in_part, "seq", axis=0, tiled=True)
    out_sum, branch_sum = pair_sum[:width].astype(f32), pair_sum[width:].astype(f32)
    gate_other, out_sum, branch_sum = tied(swap(gate_w, "seq", 1), out_sum, branch_sum)
    halves = [(gate_w, gate_other, 1), (up_w, swap(up_w, "seq", 1), 1), (down_w, swap(down_w, "seq", 1), 0)]
    output = (mid + dense_out).astype(bf16)
    own = tokens.astype(f32)
    own_root = rms(own)
    rows_grad, mixer_gain_part = norm_back(normed_grad, own * own_root, mixer_scale, own_root)
    tokens_grad = mid_grad + rows_grad

    small = jnp.stack([mixer_gain_part, dense_gain_part])
    whole = []
    for axis, size in (("tp", tp_size), ("seq", seq_size)):
        if axis == "seq":
            gain_own = lax.dynamic_slice_in_dim(small, tp_place * gain_share, gain_share, 1)
            wide = max(width, gain_share)
            fit = lambda v: jnp.pad(v, ((0, 0), (0, wide - v.shape[1])))
            small = jnp.concatenate([fit(sums), fit(gain_own)])
        bit = 1
        while bit < size:
            other = swap(small, axis, bit)
            if halves:
                mine, theirs, along = halves.pop(0)
                made, other = tied(joined(mine, theirs, places, along), other)
                whole.append(made)
            small = small + other
            bit *= 2
    gate_sum, up_sum, down_sum = whole
    sums, gain_sum = small[:-2, :width], small[-2:, :gain_share]
    decay_sum = 8.0 * jax.nn.sigmoid(-decay_param) * sums[2]
    rate_sum, input_sum = both_halves(block_sum, swap(block_sum, "seq", 1), core)
    rate_sum, input_sum = rate_sum.astype(f32), input_sum.astype(f32)
    return (
        output,
        tokens_grad,
        gain_sum[0],
        in_sum.astype(f32).T,
        branch_sum.astype(f32).T,
        sums[4 : 4 + taps_n],
        sums[3],
        rate_sum,
        sums[0],
        input_sum,
        sums[1],
        decay_sum,
        out_sum.astype(f32),
        gain_sum[1],
        gate_sum,
        up_sum,
        down_sum,
    )


def solution(mesh):
    return jax.shard_map(
        shards,
        mesh=mesh,
        in_specs=(
            P(("seq", "tp"), None),
            P("tp"),
            P(None, "tp"),
            P(None, "tp"),
            P(None, "tp"),
            P("tp"),
            P("tp", None, None),
            P("tp"),
            P("tp", None, None),
            P("tp"),
            P("tp"),
            P("tp", None),
            P("tp"),
            P(None, "tp"),
            P(None, "tp"),
            P("tp", None),
            P("seq"),
            P(("seq", "tp"), None),
        ),
        out_specs=(
            P(("seq", "tp"), None),
            P(("seq", "tp"), None),
            P("tp"),
            P(None, "tp"),
            P(None, "tp"),
            P(None, "tp"),
            P("tp"),
            P("tp", None, None),
            P("tp"),
            P("tp", None, None),
            P("tp"),
            P("tp"),
            P("tp", None),
            P("tp"),
            P(None, "tp"),
            P(None, "tp"),
            P("tp", None),
        ),
        check_vma=False,
    )
```
